32 devices in a mesh: groups: 2 (over y), expert: 4 (over x, core), dp: 4 (over z).
Axes of the slice: x: 2, y: 2, z: 4, core: 2. Of those that a mesh axis runs over, the one named last changes fastest.
Arguments:
- tokens: bfloat16 [512, 2048], P(('groups', 'expert', 'dp')), parts along dimension 0, may hold values from -6 to 6
- expert_ids: int32 [512, 8], P(('groups', 'expert', 'dp')), parts along dimension 0, may hold values from 0 to 15, as said below
- slot_index: int32 [512, 8], P(('groups', 'expert', 'dp')), parts along dimension 0, may hold values from 0 to 15, as said below
- route_weights: bfloat16 [512, 8], P(('groups', 'expert', 'dp')), parts along dimension 0, may hold values from 0.099609375 to 1
- w_gate: bfloat16 [16, 2048, 768], P('expert'), may hold values from -0.125 to 0.125
- w_up: bfloat16 [16, 2048, 768], P('expert'), may hold values from -0.125 to 0.125
- w_down: bfloat16 [16, 768, 2048], P('expert'), may hold values from -0.21875 to 0.21875
- block_masks: int32 [16, 6], P('expert'), may hold values from 0 to 1, as said below
- cotangent: bfloat16 [512, 2048], P(('groups', 'expert', 'dp')), parts along dimension 0, may hold values from -6 to 6
Outputs:
- mixed: bfloat16 [512, 2048], P(('groups', 'expert', 'dp')), parts along dimension 0
- token_grad: bfloat16 [512, 2048], P(('groups', 'expert', 'dp')), parts along dimension 0
- route_grad: float32 [512, 8], P(('groups', 'expert', 'dp')), parts along dimension 0
- grad_gate: float32 [32, 2048, 768], P(('groups', 'expert'), 'dp'), parts along dimension 0
- grad_up: float32 [32, 2048, 768], P(('groups', 'expert'), 'dp'), parts along dimension 0
- grad_down: float32 [32, 768, 2048], P(('groups', 'expert'), None, 'dp'), parts along dimension 0
The draws below stay inside these ranges and needn't reach their ends.
There are 2 independent parts, one for each index of `groups`. The reference program is written for one: setup_inputs(seed, part) draws one part's arguments, and reference() takes and returns one part's arrays. A program takes and returns all parts, laid end to end along the dimension named above; an argument that names none is the same for every part. Nothing has to cross between parts.
Inputs may be any that keep to these rules, and one draw needn't show every extreme that they name: `expert_ids`: each token names 8 different experts. The tokens of one device name any one expert at most 16 times. slot_index[t, k] counts the routes of the same device's tokens to the same expert that come before (t, k) in row-major order of tokens and routes. `block_masks`: each expert keeps 3 to 6 of its 6 blocks.
All inputs are finite; a program needn't handle non-finite values.
Results may differ from the reference program's by a relative error of at most 0.012.
Values may be sent and summed in bfloat16 or wider, within the bound.
No kernel may reach another device: no remote copies, remote signals or barrier semaphores. Data moves between devices by JAX's collectives and lax.ppermute only.
A program may use at most 256 MiB of HBM per device.

```python
import math
import jax
import jax.numpy as jnp
from jax import lax

D = 2048
BLK = 128
NB = 6
FF = 768
TOP = 8
EXPERTS = 16
TOK_DEV = 16
CAP = 16
TOKENS = 256
N_EXPERT = 4
N_DP = 4


def route_table(key):
    key_hot, key_favour, key_score, key_order = jax.random.split(key, 4)
    hot_column = jax.random.randint(key_hot, (N_DP,), 0, EXPERTS)
    block_of = jnp.arange(TOKENS, dtype=jnp.int32) // TOK_DEV
    hottest = hot_column[block_of % N_DP]
    favour = jax.random.randint(key_favour, (EXPERTS,), 0, 4)
    score = jax.random.randint(key_score, (TOKENS, EXPERTS), 0, 4096) + favour[None, :] * 2048
    score = score * EXPERTS + jnp.arange(EXPERTS, dtype=jnp.int32)[None, :]
    score = jnp.where(jnp.arange(EXPERTS, dtype=jnp.int32)[None, :] == hottest[:, None], -1, score)
    _, others = lax.top_k(score, TOP - 1)
    chosen = jnp.concatenate([hottest[:, None], others.astype(jnp.int32)], axis=1)
    shuffle = jax.random.randint(key_order, (TOKENS, TOP), 0, 1 << 20) * TOP + jnp.arange(TOP, dtype=jnp.int32)[None, :]
    order = jnp.argsort(shuffle, axis=1)
    return jnp.take_along_axis(chosen, order, axis=1).astype(jnp.int32)


def draw_expert_ids(key, part):
    return route_table(key)


def draw_slot_index(key, part):
    chosen = route_table(key)
    flat = chosen.reshape(TOKENS // TOK_DEV, TOK_DEV * TOP)
    onehot = (flat[:, :, None] == jnp.arange(EXPERTS, dtype=jnp.int32)[None, None, :]).astype(jnp.int32)
    before = jnp.cumsum(onehot, axis=1) - onehot
    return jnp.sum(before * onehot, axis=2).reshape(TOKENS, TOP).astype(jnp.int32)


def draw_block_masks(key, part):
    key = jax.random.fold_in(key, 7)
    key_count, key_rank = jax.random.split(key)
    counts = jax.random.randint(key_count, (EXPERTS, 1), 3, NB + 1)
    scores = jax.random.randint(key_rank, (EXPERTS, NB), 0, 1 << 20) * NB + jnp.arange(NB, dtype=jnp.int32)[None, :]
    ranking = jnp.argsort(jnp.argsort(scores, axis=1), axis=1)
    return (ranking < counts).astype(jnp.int32)


def steps_of(own_key, shape, cuts, smallest, top_value):
    loudness, own = 1.0, jax.random.fold_in(own_key, 6)
    for position, blocks in cuts:
        draws = jnp.exp(jax.random.uniform(jax.random.fold_in(own, position), (blocks,), jnp.float32, smallest / len(cuts), top_value / len(cuts)))
        loudness = loudness * jnp.repeat(draws, shape[position] // blocks).reshape([-1 if axis == position else 1 for axis in range(len(shape))])
    return loudness


def noise(own_key, extent, scale, bound, shards=(), kind=jnp.bfloat16):
    factor_of = steps_of(own_key, extent, shards, -0.22, 0.18) if shards else 1.0
    values = jax.random.normal(own_key, extent, jnp.float32) * scale * factor_of
    return jnp.minimum(jnp.maximum(values, -bound), bound).astype(kind)


def setup_inputs(seed: int = 0, part: int = 0) -> dict:
    streams_of = jax.random.split(jax.random.key(seed), 10)
    part_keys = jax.random.split(jax.random.fold_in(streams_of[9], part), 10)
    tokens = noise(part_keys[0], (TOKENS, D), 1.0, 6.0, ((0, 16),))
    expert_ids = draw_expert_ids(jax.random.fold_in(jax.random.fold_in(streams_of[9], part), 71), part)
    slot_index = draw_slot_index(jax.random.fold_in(jax.random.fold_in(streams_of[9], part), 71), part)
    route_weights = jnp.clip(jnp.exp(math.log(1.0) - 2.306499 * jax.random.uniform(part_keys[3], (TOKENS, TOP), jnp.float32) ** steps_of(part_keys[3], (TOKENS, TOP), ((0, 16),), -0.2, 0.2)), 0.099609375, 1.0).astype(jnp.bfloat16)
    w_gate = noise(streams_of[4], (EXPERTS, D, FF), D ** -0.5, 0.125, ((0, 4),))
    w_up = noise(streams_of[5], (EXPERTS, D, FF), D ** -0.5, 0.125, ((0, 4),))
    w_down = noise(streams_of[6], (EXPERTS, FF, D), FF ** -0.5, 0.21875, ((0, 4),))
    block_masks = draw_block_masks(jax.random.fold_in(streams_of[9], 71), part)
    cotangent = noise(part_keys[8], (TOKENS, D), 1.0, 6.0, ((0, 16),))
    return {"tokens": tokens, "expert_ids": expert_ids, "slot_index": slot_index, "route_weights": route_weights, "w_gate": w_gate, "w_up": w_up, "w_down": w_down, "block_masks": block_masks, "cotangent": cotangent}


def place_rows(values, target, slots_total):
    width = values.shape[-1]
    empty = jnp.zeros((slots_total, width), jnp.bfloat16)
    return empty.at[target.reshape(-1)].set(values.reshape(-1, width))


def reference(tokens, expert_ids, slot_index, route_weights, w_gate, w_up, w_down, block_masks, cotangent):
    sources = N_EXPERT
    columns = N_DP
    slots_total = EXPERTS * CAP

    def cut(array):
        return array.reshape((sources, columns, TOK_DEV) + array.shape[1:])

    token_blocks = cut(tokens)
    id_blocks = cut(expert_ids)
    slot_blocks = cut(slot_index)
    weight_blocks = cut(route_weights)
    cot_blocks = cut(cotangent)
    keep = jnp.repeat(block_masks.astype(jnp.float32), BLK, axis=1)[:, None, :]
    gate_full = w_gate.astype(jnp.float32)
    up_full = w_up.astype(jnp.float32)
    down_full = w_down.astype(jnp.float32)

    def to_inbox(sent):
        return sent.reshape(sources, EXPERTS, CAP, D).transpose(1, 0, 2, 3).reshape(EXPERTS, sources * CAP, D)

    def to_outbox(boxes):
        return boxes.reshape(EXPERTS, sources, CAP, D).transpose(1, 0, 2, 3).reshape(sources, slots_total, D)

    def place_all(values, target):
        return jax.vmap(lambda v, p: place_rows(v, p, slots_total))(values, target)

    def read_all(boxes, target):
        return jax.vmap(lambda b, p: b[p.reshape(-1)].reshape(p.shape + (D,)))(boxes, target)

    def column(carry, index):
        x_col = lax.dynamic_index_in_dim(token_blocks, index, 1, keepdims=False)
        ids = lax.dynamic_index_in_dim(id_blocks, index, 1, keepdims=False)
        slots = lax.dynamic_index_in_dim(slot_blocks, index, 1, keepdims=False)
        weights = lax.dynamic_index_in_dim(weight_blocks, index, 1, keepdims=False).astype(jnp.float32)
        cot_col = lax.dynamic_index_in_dim(cot_blocks, index, 1, keepdims=False).astype(jnp.float32)
        target = (ids * CAP + slots).astype(jnp.int32)
        repeated = jnp.broadcast_to(x_col[:, :, None, :], (sources, TOK_DEV, TOP, D))
        inbox = to_inbox(place_all(repeated, target))
        inbox_f = inbox.astype(jnp.float32)
        gate_pre = jnp.einsum('erd,edf->erf', inbox_f, gate_full)
        up_proj = jnp.einsum('erd,edf->erf', inbox_f, up_full)
        sigma = jax.nn.sigmoid(gate_pre)
        hidden = (gate_pre * sigma * up_proj * keep).astype(jnp.bfloat16)
        outbox = jnp.einsum('erf,efd->erd', hidden.astype(jnp.float32), down_full).astype(jnp.bfloat16)
        routed = read_all(to_outbox(outbox), target).astype(jnp.float32)
        mixed = jnp.sum(weights[..., None] * routed, axis=2).astype(jnp.bfloat16)
        route_grad = jnp.sum(cot_col[:, :, None, :] * routed, axis=3)
        scaled = (weights[..., None] * cot_col[:, :, None, :]).astype(jnp.bfloat16)
        grad_box = to_inbox(place_all(scaled, target)).astype(jnp.float32)
        d_hidden = jnp.einsum('erd,efd->erf', grad_box, down_full) * keep
        d_up = (d_hidden * (gate_pre * sigma)).astype(jnp.bfloat16)
        d_gate = (d_hidden * up_proj * sigma * (1.0 + gate_pre * (1.0 - sigma))).astype(jnp.bfloat16)
        d_inbox = (jnp.einsum('erf,edf->erd', d_gate.astype(jnp.float32), gate_full)
                   + jnp.einsum('erf,edf->erd', d_up.astype(jnp.float32), up_full)).astype(jnp.bfloat16)
        d_routed = read_all(to_outbox(d_inbox), target).astype(jnp.float32)
        token_grad = jnp.sum(d_routed, axis=2).astype(jnp.bfloat16)
        part_gate = jnp.einsum('erd,erf->edf', inbox_f, d_gate.astype(jnp.float32)).astype(jnp.bfloat16)
        part_up = jnp.einsum('erd,erf->edf', inbox_f, d_up.astype(jnp.float32)).astype(jnp.bfloat16)
        part_down = jnp.einsum('erf,erd->efd', hidden.astype(jnp.float32), grad_box).astype(jnp.bfloat16)
        part_gate, part_up, part_down = lax.optimization_barrier((part_gate, part_up, part_down))
        carry = (carry[0] + part_gate.astype(jnp.float32),
                 carry[1] + part_up.astype(jnp.float32),
                 carry[2] + part_down.astype(jnp.float32))
        return carry, (mixed, token_grad, route_grad)

    start = (jnp.zeros((EXPERTS, D, FF), jnp.float32), jnp.zeros((EXPERTS, D, FF), jnp.float32),
             jnp.zeros((EXPERTS, FF, D), jnp.float32))
    grads, outputs = lax.scan(column, start, jnp.arange(columns, dtype=jnp.int32))
    mixed = outputs[0].transpose(1, 0, 2, 3).reshape(TOKENS, D)
    token_grad = outputs[1].transpose(1, 0, 2, 3).reshape(TOKENS, D)
    route_grad = outputs[2].transpose(1, 0, 2, 3).reshape(TOKENS, TOP)
    return (mixed, token_grad, route_grad, grads[0], grads[1], grads[2])
```

```python
import jax
import jax.numpy as jnp
from jax import lax
from jax.sharding import PartitionSpec as P

BLK = 128
LANES = 128


def round_up(value, unit):
    return -(-value // unit) * unit


def per_device(
    tokens, expert_ids, slot_index, route_weights, w_gate, w_up, w_down, block_masks, cotangent
):
    rows, width = tokens.shape
    local_experts, _, hidden_units = w_gate.shape
    experts = local_experts * lax.axis_size("expert")
    here, column = lax.axis_index("expert"), lax.axis_index("dp")
    chosen = expert_ids[:, :, None] == jnp.arange(experts, dtype=jnp.int32)
    dense = jnp.sum(jnp.where(chosen, route_weights[:, :, None].astype(jnp.float32), 0.0), axis=1)
    pad = round_up(experts, LANES) - experts
    dense = jnp.pad(dense, ((0, 0), (0, pad))).astype(jnp.bfloat16)
    packet = jnp.concatenate([tokens, cotangent, dense], axis=1)
    everyone = lax.all_gather(packet, ("dp", "expert"), axis=0, tiled=True)
    x, cot = everyone[:, :width], everyone[:, width : 2 * width]
    weights = lax.dynamic_slice_in_dim(
        everyone, 2 * width + here * local_experts, local_experts, axis=1
    ).astype(jnp.float32)
    weights = weights.T[:, :, None]
    keep = jnp.repeat(block_masks.astype(jnp.float32), BLK, axis=1)[:, None, :]

    gate_pre = jnp.einsum("td,edf->etf", x, w_gate, preferred_element_type=jnp.float32)
    up_proj = jnp.einsum("td,edf->etf", x, w_up, preferred_element_type=jnp.float32)
    back = jnp.einsum("td,efd->etf", cot, w_down, preferred_element_type=jnp.float32) * keep
    sigma = jax.nn.sigmoid(gate_pre)
    silu = gate_pre * sigma
    hidden = silu * up_proj * keep
    own = lax.axis_size("expert") * rows
    inner = lax.dynamic_slice_in_dim(jnp.sum(hidden * back, axis=2), column * own, own, axis=1)
    hidden = (hidden * weights).astype(jnp.bfloat16)
    d_hidden = back * weights
    d_up = (d_hidden * silu).astype(jnp.bfloat16)
    d_gate = (d_hidden * up_proj * sigma * (1.0 + gate_pre * (1.0 - sigma))).astype(jnp.bfloat16)

    def mine(array):
        return lax.dynamic_slice_in_dim(array, column * own, own, axis=1)

    mixed = jnp.einsum("etf,efd->td", mine(hidden), w_down, preferred_element_type=jnp.float32)
    token_grad = jnp.einsum(
        "etf,edf->td", mine(d_gate), w_gate, preferred_element_type=jnp.float32
    ) + jnp.einsum("etf,edf->td", mine(d_up), w_up, preferred_element_type=jnp.float32)
    inner = jnp.pad(inner.T, ((0, 0), (0, LANES // 2 - local_experts)))
    high = inner.astype(jnp.bfloat16)
    low = (inner - high.astype(jnp.float32)).astype(jnp.bfloat16)
    back_packet = jnp.concatenate(
        [mixed.astype(jnp.bfloat16), token_grad.astype(jnp.bfloat16), high, low], axis=1
    )
    arrived = lax.all_to_all(back_packet, "expert", split_axis=0, concat_axis=0, tiled=True)
    arrived = arrived.reshape(-1, rows, 2 * width + LANES).astype(jnp.float32)
    total = jnp.sum(arrived[:, :, : 2 * width], axis=0).astype(jnp.bfloat16)
    tail = arrived[:, :, 2 * width :]
    inner = tail[:, :, :local_experts] + tail[:, :, LANES // 2 : LANES // 2 + local_experts]
    inner = inner.transpose(1, 0, 2).reshape(rows, experts)
    route_grad = jnp.sum(jnp.where(chosen, inner[:, None, :], 0.0), axis=2)

    part = width // lax.axis_size("dp")
    x_part = lax.dynamic_slice_in_dim(x, column * part, part, axis=1)
    cot_part = lax.dynamic_slice_in_dim(cot, column * part, part, axis=1)
    grad_gate = jnp.einsum("td,etf->edf", x_part, d_gate, preferred_element_type=jnp.float32)
    grad_up = jnp.einsum("td,etf->edf", x_part, d_up, preferred_element_type=jnp.float32)
    grad_down = jnp.einsum("etf,td->efd", hidden, cot_part, preferred_element_type=jnp.float32)
    return (total[:, :width], total[:, width:], route_grad, grad_gate, grad_up, grad_down)


def solution(mesh):
    rows = P(("groups", "expert", "dp"), None)
    experts = P("expert", None, None)
    return jax.shard_map(
        per_device,
        mesh=mesh,
        in_specs=(rows, rows, rows, rows, experts, experts, experts, P("expert", None), rows),
        out_specs=(
            rows,
            rows,
            rows,
            P(("groups", "expert"), "dp", None),
            P(("groups", "expert"), "dp", None),
            P(("groups", "expert"), None, "dp"),
        ),
        check_vma=False,
    )
```

```python
import functools

import jax
import jax.numpy as jnp
from jax import lax
from jax.experimental import pallas as pl
from jax.experimental.pallas import tpu as pltpu
from jax.sharding import PartitionSpec as P

BLK = 128
LANES = 128
CHUNK = 256
WIDE = 512
MIB = 1 << 20

VMEM = pl.BlockSpec(memory_space=pltpu.VMEM)
SMEM = pl.BlockSpec(memory_space=pltpu.SMEM)
ANY = pl.BlockSpec(memory_space=pl.ANY)

NN = (((1,), (0,)), ((), ()))
NT = (((1,), (1,)), ((), ()))
TN = (((0,), (0,)), ((), ()))


def dot(a, b, dims):
    return lax.dot_general(a, b, dims, preferred_element_type=jnp.float32)


def lane_ids(rows, lanes):
    return lax.broadcasted_iota(jnp.int32, (rows, lanes), 1)


def pack_kernel(tokens, cotangent, expert_ids, route_weights, packet):
    rows, width = tokens.shape
    lanes = packet.shape[1] - 2 * width
    packet[:, :width] = tokens[...]
    packet[:, width : 2 * width] = cotangent[...]
    at = lane_ids(rows, lanes)
    values = route_weights[...].astype(jnp.float32)
    dense = jnp.zeros((rows, lanes), jnp.float32)
    for k in range(expert_ids.shape[1]):
        dense += jnp.where(expert_ids[:, k : k + 1] == at, values[:, k : k + 1], 0.0)
    packet[:, 2 * width :] = dense.astype(packet.dtype)


def load_kernel(*refs):
    count = len(refs) // 2
    sems = refs[-1]
    copies = [
        pltpu.make_async_copy(refs[i], refs[count + i], sems.at[i]) for i in range(count)
    ]
    for copy in copies:
        copy.start()
    for copy in copies:
        copy.wait()


def hidden_terms(x, cot, weights, masks, w_gate, w_up, w_down, expert, start):
    cols = pl.ds(start, CHUNK)
    gate_pre = dot(x, w_gate[expert, :, cols], NN)
    up_proj = dot(x, w_up[expert, :, cols], NN)
    back = dot(cot, w_down[expert, cols, :], NT)
    at = lane_ids(1, CHUNK)
    keep = jnp.zeros((1, CHUNK), jnp.float32)
    for j in range(CHUNK // BLK):
        kept = masks[expert, start // BLK + j].astype(jnp.float32)
        keep = jnp.where(at // BLK == j, kept, keep)
    sigma = 1.0 / (1.0 + jnp.exp(-gate_pre))
    silu = gate_pre * sigma
    hidden = silu * up_proj * keep
    d_hidden = back * (weights * keep)
    d_up = d_hidden * silu
    d_gate = d_hidden * up_proj * (sigma + silu * (1.0 - sigma))
    inner = jnp.sum(hidden * back, axis=1, keepdims=True)
    bf16 = jnp.bfloat16
    return (hidden * weights).astype(bf16), d_gate.astype(bf16), d_up.astype(bf16), inner


def weight_column(dense, index):
    at = lane_ids(*dense.shape)
    return jnp.sum(jnp.where(at == index, dense, 0.0), axis=1, keepdims=True)


def own_kernel(count, *refs):
    packets, refs = refs[:count], refs[count:]
    masks, w_gate, w_up, w_down, hidden_ref, d_gate_ref, d_up_ref, inner_ref, x, cot = refs
    rows = packets[0].shape[0]
    width = w_gate.shape[1]
    for i, packet in enumerate(packets):
        x[i * rows : (i + 1) * rows] = packet[:, :width]
        cot[i * rows : (i + 1) * rows] = packet[:, width : 2 * width]
    dense = jnp.concatenate([packet[:, 2 * width :].astype(jnp.float32) for packet in packets])
    local_experts, _, hidden_units = w_gate.shape
    base = lax.axis_index("expert") * local_experts
    at = lane_ids(*dense.shape)

    def body(expert, inner):
        weights = weight_column(dense, base + expert)
        total = jnp.zeros((dense.shape[0], 1), jnp.float32)
        for start in range(0, hidden_units, CHUNK):
            hidden, d_gate, d_up, part = hidden_terms(
                x[...], cot[...], weights, masks, w_gate, w_up, w_down, expert, start
            )
            hidden_ref[expert, :, start : start + CHUNK] = hidden
            d_gate_ref[expert, :, start : start + CHUNK] = d_gate
            d_up_ref[expert, :, start : start + CHUNK] = d_up
            total += part
        return inner + jnp.where(at == base + expert, total, 0.0)

    inner = lax.fori_loop(0, local_experts, body, jnp.zeros(dense.shape, jnp.float32))
    high = inner.astype(jnp.bfloat16)
    lanes = dense.shape[1]
    inner_ref[:, :lanes] = high
    inner_ref[:, lanes:] = (inner - high.astype(jnp.float32)).astype(jnp.bfloat16)


def back_kernel(hidden, d_gate, d_up, inner, w_gate, w_up, w_down, *outs):
    local_experts, width, _ = w_gate.shape
    rows = outs[0].shape[0]

    def body(step, carry):
        start = pl.multiple_of(step * WIDE, WIDE)
        cols = pl.ds(start, WIDE)
        mixed = jnp.zeros((hidden.shape[1], WIDE), jnp.float32)
        token_grad = jnp.zeros((hidden.shape[1], WIDE), jnp.float32)
        for e in range(local_experts):
            mixed += dot(hidden[e], w_down[e, :, cols], NN)
            token_grad += dot(d_gate[e], w_gate[e, cols, :], NT)
            token_grad += dot(d_up[e], w_up[e, cols, :], NT)
        for i, out in enumerate(outs):
            block = slice(i * rows, (i + 1) * rows)
            out[:, cols] = mixed[block].astype(out.dtype)
            out[:, pl.ds(start + width, WIDE)] = token_grad[block].astype(out.dtype)
        return carry

    lax.fori_loop(0, width // WIDE, body, 0)
    for i, out in enumerate(outs):
        out[:, 2 * width :] = inner[i * rows : (i + 1) * rows]


def grad_kernel(count, *refs):
    own, others, refs = refs[:count], refs[count : 2 * count], refs[2 * count :]
    hidden_own, d_gate_own, d_up_own, masks, w_gate, w_up, w_down = refs[:7]
    grad_gate, grad_up, grad_down = refs[7:10]
    x, cot, dense, x_part, cot_part, hidden, d_gate, d_up, out_gate, out_up, out_down, sems = refs[
        10:
    ]
    local_experts, width, hidden_units = w_gate.shape
    part = x_part.shape[0]
    rows, more = own[0].shape[0], others[0].shape[0]
    own_rows, other_rows = count * rows, count * more
    column = lax.axis_index("dp")
    base = lax.axis_index("expert") * local_experts
    mine = pl.ds(pl.multiple_of(column * part, part), part)
    theirs = pl.ds(pl.multiple_of(column * part + width, part), part)
    for i in range(count):
        cot_part[i * rows : (i + 1) * rows] = own[i][:, theirs]
        low = i * more
        x[low : low + more] = others[i][:, :width]
        cot[low : low + more] = others[i][:, width : 2 * width]
        dense[low : low + more] = others[i][:, 2 * width :].astype(jnp.float32)
        cot_part[own_rows + low : own_rows + low + more] = others[i][:, theirs]
    every = jnp.concatenate([ref[:, mine] for ref in own + others])
    x_part[...] = every.T
    chunks = hidden_units // CHUNK

    def copies(step, slot):
        expert, start = step // chunks, pl.multiple_of(step % chunks * CHUNK, CHUNK)
        cols = pl.ds(start, CHUNK)
        return [
            pltpu.make_async_copy(out_gate.at[slot], grad_gate.at[expert, :, cols], sems.at[slot, 0]),
            pltpu.make_async_copy(out_up.at[slot], grad_up.at[expert, :, cols], sems.at[slot, 1]),
            pltpu.make_async_copy(out_down.at[slot], grad_down.at[expert, cols, :], sems.at[slot, 2]),
        ]

    tile = other_rows if other_rows <= 256 else 128

    def body(step, carry):
        expert, start = step // chunks, pl.multiple_of(step % chunks * CHUNK, CHUNK)
        cols = pl.ds(start, CHUNK)
        slot = step % 2
        hidden[:own_rows] = hidden_own[expert, :, cols]
        d_gate[:own_rows] = d_gate_own[expert, :, cols]
        d_up[:own_rows] = d_up_own[expert, :, cols]
        for low in range(0, other_rows, tile):
            weights = weight_column(dense[low : low + tile], base + expert)
            terms = hidden_terms(
                x[low : low + tile],
                cot[low : low + tile],
                weights,
                masks,
                w_gate,
                w_up,
                w_down,
                expert,
                start,
            )
            put = slice(own_rows + low, own_rows + low + tile)
            hidden[put], d_gate[put], d_up[put] = terms[:3]

        @pl.when(step >= 2)
        def _():
            for copy in copies(step - 2, slot):
                copy.wait()

        out_gate[slot] = dot(x_part[...], d_gate[...], NN)
        out_up[slot] = dot(x_part[...], d_up[...], NN)
        out_down[slot] = dot(hidden[...], cot_part[...], TN)
        for copy in copies(step, slot):
            copy.start()
        return carry

    steps = local_experts * chunks
    lax.fori_loop(0, steps, body, 0)
    for step in range(max(steps - 2, 0), steps):
        for copy in copies(step, step % 2):
            copy.wait()


def sum_kernel(count, *refs):
    blocks, (expert_ids, mixed, token_grad, route_grad) = refs[:count], refs[count:]
    width = mixed.shape[1]
    lanes = (blocks[0].shape[1] - 2 * width) // 2
    for out, low in ((mixed, 0), (token_grad, width)):
        total = blocks[0][:, low : low + width].astype(jnp.float32)
        for block in blocks[1:]:
            total += block[:, low : low + width].astype(jnp.float32)
        out[...] = total.astype(out.dtype)
    inner = jnp.zeros((mixed.shape[0], lanes), jnp.float32)
    for block in blocks:
        tail = block[:, 2 * width :].astype(jnp.float32)
        inner += tail[:, :lanes] + tail[:, lanes:]
    at = lane_ids(*inner.shape)
    for k in range(expert_ids.shape[1]):
        hit = jnp.where(expert_ids[:, k : k + 1] == at, inner, 0.0)
        route_grad[:, k : k + 1] = jnp.sum(hit, axis=1, keepdims=True)


def shift(value, axis, by):
    size = lax.axis_size(axis)
    return lax.ppermute(value, axis, [(i, (i + by) % size) for i in range(size)])


def cost(flops, moved):
    return pl.CostEstimate(flops=flops, bytes_accessed=moved, transcendentals=0)


def per_device(
    tokens, expert_ids, slot_index, route_weights, w_gate, w_up, w_down, block_masks, cotangent
):
    rows, width = tokens.shape
    local_experts, _, hidden_units = w_gate.shape
    sources, columns = lax.axis_size("expert"), lax.axis_size("dp")
    lanes = -(-local_experts * sources // LANES) * LANES
    bf16, f32 = jnp.bfloat16, jnp.float32
    struct = jax.ShapeDtypeStruct
    one = 2 * local_experts * width * hidden_units

    packet = pl.pallas_call(
        pack_kernel,
        out_shape=struct((rows, 2 * width + lanes), bf16),
        in_specs=[VMEM] * 4,
        out_specs=VMEM,
        compiler_params=pltpu.CompilerParams(vmem_limit_bytes=4 * MIB),
        name="pack",
    )(tokens, cotangent, expert_ids, route_weights)

    same_column = [packet] + [shift(packet, "expert", i) for i in range(1, sources)]
    same_expert = [shift(packet, "dp", i) for i in range(1, columns)]

    weights = (w_gate, w_up, w_down)
    weights = pl.pallas_call(
        load_kernel,
        out_shape=[pltpu.VMEM(w.shape, w.dtype) for w in weights],
        in_specs=[ANY] * 3,
        out_specs=[VMEM] * 3,
        scratch_shapes=[pltpu.SemaphoreType.DMA((3,))],
        cost_estimate=cost(0, 3 * one),
        compiler_params=pltpu.CompilerParams(vmem_limit_bytes=1 * MIB),
        name="load",
    )(*weights)
    weights = [pltpu.with_memory_space_constraint(w, pltpu.VMEM) for w in weights]

    own = sources * rows
    hidden, d_gate, d_up, inner = pl.pallas_call(
        functools.partial(own_kernel, sources),
        out_shape=[struct((local_experts, own, hidden_units), bf16)] * 3
        + [struct((own, 2 * lanes), bf16)],
        in_specs=[VMEM] * sources + [SMEM] + [VMEM] * 3,
        out_specs=[VMEM] * 4,
        scratch_shapes=[pltpu.VMEM((own, width), bf16)] * 2,
        cost_estimate=cost(3 * own * one, 3 * one),
        compiler_params=pltpu.CompilerParams(vmem_limit_bytes=16 * MIB),
        name="own_hidden",
    )(*same_column, block_masks, *weights)

    theirs = jnp.concatenate(same_expert)
    others = [theirs] + [shift(theirs, "expert", i) for i in range(1, sources)]

    partials = pl.pallas_call(
        back_kernel,
        out_shape=[struct((rows, 2 * width + 2 * lanes), bf16)] * sources,
        in_specs=[VMEM] * 7,
        out_specs=[VMEM] * sources,
        cost_estimate=cost(3 * own * one, 3 * one),
        compiler_params=pltpu.CompilerParams(vmem_limit_bytes=16 * MIB),
        name="own_back",
    )(hidden, d_gate, d_up, inner, *weights)
    arrived = [partials[0]] + [shift(partials[i], "expert", -i) for i in range(1, sources)]

    part = width // columns
    other_rows = own * (columns - 1)
    everyone = own * columns
    grad_gate, grad_up, grad_down = pl.pallas_call(
        functools.partial(grad_kernel, sources),
        out_shape=[
            struct((local_experts, part, hidden_units), f32),
            struct((local_experts, part, hidden_units), f32),
            struct((local_experts, hidden_units, part), f32),
        ],
        in_specs=[VMEM] * (2 * sources + 3) + [SMEM] + [VMEM] * 3,
        out_specs=[ANY] * 3,
        scratch_shapes=[
            pltpu.VMEM((other_rows, width), bf16),
            pltpu.VMEM((other_rows, width), bf16),
            pltpu.VMEM((other_rows, lanes), f32),
            pltpu.VMEM((part, everyone), bf16),
            pltpu.VMEM((everyone, part), bf16),
            pltpu.VMEM((everyone, CHUNK), bf16),
            pltpu.VMEM((everyone, CHUNK), bf16),
            pltpu.VMEM((everyone, CHUNK), bf16),
            pltpu.VMEM((2, part, CHUNK), f32),
            pltpu.VMEM((2, part, CHUNK), f32),
            pltpu.VMEM((2, CHUNK, part), f32),
            pltpu.SemaphoreType.DMA((2, 3)),
        ],
        cost_estimate=cost((3 * other_rows + 3 * own) * one, 3 * one),
        compiler_params=pltpu.CompilerParams(vmem_limit_bytes=24 * MIB),
        name="grads",
    )(*same_column, *others, hidden, d_gate, d_up, block_masks, *weights)

    mixed, token_grad, route_grad = pl.pallas_call(
        functools.partial(sum_kernel, sources),
        out_shape=[
            struct((rows, width), bf16),
            struct((rows, width), bf16),
            struct(expert_ids.shape, f32),
        ],
        in_specs=[VMEM] * (sources + 1),
        out_specs=[VMEM] * 3,
        compiler_params=pltpu.CompilerParams(vmem_limit_bytes=4 * MIB),
        name="sum",
    )(*arrived, expert_ids)
    return (mixed, token_grad, route_grad, grad_gate, grad_up, grad_down)


def solution(mesh):
    rows = P(("groups", "expert", "dp"), None)
    experts = P("expert", None, None)
    return jax.shard_map(
        per_device,
        mesh=mesh,
        in_specs=(rows, rows, rows, rows, experts, experts, experts, P("expert", None), rows),
        out_specs=(
            rows,
            rows,
            rows,
            P(("groups", "expert"), "dp", None),
            P(("groups", "expert"), "dp", None),
            P(("groups", "expert"), None, "dp"),
        ),
        check_vma=False,
    )
```

```python
import functools

import jax
import jax.numpy as jnp
from jax import lax
from jax.experimental import pallas as pl
from jax.experimental.pallas import tpu as pltpu
from jax.sharding import PartitionSpec as P

BLK = 128
LANES = 128
CHUNK = 256
WIDE = 512
TILE = 256
MIB = 1 << 20

VMEM = pl.BlockSpec(memory_space=pltpu.VMEM)
SMEM = pl.BlockSpec(memory_space=pltpu.SMEM)
ANY = pl.BlockSpec(memory_space=pl.ANY)

NN = (((1,), (0,)), ((), ()))
NT = (((1,), (1,)), ((), ()))
TN = (((0,), (0,)), ((), ()))


def dot(a, b, dims):
    return lax.dot_general(a, b, dims, preferred_element_type=jnp.float32)


def lane_ids(rows, lanes):
    return lax.broadcasted_iota(jnp.int32, (rows, lanes), 1)


def route_kernel(cotangent, expert_ids, route_weights, packet):
    rows, width = cotangent.shape
    lanes = packet.shape[1] - width
    packet[:, :width] = cotangent[...]
    at = lane_ids(rows, lanes)
    values = route_weights[...].astype(jnp.float32)
    dense = jnp.zeros((rows, lanes), jnp.float32)
    for k in range(expert_ids.shape[1]):
        dense += jnp.where(expert_ids[:, k : k + 1] == at, values[:, k : k + 1], 0.0)
    packet[:, width:] = dense.astype(packet.dtype)


def load_kernel(*refs):
    count = len(refs) // 2
    sems = refs[-1]
    copies = [
        pltpu.make_async_copy(refs[i], refs[count + i], sems.at[i]) for i in range(count)
    ]
    for copy in copies:
        copy.start()
    for copy in copies:
        copy.wait()


def over_tiles(local_experts, tokens, body):
    tiles = tokens // TILE

    def step(index, carry):
        body(index // tiles, pl.ds(pl.multiple_of(index % tiles * TILE, TILE), TILE))
        return carry

    lax.fori_loop(0, local_experts * tiles, step, 0)


def gate_up_kernel(x, masks, w_gate, w_up, hidden, slope_up, slope_gate):
    local_experts, _, hidden_units = w_gate.shape

    def body(expert, rows):
        for start in range(0, hidden_units, CHUNK):
            cols = slice(start, start + CHUNK)
            gate_pre = dot(x[rows, :], w_gate[expert, :, cols], NN)
            up_proj = dot(x[rows, :], w_up[expert, :, cols], NN)
            at = lane_ids(1, CHUNK)
            keep = jnp.zeros((1, CHUNK), jnp.float32)
            for j in range(CHUNK // BLK):
                kept = masks[expert, start // BLK + j].astype(jnp.float32)
                keep = jnp.where(at // BLK == j, kept, keep)
            sigma = 1.0 / (1.0 + jnp.exp(-gate_pre))
            silu = gate_pre * sigma
            up_kept = up_proj * keep
            hidden[expert, rows, cols] = silu * up_kept
            slope_up[expert, rows, cols] = silu * keep
            slope_gate[expert, rows, cols] = up_kept * (sigma + silu * (1.0 - sigma))

    over_tiles(local_experts, x.shape[0], body)


def hidden_kernel(packet, hidden, slope_up, slope_gate, w_down, out, d_gate, d_up, inner):
    local_experts, hidden_units, width = w_down.shape
    tokens = packet.shape[0]
    lanes = packet.shape[1] - width
    base = lax.axis_index("expert") * local_experts
    inner[...] = jnp.zeros(inner.shape, inner.dtype)

    def body(expert, rows):
        at = lane_ids(TILE, lanes)
        dense = packet[rows, width:].astype(jnp.float32)
        hit = at == base + expert
        weights = jnp.sum(jnp.where(hit, dense, 0.0), axis=1, keepdims=True)
        total = jnp.zeros((TILE, 1), jnp.float32)
        for start in range(0, hidden_units, CHUNK):
            cols = slice(start, start + CHUNK)
            back = dot(packet[rows, :width], w_down[expert, cols, :], NT)
            units = hidden[expert, rows, cols]
            total += jnp.sum(units * back, axis=1, keepdims=True)
            back = back * weights
            out[expert, rows, cols] = (units * weights).astype(out.dtype)
            d_gate[expert, rows, cols] = (back * slope_gate[expert, rows, cols]).astype(out.dtype)
            d_up[expert, rows, cols] = (back * slope_up[expert, rows, cols]).astype(out.dtype)
        inner[rows, :] += jnp.where(hit, total, 0.0)

    over_tiles(local_experts, tokens, body)


def back_kernel(hidden, d_gate, d_up, inner, w_gate, w_up, w_down, *outs):
    local_experts, width, _ = w_gate.shape
    rows = outs[0].shape[0]
    own = rows * len(outs)
    mine = pl.ds(pl.multiple_of(lax.axis_index("dp") * own, own), own)

    def body(step, carry):
        start = pl.multiple_of(step * WIDE, WIDE)
        cols = pl.ds(start, WIDE)
        mixed = jnp.zeros((own, WIDE), jnp.float32)
        token_grad = jnp.zeros((own, WIDE), jnp.float32)
        for e in range(local_experts):
            mixed += dot(hidden[e, mine, :], w_down[e, :, cols], NN)
            token_grad += dot(d_gate[e, mine, :], w_gate[e, cols, :], NT)
            token_grad += dot(d_up[e, mine, :], w_up[e, cols, :], NT)
        for i, out in enumerate(outs):
            block = slice(i * rows, (i + 1) * rows)
            out[:, cols] = mixed[block].astype(out.dtype)
            out[:, pl.ds(start + width, WIDE)] = token_grad[block].astype(out.dtype)
        return carry

    lax.fori_loop(0, width // WIDE, body, 0)
    lanes = inner.shape[1]
    part = inner[mine, :]
    high = part.astype(jnp.bfloat16)
    low = (part - high.astype(jnp.float32)).astype(jnp.bfloat16)
    for i, out in enumerate(outs):
        block = slice(i * rows, (i + 1) * rows)
        out[:, 2 * width : 2 * width + lanes] = high[block]
        out[:, 2 * width + lanes :] = low[block]


def grad_kernel(x, packet, hidden, d_gate, d_up, *refs):
    grad_gate, grad_up, grad_down, done, x_part, cot_part, out_gate, out_up, out_down, sems = refs
    local_experts, _, hidden_units = hidden.shape
    part = x_part.shape[0]
    mine = pl.ds(pl.multiple_of(lax.axis_index("dp") * part, part), part)
    x_part[...] = x[:, mine].T
    cot_part[...] = packet[:, mine]
    done[...] = jnp.zeros(done.shape, done.dtype)
    chunks = hidden_units // CHUNK

    def copies(step, slot):
        expert, start = step // chunks, pl.multiple_of(step % chunks * CHUNK, CHUNK)
        cols = pl.ds(start, CHUNK)
        return [
            pltpu.make_async_copy(out_gate.at[slot], grad_gate.at[expert, :, cols], sems.at[slot, 0]),
            pltpu.make_async_copy(out_up.at[slot], grad_up.at[expert, :, cols], sems.at[slot, 1]),
            pltpu.make_async_copy(out_down.at[slot], grad_down.at[expert, cols, :], sems.at[slot, 2]),
        ]

    def body(step, carry):
        expert, start = step // chunks, pl.multiple_of(step % chunks * CHUNK, CHUNK)
        cols = pl.ds(start, CHUNK)
        slot = step % 2

        @pl.when(step >= 2)
        def _():
            for copy in copies(step - 2, slot):
                copy.wait()

        out_gate[slot] = dot(x_part[...], d_gate[expert, :, cols], NN)
        out_up[slot] = dot(x_part[...], d_up[expert, :, cols], NN)
        out_down[slot] = dot(hidden[expert, :, cols], cot_part[...], TN)
        for copy in copies(step, slot):
            copy.start()
        return carry

    steps = local_experts * chunks
    lax.fori_loop(0, steps, body, 0)
    for step in range(max(steps - 2, 0), steps):
        for copy in copies(step, step % 2):
            copy.wait()


def sum_kernel(count, *refs):
    blocks, (expert_ids, _, mixed, token_grad, route_grad) = refs[:count], refs[count:]
    width = mixed.shape[1]
    lanes = (blocks[0].shape[1] - 2 * width) // 2
    for out, low in ((mixed, 0), (token_grad, width)):
        total = blocks[0][:, low : low + width].astype(jnp.float32)
        for block in blocks[1:]:
            total += block[:, low : low + width].astype(jnp.float32)
        out[...] = total.astype(out.dtype)
    inner = jnp.zeros((mixed.shape[0], lanes), jnp.float32)
    for block in blocks:
        tail = block[:, 2 * width :].astype(jnp.float32)
        inner += tail[:, :lanes] + tail[:, lanes:]
    at = lane_ids(*inner.shape)
    for k in range(expert_ids.shape[1]):
        hit = jnp.where(expert_ids[:, k : k + 1] == at, inner, 0.0)
        route_grad[:, k : k + 1] = jnp.sum(hit, axis=1, keepdims=True)


def shift(value, axis, by):
    size = lax.axis_size(axis)
    return lax.ppermute(value, axis, [(i, (i + by) % size) for i in range(size)])


def cost(flops, moved):
    return pl.CostEstimate(flops=flops, bytes_accessed=moved, transcendentals=0)


def per_device(
    tokens, expert_ids, slot_index, route_weights, w_gate, w_up, w_down, block_masks, cotangent
):
    rows, width = tokens.shape
    local_experts, _, hidden_units = w_gate.shape
    sources, columns = lax.axis_size("expert"), lax.axis_size("dp")
    lanes = -(-local_experts * sources // LANES) * LANES
    own = sources * rows
    everyone = own * columns
    bf16, f32 = jnp.bfloat16, jnp.float32
    struct = jax.ShapeDtypeStruct
    one = 2 * local_experts * width * hidden_units

    packet = pl.pallas_call(
        route_kernel,
        out_shape=struct((rows, width + lanes), bf16),
        in_specs=[VMEM] * 3,
        out_specs=VMEM,
        compiler_params=pltpu.CompilerParams(vmem_limit_bytes=4 * MIB),
        name="route",
    )(cotangent, expert_ids, route_weights)
    x = lax.all_gather(tokens, ("dp", "expert"), axis=0, tiled=True)
    packets = lax.all_gather(packet, ("dp", "expert"), axis=0, tiled=True)

    weights = (w_gate, w_up, w_down)
    weights = pl.pallas_call(
        load_kernel,
        out_shape=[pltpu.VMEM(w.shape, w.dtype) for w in weights],
        in_specs=[ANY] * 3,
        out_specs=[VMEM] * 3,
        scratch_shapes=[pltpu.SemaphoreType.DMA((3,))],
        cost_estimate=cost(0, 3 * one),
        compiler_params=pltpu.CompilerParams(vmem_limit_bytes=1 * MIB),
        name="load",
    )(*weights)
    gate, up, down = [pltpu.with_memory_space_constraint(w, pltpu.VMEM) for w in weights]

    units = struct((local_experts, everyone, hidden_units), f32)
    factors = pl.pallas_call(
        gate_up_kernel,
        out_shape=[units] * 3,
        in_specs=[VMEM, SMEM, VMEM, VMEM],
        out_specs=[VMEM] * 3,
        cost_estimate=cost(2 * everyone * one, 2 * one),
        compiler_params=pltpu.CompilerParams(vmem_limit_bytes=12 * MIB),
        name="gate_up",
    )(x, block_masks, gate, up)

    units = struct((local_experts, everyone, hidden_units), bf16)
    hidden, d_gate, d_up, inner = pl.pallas_call(
        hidden_kernel,
        out_shape=[units] * 3 + [struct((everyone, lanes), f32)],
        in_specs=[VMEM] * 5,
        out_specs=[VMEM] * 4,
        cost_estimate=cost(everyone * one, one),
        compiler_params=pltpu.CompilerParams(vmem_limit_bytes=12 * MIB),
        name="hidden",
    )(packets, *factors, down)

    partials = pl.pallas_call(
        back_kernel,
        out_shape=[struct((rows, 2 * width + 2 * lanes), bf16)] * sources,
        in_specs=[VMEM] * 7,
        out_specs=[VMEM] * sources,
        cost_estimate=cost(3 * own * one, 3 * one),
        compiler_params=pltpu.CompilerParams(vmem_limit_bytes=12 * MIB),
        name="back",
    )(hidden, d_gate, d_up, inner, gate, up, down)
    stacked = jnp.stack(partials)
    arrived = lax.all_to_all(stacked, "expert", split_axis=0, concat_axis=0, tiled=True)
    arrived = [arrived[i] for i in range(sources)]

    part = width // columns
    grad_gate, grad_up, grad_down, done = pl.pallas_call(
        grad_kernel,
        out_shape=[
            struct((local_experts, part, hidden_units), f32),
            struct((local_experts, part, hidden_units), f32),
            struct((local_experts, hidden_units, part), f32),
            struct((8, LANES), f32),
        ],
        in_specs=[VMEM] * 5,
        out_specs=[ANY] * 3 + [VMEM],
        scratch_shapes=[
            pltpu.VMEM((part, everyone), bf16),
            pltpu.VMEM((everyone, part), bf16),
            pltpu.VMEM((2, part, CHUNK), f32),
            pltpu.VMEM((2, part, CHUNK), f32),
            pltpu.VMEM((2, CHUNK, part), f32),
            pltpu.SemaphoreType.DMA((2, 3)),
        ],
        cost_estimate=cost(3 * everyone * one // columns, 6 * one // columns),
        compiler_params=pltpu.CompilerParams(vmem_limit_bytes=16 * MIB),
        name="grads",
    )(x, packets, hidden, d_gate, d_up)

    mixed, token_grad, route_grad = pl.pallas_call(
        functools.partial(sum_kernel, sources),
        out_shape=[
            struct((rows, width), bf16),
            struct((rows, width), bf16),
            struct(expert_ids.shape, f32),
        ],
        in_specs=[VMEM] * (sources + 2),
        out_specs=[VMEM] * 3,
        compiler_params=pltpu.CompilerParams(vmem_limit_bytes=4 * MIB),
        name="sum",
    )(*arrived, expert_ids, done)
    return (mixed, token_grad, route_grad, grad_gate, grad_up, grad_down)


def solution(mesh):
    rows = P(("groups", "expert", "dp"), None)
    experts = P("expert", None, None)
    return jax.shard_map(
        per_device,
        mesh=mesh,
        in_specs=(rows, rows, rows, rows, experts, experts, experts, P("expert", None), rows),
        out_specs=(
            rows,
            rows,
            rows,
            P(("groups", "expert"), "dp", None),
            P(("groups", "expert"), "dp", None),
            P(("groups", "expert"), None, "dp"),
        ),
        check_vma=False,
    )
```

```python
import functools

import jax
import jax.numpy as jnp
from jax import lax
from jax.experimental import pallas as pl
from jax.experimental.pallas import tpu as pltpu
from jax.sharding import PartitionSpec as P

BLK = 128
LANES = 128
CHUNK = 256
TILE = 256
BUFFERS = 3
MIB = 1 << 20

VMEM = pl.BlockSpec(memory_space=pltpu.VMEM)
SMEM = pl.BlockSpec(memory_space=pltpu.SMEM)
HBM = pl.BlockSpec(memory_space=pltpu.HBM)

NN = (((1,), (0,)), ((), ()))
NT = (((1,), (1,)), ((), ()))
TN = (((0,), (0,)), ((), ()))


def dot(a, b, dims):
    return lax.dot_general(a, b, dims, preferred_element_type=jnp.float32)


def ids_along(shape, axis):
    return lax.broadcasted_iota(jnp.int32, shape, axis)


def aligned(index, size):
    return pl.ds(pl.multiple_of(index * size, size), size)


def route_kernel(cotangent, expert_ids, route_weights, packet):
    rows, width = cotangent.shape
    lanes = packet.shape[1] - width
    packet[:, :width] = cotangent[...]
    at = ids_along((lanes, rows), 0)
    values = route_weights[...].astype(jnp.float32)
    dense = jnp.zeros((lanes, rows), jnp.float32)
    for k in range(expert_ids.shape[0]):
        dense += jnp.where(expert_ids[k : k + 1, :] == at, values[k : k + 1, :], 0.0)
    packet[:, width:] = dense.T.astype(packet.dtype)


def stream(steps, copies, body):
    ahead = BUFFERS - 1
    for step in range(min(ahead, steps)):
        for copy in copies(step, step % BUFFERS):
            copy.start()

    def turn(step, carry):
        later = step + ahead

        @pl.when(later < steps)
        def _():
            for copy in copies(later, lax.rem(later, BUFFERS)):
                copy.start()

        slot = lax.rem(step, BUFFERS)
        for copy in copies(step, slot):
            copy.wait()
        body(step, slot)
        return carry

    lax.fori_loop(0, steps, turn, 0)


def over_tiles(tokens, body):
    if tokens == TILE:
        body(slice(0, TILE))
    else:

        def turn(tile, carry):
            body(aligned(tile, TILE))
            return carry

        lax.fori_loop(0, tokens // TILE, turn, 0)


def gate_up_kernel(x, masks, w_gate, w_up, hidden, slope_up, slope_gate, gate_buf, up_buf, sems):
    local_experts, _, hidden_units = w_gate.shape
    chunks = hidden_units // CHUNK

    def place(step):
        return step // chunks, lax.rem(step, chunks)

    def copies(step, slot):
        expert, chunk = place(step)
        cols = aligned(chunk, CHUNK)
        return [
            pltpu.make_async_copy(w_gate.at[expert, :, cols], gate_buf.at[slot], sems.at[slot, 0]),
            pltpu.make_async_copy(w_up.at[expert, :, cols], up_buf.at[slot], sems.at[slot, 1]),
        ]

    def body(step, slot):
        expert, chunk = place(step)
        cols = aligned(chunk, CHUNK)
        at = ids_along((1, CHUNK), 1)
        keep = jnp.zeros((1, CHUNK), jnp.float32)
        for j in range(CHUNK // BLK):
            kept = masks[expert, chunk * (CHUNK // BLK) + j].astype(jnp.float32)
            keep = jnp.where(at // BLK == j, kept, keep)

        def tile(rows):
            gate_pre = dot(x[rows, :], gate_buf[slot], NN)
            up_proj = dot(x[rows, :], up_buf[slot], NN)
            sigma = 1.0 / (1.0 + jnp.exp(-gate_pre))
            silu = gate_pre * sigma
            up_kept = up_proj * keep
            hidden[expert, rows, cols] = silu * up_kept
            slope_up[expert, rows, cols] = silu * keep
            slope_gate[expert, rows, cols] = up_kept * (sigma + silu * (1.0 - sigma))

        over_tiles(x.shape[0], tile)

    stream(local_experts * chunks, copies, body)


def hidden_kernel(order, *refs):
    packet, units, slope_up, slope_gate, w_gate, w_up, w_down, hidden, d_gate, d_up = refs[:10]
    outs, refs = refs[10 : 10 + len(order)], refs[10 + len(order) :]
    inner, mixed, token_grad, gate_buf, up_buf, down_buf, sems = refs
    local_experts, hidden_units, width = w_down.shape
    tokens, part = mixed.shape
    lanes = packet.shape[1] - width
    chunks = hidden_units // CHUNK
    base = lax.axis_index("expert") * local_experts
    mine = aligned(lax.axis_index("dp"), part)
    inner[...] = jnp.zeros(inner.shape, inner.dtype)
    mixed[...] = jnp.zeros(mixed.shape, mixed.dtype)
    token_grad[...] = jnp.zeros(token_grad.shape, token_grad.dtype)

    def place(step):
        return step // chunks, lax.rem(step, chunks)

    def copies(step, slot):
        expert, chunk = place(step)
        cols = aligned(chunk, CHUNK)
        return [
            pltpu.make_async_copy(w_down.at[expert, cols, :], down_buf.at[slot], sems.at[slot, 0]),
            pltpu.make_async_copy(w_gate.at[expert, mine, cols], gate_buf.at[slot], sems.at[slot, 1]),
            pltpu.make_async_copy(w_up.at[expert, mine, cols], up_buf.at[slot], sems.at[slot, 2]),
        ]

    def body(step, slot):
        expert, chunk = place(step)
        cols = aligned(chunk, CHUNK)

        def tile(rows):
            back = dot(packet[rows, :width], down_buf[slot], NT)
            dense = packet[rows, width:].astype(jnp.float32)
            hit = ids_along((TILE, lanes), 1) == base + expert
            weights = jnp.sum(jnp.where(hit, dense, 0.0), axis=1, keepdims=True)
            part_units = units[expert, rows, cols]
            total = jnp.sum(part_units * back, axis=1, keepdims=True)
            inner[rows, :] += jnp.where(hit, total, 0.0)
            back = back * weights
            new_hidden = (part_units * weights).astype(jnp.bfloat16)
            new_gate = (back * slope_gate[expert, rows, cols]).astype(jnp.bfloat16)
            new_up = (back * slope_up[expert, rows, cols]).astype(jnp.bfloat16)
            hidden[expert, rows, cols] = new_hidden
            d_gate[expert, rows, cols] = new_gate
            d_up[expert, rows, cols] = new_up
            mixed[rows, :] += dot(new_hidden, down_buf[slot, :, mine], NN)
            token_grad[rows, :] += dot(new_gate, gate_buf[slot], NT) + dot(new_up, up_buf[slot], NT)

        over_tiles(tokens, tile)

    stream(local_experts * chunks, copies, body)
    rows = outs[0].shape[0]
    for i, out in enumerate(outs):
        block = slice(i * rows, (i + 1) * rows)
        out[:, :part] = mixed[block].astype(out.dtype)
        out[:, part : 2 * part] = token_grad[block].astype(out.dtype)
        high = inner[block].astype(jnp.bfloat16)
        out[:, 2 * part : 2 * part + lanes] = high
        out[:, 2 * part + lanes :] = (inner[block] - high.astype(jnp.float32)).astype(jnp.bfloat16)


def write_out(steps, place, outs, bufs, sems, body):
    def copies(step, slot):
        return [
            pltpu.make_async_copy(buf.at[slot], out.at[place(step)], sems.at[slot, i])
            for i, (out, buf) in enumerate(zip(outs, bufs))
        ]

    def turn(step, carry):
        slot = lax.rem(step, 2)

        @pl.when(step >= 2)
        def _():
            for copy in copies(step - 2, slot):
                copy.wait()

        body(step, slot)
        for copy in copies(step, slot):
            copy.start()
        return carry

    lax.fori_loop(0, steps, turn, 0)
    for step in range(max(steps - 2, 0), steps):
        for copy in copies(step, step % 2):
            copy.wait()


def grad_in_kernel(x, d_gate, d_up, grad_gate, grad_up, done, x_part, out_gate, out_up, sems):
    local_experts, _, hidden_units = d_gate.shape
    part = x_part.shape[0]
    x_part[...] = x[:, aligned(lax.axis_index("dp"), part)].T
    done[...] = jnp.zeros(done.shape, done.dtype)
    chunks = hidden_units // CHUNK

    def place(step):
        return step // chunks, slice(None), aligned(lax.rem(step, chunks), CHUNK)

    def body(step, slot):
        out_gate[slot] = dot(x_part[...], d_gate[place(step)], NN)
        out_up[slot] = dot(x_part[...], d_up[place(step)], NN)

    write_out(
        local_experts * chunks, place, (grad_gate, grad_up), (out_gate, out_up), sems, body
    )


def grad_out_kernel(packet, hidden, after, grad_down, done, cot_part, out_down, sems):
    local_experts, _, hidden_units = hidden.shape
    part = cot_part.shape[1]
    cot_part[...] = packet[:, aligned(lax.axis_index("dp"), part)]
    done[...] = jnp.zeros(done.shape, done.dtype)
    chunks = hidden_units // CHUNK

    def place(step):
        return step // chunks, aligned(lax.rem(step, chunks), CHUNK), slice(None)

    def body(step, slot):
        units = hidden[step // chunks, :, aligned(lax.rem(step, chunks), CHUNK)]
        out_down[slot] = dot(units, cot_part[...], TN)

    write_out(local_experts * chunks, place, (grad_down,), (out_down,), sems, body)


def reduce_kernel(count, *refs):
    blocks, refs = refs[:count], refs[count:]
    expert_ids, after, route_grad = refs[:3]
    outs, done = refs[3:-1], refs[-1]
    done[...] = jnp.zeros(done.shape, done.dtype)
    rows, both = outs[0].shape
    lanes = (blocks[0].shape[1] - both) // 2
    for j, out in enumerate(outs):
        total = jnp.zeros((rows, both), jnp.float32)
        for block in blocks:
            total += block[j * rows : (j + 1) * rows, :both].astype(jnp.float32)
        out[...] = total.astype(out.dtype)
    inner = jnp.zeros((rows, lanes), jnp.float32)
    for block in blocks:
        tail = block[:rows, both:].astype(jnp.float32)
        inner += tail[:, :lanes] + tail[:, lanes:]
    inner = inner.T
    at = ids_along(inner.shape, 0)
    for k in range(expert_ids.shape[0]):
        hit = jnp.where(expert_ids[k : k + 1, :] == at, inner, 0.0)
        route_grad[k : k + 1, :] = jnp.sum(hit, axis=0, keepdims=True)


def join_kernel(order, *refs):
    blocks, (after, mixed, token_grad) = refs[: len(order)], refs[len(order) :]
    part = blocks[0].shape[1] // 2
    column = lax.axis_index("dp")
    for other, block in zip(order, blocks):
        cols = aligned(column ^ other, part)
        mixed[:, cols] = block[:, :part]
        token_grad[:, cols] = block[:, part:]


def swap(value, axis, mask):
    size = lax.axis_size(axis)
    return lax.ppermute(value, axis, [(i, i ^ mask) for i in range(size)])


def gather(value, axis, masks):
    for mask in masks:
        value = jnp.concatenate([value, swap(value, axis, mask)])
    return value


def masks_of(size):
    masks = [1 << bit for bit in reversed(range(size.bit_length() - 1))]
    order = [0]
    for mask in masks:
        order = order + [other ^ mask for other in order]
    return masks, order


def cost(flops, moved):
    return pl.CostEstimate(flops=flops, bytes_accessed=moved, transcendentals=0)


def params(mib):
    return pltpu.CompilerParams(vmem_limit_bytes=mib * MIB)


def per_device(
    tokens, expert_ids, slot_index, route_weights, w_gate, w_up, w_down, block_masks, cotangent
):
    rows, width = tokens.shape
    local_experts, _, hidden_units = w_gate.shape
    sources, columns = lax.axis_size("expert"), lax.axis_size("dp")
    expert_masks, expert_order = masks_of(sources)
    column_masks, column_order = masks_of(columns)
    lanes = -(-local_experts * sources // LANES) * LANES
    part = width // columns
    everyone = sources * columns * rows
    bf16, f32 = jnp.bfloat16, jnp.float32
    struct = jax.ShapeDtypeStruct
    one = 2 * local_experts * width * hidden_units
    dummy = struct((8, LANES), f32)
    ids_t = expert_ids.T
    w_gate, w_up, w_down = [
        pltpu.with_memory_space_constraint(w, pltpu.HBM) for w in (w_gate, w_up, w_down)
    ]

    packet = pl.pallas_call(
        route_kernel,
        out_shape=struct((rows, width + lanes), bf16),
        in_specs=[VMEM] * 3,
        out_specs=VMEM,
        compiler_params=params(4),
        name="route",
    )(cotangent, ids_t, route_weights.T)
    x = gather(gather(tokens, "dp", column_masks), "expert", expert_masks)
    packets = gather(gather(packet, "dp", column_masks), "expert", expert_masks)

    units = struct((local_experts, everyone, hidden_units), f32)
    factors = pl.pallas_call(
        gate_up_kernel,
        out_shape=[units] * 3,
        in_specs=[VMEM, SMEM, HBM, HBM],
        out_specs=[VMEM] * 3,
        scratch_shapes=[pltpu.VMEM((BUFFERS, width, CHUNK), bf16)] * 2
        + [pltpu.SemaphoreType.DMA((BUFFERS, 2))],
        cost_estimate=cost(2 * everyone * one, 2 * one),
        compiler_params=params(16),
        name="gate_up",
    )(x, block_masks, w_gate, w_up)

    units = struct((local_experts, everyone, hidden_units), bf16)
    hidden, d_gate, d_up, *partials = pl.pallas_call(
        functools.partial(hidden_kernel, expert_order),
        out_shape=[units] * 3
        + [struct((columns * rows, 2 * part + 2 * lanes), bf16)] * sources,
        in_specs=[VMEM] * 4 + [HBM] * 3,
        out_specs=[VMEM] * (3 + sources),
        scratch_shapes=[
            pltpu.VMEM((everyone, lanes), f32),
            pltpu.VMEM((everyone, part), f32),
            pltpu.VMEM((everyone, part), f32),
            pltpu.VMEM((BUFFERS, part, CHUNK), bf16),
            pltpu.VMEM((BUFFERS, part, CHUNK), bf16),
            pltpu.VMEM((BUFFERS, CHUNK, width), bf16),
            pltpu.SemaphoreType.DMA((BUFFERS, 3)),
        ],
        cost_estimate=cost(2 * everyone * one, 2 * one),
        compiler_params=params(24),
        name="hidden",
    )(packets, *factors, w_gate, w_up, w_down)
    arrived = [
        swap(partial, "expert", other) if other else partial
        for other, partial in zip(expert_order, partials)
    ]

    grad_gate, grad_up, done_in = pl.pallas_call(
        grad_in_kernel,
        out_shape=[struct((local_experts, part, hidden_units), f32)] * 2 + [dummy],
        in_specs=[VMEM] * 3,
        out_specs=[HBM] * 2 + [VMEM],
        scratch_shapes=[
            pltpu.VMEM((part, everyone), bf16),
            pltpu.VMEM((2, part, CHUNK), f32),
            pltpu.VMEM((2, part, CHUNK), f32),
            pltpu.SemaphoreType.DMA((2, 2)),
        ],
        cost_estimate=cost(2 * everyone * one // columns, 4 * one // columns),
        compiler_params=params(16),
        name="grad_in",
    )(x, d_gate, d_up)

    route_grad, *blocks, done_sum = pl.pallas_call(
        functools.partial(reduce_kernel, sources),
        out_shape=[struct(ids_t.shape, f32)] + [struct((rows, 2 * part), bf16)] * columns + [dummy],
        in_specs=[VMEM] * (sources + 2),
        out_specs=[VMEM] * (columns + 2),
        compiler_params=params(4),
        name="reduce",
    )(*arrived, ids_t, done_in)
    blocks = [
        swap(block, "dp", other) if other else block for other, block in zip(column_order, blocks)
    ]

    grad_down, done_out = pl.pallas_call(
        grad_out_kernel,
        out_shape=[struct((local_experts, hidden_units, part), f32), dummy],
        in_specs=[VMEM] * 3,
        out_specs=[HBM, VMEM],
        scratch_shapes=[
            pltpu.VMEM((everyone, part), bf16),
            pltpu.VMEM((2, CHUNK, part), f32),
            pltpu.SemaphoreType.DMA((2, 1)),
        ],
        cost_estimate=cost(everyone * one // columns, 2 * one // columns),
        compiler_params=params(16),
        name="grad_out",
    )(packets, hidden, done_sum)

    mixed, token_grad = pl.pallas_call(
        functools.partial(join_kernel, column_order),
        out_shape=[struct((rows, width), bf16)] * 2,
        in_specs=[VMEM] * (columns + 1),
        out_specs=[VMEM] * 2,
        compiler_params=params(4),
        name="join",
    )(*blocks, done_out)
    return (mixed, token_grad, route_grad.T, grad_gate, grad_up, grad_down)


def solution(mesh):
    rows = P(("groups", "expert", "dp"), None)
    experts = P("expert", None, None)
    return jax.shard_map(
        per_device,
        mesh=mesh,
        in_specs=(rows, rows, rows, rows, experts, experts, experts, P("expert", None), rows),
        out_specs=(
            rows,
            rows,
            rows,
            P(("groups", "expert"), "dp", None),
            P(("groups", "expert"), "dp", None),
            P(("groups", "expert"), None, "dp"),
        ),
        check_vma=False,
    )
```

```python
import functools

import jax
import jax.numpy as jnp
from jax import lax
from jax.experimental import pallas as pl
from jax.experimental.pallas import tpu as pltpu
from jax.sharding import PartitionSpec as P

BLK = 128
LANES = 128
CHUNK = 256
TILE = 256
MIB = 1 << 20

VMEM = pl.BlockSpec(memory_space=pltpu.VMEM)
SMEM = pl.BlockSpec(memory_space=pltpu.SMEM)
HBM = pl.BlockSpec(memory_space=pltpu.HBM)

NN = (((1,), (0,)), ((), ()))
NT = (((1,), (1,)), ((), ()))


def dot(a, b, dims):
    return lax.dot_general(a, b, dims, preferred_element_type=jnp.float32)


def ids_along(shape, axis):
    return lax.broadcasted_iota(jnp.int32, shape, axis)


def aligned(index, size):
    return pl.ds(pl.multiple_of(index * size, size), size)


def route_kernel(
    tokens, cotangent, expert_ids, route_weights, own_tokens, packet, ids, values, sems
):
    rows, width = tokens.shape
    lanes = packet.shape[1] - width
    copies = [
        pltpu.make_async_copy(expert_ids, ids, sems.at[0]),
        pltpu.make_async_copy(route_weights, values, sems.at[1]),
        pltpu.make_async_copy(tokens, own_tokens, sems.at[2]),
        pltpu.make_async_copy(cotangent, packet.at[:, :width], sems.at[3]),
    ]
    for copy in copies:
        copy.start()
    for copy in copies:
        copy.wait()
    at = ids_along((lanes, rows), 0)
    weights = values[...].astype(jnp.float32)
    dense = jnp.zeros((lanes, rows), jnp.float32)
    for k in range(ids.shape[0]):
        dense += jnp.where(ids[k : k + 1, :] == at, weights[k : k + 1, :], 0.0)
    packet[:, width:] = dense.T.astype(packet.dtype)


def load_kernel(source, value, target, same, sem):
    copy = pltpu.make_async_copy(source, target, sem)
    copy.start()
    same[...] = value[...]
    copy.wait()


def over_tiles(tokens, body):
    if tokens == TILE:
        body(slice(0, TILE))
    else:

        def turn(tile, carry):
            body(aligned(tile, TILE))
            return carry

        lax.fori_loop(0, tokens // TILE, turn, 0)


def gate_up_kernel(x, masks, gate, up, hidden, slope_up, slope_gate):
    local_experts, _, hidden_units = gate.shape
    bf16 = jnp.bfloat16

    def one_expert(expert, carry):
        def tile(rows):
            for start in range(0, hidden_units, CHUNK):
                cols = slice(start, start + CHUNK)
                gate_pre = dot(x[rows, :], gate[expert, :, cols], NN)
                up_proj = dot(x[rows, :], up[expert, :, cols], NN)
                at = ids_along((1, CHUNK), 1)
                keep = jnp.zeros((1, CHUNK), jnp.float32)
                for j in range(CHUNK // BLK):
                    kept = masks[expert, start // BLK + j].astype(jnp.float32)
                    keep = jnp.where(at // BLK == j, kept, keep)
                sigma = 1.0 / (1.0 + jnp.exp(-gate_pre))
                silu = gate_pre * sigma
                up_kept = up_proj * keep
                hidden[expert, rows, cols] = (silu * up_kept).astype(bf16)
                slope_up[expert, rows, cols] = (silu * keep).astype(bf16)
                slope = up_kept * (sigma + silu * (1.0 - sigma))
                slope_gate[expert, rows, cols] = slope.astype(bf16)

        over_tiles(x.shape[0], tile)
        return carry

    lax.fori_loop(0, local_experts, one_expert, 0)


def stack(pieces, target, cols=slice(None)):
    rows = pieces[0].shape[0]
    for i, piece in enumerate(pieces):
        target[i * rows : (i + 1) * rows] = piece[:, cols]


def hidden_kernel(count, *refs):
    pieces, refs = refs[:count], refs[count:]
    units, slope_up, slope_gate, gate, up, w_down, hidden, d_gate, d_up = refs[:9]
    outs, refs = refs[9 : 9 + count], refs[9 + count :]
    packet, inner, mixed, token_grad, down_buf, sems = refs
    local_experts, hidden_units, width = w_down.shape
    tokens, part = mixed.shape
    lanes = packet.shape[1] - width
    base = lax.axis_index("expert") * local_experts
    mine = aligned(lax.axis_index("dp"), part)
    inner[...] = jnp.zeros(inner.shape, inner.dtype)
    mixed[...] = jnp.zeros(mixed.shape, mixed.dtype)
    token_grad[...] = jnp.zeros(token_grad.shape, token_grad.dtype)

    def copies(expert):
        slot = lax.rem(expert, 2)
        return [
            pltpu.make_async_copy(
                w_down.at[expert, slice(start, start + CHUNK), :],
                down_buf.at[slot, slice(start, start + CHUNK), :],
                sems.at[slot, start // CHUNK],
            )
            for start in range(0, hidden_units, CHUNK)
        ]

    for copy in copies(0):
        copy.start()
    stack(pieces, packet)

    def one_expert(expert, carry):
        @pl.when(expert + 1 < local_experts)
        def _():
            for copy in copies(expert + 1):
                copy.start()

        down = down_buf.at[lax.rem(expert, 2)]
        for copy in copies(expert):
            copy.wait()

        def tile(rows):
            dense = packet[rows, width:].astype(jnp.float32)
            hit = ids_along((TILE, lanes), 1) == base + expert
            weights = jnp.sum(jnp.where(hit, dense, 0.0), axis=1, keepdims=True)
            total = jnp.zeros((TILE, 1), jnp.float32)
            for start in range(0, hidden_units, CHUNK):
                cols = slice(start, start + CHUNK)
                back = dot(packet[rows, :width], down[cols, :], NT)
                part_units = units[expert, rows, cols].astype(jnp.float32)
                total += jnp.sum(part_units * back, axis=1, keepdims=True)
                back = back * weights
                bf16, f32 = jnp.bfloat16, jnp.float32
                hidden[expert, rows, cols] = (part_units * weights).astype(bf16)
                d_gate[expert, rows, cols] = (back * slope_gate[expert, rows, cols].astype(f32)).astype(bf16)
                d_up[expert, rows, cols] = (back * slope_up[expert, rows, cols].astype(f32)).astype(bf16)
            inner[rows, :] += jnp.where(hit, total, 0.0)
            mixed[rows, :] += dot(hidden[expert, rows, :], down[:, mine], NN)
            token_grad[rows, :] += dot(d_gate[expert, rows, :], gate[expert, mine, :], NT) + dot(
                d_up[expert, rows, :], up[expert, mine, :], NT
            )

        over_tiles(tokens, tile)
        return carry

    lax.fori_loop(0, local_experts, one_expert, 0)
    rows = outs[0].shape[0]
    for i, out in enumerate(outs):
        block = slice(i * rows, (i + 1) * rows)
        out[:, :part] = mixed[block].astype(out.dtype)
        out[:, part : 2 * part] = token_grad[block].astype(out.dtype)
        high = inner[block].astype(jnp.bfloat16)
        out[:, 2 * part : 2 * part + lanes] = high
        out[:, 2 * part + lanes :] = (inner[block] - high.astype(jnp.float32)).astype(jnp.bfloat16)


def write_out(steps, place, outs, bufs, sems, body):
    def copies(step, slot):
        return [
            pltpu.make_async_copy(buf.at[slot], out.at[place(step)], sems.at[slot, i])
            for i, (out, buf) in enumerate(zip(outs, bufs))
        ]

    def turn(step, carry):
        slot = lax.rem(step, 2)

        @pl.when(step >= 2)
        def _():
            for copy in copies(step - 2, slot):
                copy.wait()

        body(step, slot)
        for copy in copies(step, slot):
            copy.start()
        return carry

    lax.fori_loop(0, steps, turn, 0)
    for step in range(max(steps - 2, 0), steps):
        for copy in copies(step, step % 2):
            copy.wait()


def grad_in_kernel(x, d_gate, d_up, grad_gate, grad_up, done, x_part, out_gate, out_up, sems):
    local_experts, _, hidden_units = d_gate.shape
    part, rows = x_part.shape[0], out_gate.shape[1]
    x_part[...] = x[:, aligned(lax.axis_index("dp"), part)].T
    done[...] = jnp.zeros(done.shape, done.dtype)
    blocks = part // rows

    def place(step):
        return step // blocks, aligned(lax.rem(step, blocks), rows), slice(None)

    def body(step, slot):
        expert, block, _ = place(step)
        out_gate[slot] = dot(x_part[block, :], d_gate[expert], NN)
        out_up[slot] = dot(x_part[block, :], d_up[expert], NN)

    write_out(
        local_experts * blocks, place, (grad_gate, grad_up), (out_gate, out_up), sems, body
    )


def grad_out_kernel(count, *refs):
    pieces, refs = refs[:count], refs[count:]
    hidden, after, grad_down, done, cot_part, out_down, sems = refs
    local_experts, _, hidden_units = hidden.shape
    part = cot_part.shape[1]
    stack(pieces, cot_part, aligned(lax.axis_index("dp"), part))
    done[...] = jnp.zeros(done.shape, done.dtype)
    chunks = hidden_units // CHUNK

    def place(step):
        return step // chunks, aligned(lax.rem(step, chunks), CHUNK), slice(None)

    def body(step, slot):
        units = hidden[step // chunks, :, aligned(lax.rem(step, chunks), CHUNK)]
        out_down[slot] = dot(units.T, cot_part[...], NN)

    write_out(local_experts * chunks, place, (grad_down,), (out_down,), sems, body)


def reduce_kernel(count, *refs):
    blocks, refs = refs[:count], refs[count:]
    expert_ids, after, route_grad = refs[:3]
    outs, done = refs[3:-1], refs[-1]
    done[...] = jnp.zeros(done.shape, done.dtype)
    rows, both = outs[0].shape
    lanes = (blocks[0].shape[1] - both) // 2
    for j, out in enumerate(outs):
        total = jnp.zeros((rows, both), jnp.float32)
        for block in blocks:
            total += block[j * rows : (j + 1) * rows, :both].astype(jnp.float32)
        out[...] = total.astype(out.dtype)
    inner = jnp.zeros((rows, lanes), jnp.float32)
    for block in blocks:
        tail = block[:rows, both:].astype(jnp.float32)
        inner += tail[:, :lanes] + tail[:, lanes:]
    inner = inner.T
    at = ids_along(inner.shape, 0)
    for k in range(expert_ids.shape[0]):
        hit = jnp.where(expert_ids[k : k + 1, :] == at, inner, 0.0)
        route_grad[k : k + 1, :] = jnp.sum(hit, axis=0, keepdims=True)


def join_kernel(order, *refs):
    blocks, (after, mixed, token_grad) = refs[: len(order)], refs[len(order) :]
    part = blocks[0].shape[1] // 2
    column = lax.axis_index("dp")
    for other, block in zip(order, blocks):
        cols = aligned(column ^ other, part)
        mixed[:, cols] = block[:, :part]
        token_grad[:, cols] = block[:, part:]


def swap(value, axis, mask):
    size = lax.axis_size(axis)
    return lax.ppermute(value, axis, [(i, i ^ mask) for i in range(size)])


def exchange(value, axis, masks):
    return [swap(value, axis, mask) for mask in masks]


def in_hbm(array):
    return pltpu.with_memory_space_constraint(array, pltpu.HBM)


def in_vmem(array):
    return pltpu.with_memory_space_constraint(array, pltpu.VMEM)


def cost(flops, moved):
    return pl.CostEstimate(flops=flops, bytes_accessed=moved, transcendentals=0)


def params(mib):
    return pltpu.CompilerParams(vmem_limit_bytes=mib * MIB)


def per_device(
    tokens, expert_ids, slot_index, route_weights, w_gate, w_up, w_down, block_masks, cotangent
):
    rows, width = tokens.shape
    local_experts, _, hidden_units = w_gate.shape
    sources, columns = lax.axis_size("expert"), lax.axis_size("dp")
    column_order = list(range(columns))
    chips = list(range(2, sources, 2))
    expert_order = [0] + chips + [chip ^ 1 for chip in [0] + chips]
    lanes = -(-local_experts * sources // LANES) * LANES
    part = width // columns
    everyone = sources * columns * rows
    bf16, f32 = jnp.bfloat16, jnp.float32
    struct = jax.ShapeDtypeStruct
    one = 2 * local_experts * width * hidden_units
    dummy = struct((8, LANES), f32)
    ids_t = expert_ids.T
    w_gate, w_up, w_down = [in_hbm(w) for w in (w_gate, w_up, w_down)]

    own_tokens, packet = pl.pallas_call(
        route_kernel,
        out_shape=[struct(tokens.shape, bf16), struct((rows, width + lanes), bf16)],
        in_specs=[HBM] * 4,
        out_specs=[VMEM] * 2,
        scratch_shapes=[
            pltpu.VMEM(ids_t.shape, jnp.int32),
            pltpu.VMEM(ids_t.shape, bf16),
            pltpu.SemaphoreType.DMA((4,)),
        ],
        compiler_params=params(2),
        name="route",
    )(*[in_hbm(a) for a in (tokens, cotangent, ids_t, route_weights.T)])

    def load(weight, value, name):
        return pl.pallas_call(
            load_kernel,
            out_shape=[
                pltpu.VMEM(weight.shape, weight.dtype),
                struct(value.shape, value.dtype),
            ],
            in_specs=[HBM, VMEM],
            out_specs=[VMEM] * 2,
            scratch_shapes=[pltpu.SemaphoreType.DMA],
            cost_estimate=cost(0, one),
            compiler_params=params(1),
            name=name,
        )(weight, value)

    arrived = exchange(own_tokens, "dp", column_order[1:])
    gate, own_tokens = load(w_gate, own_tokens, "load_gate")
    x_column = jnp.concatenate([own_tokens] + arrived)
    across = exchange(x_column, "expert", chips)
    packet_column = jnp.concatenate([packet] + exchange(packet, "dp", column_order[1:]))
    packet_column, across = lax.optimization_barrier((packet_column, across))
    up, x_column = load(w_up, x_column, "load_up")
    gate, up = in_vmem(gate), in_vmem(up)
    x = jnp.concatenate([x_column] + across)
    x = jnp.concatenate([x, swap(x, "expert", 1)])
    pieces = exchange(packet_column, "expert", expert_order[1:])

    units = struct((local_experts, everyone, hidden_units), bf16)
    factors = pl.pallas_call(
        gate_up_kernel,
        out_shape=[units] * 3,
        in_specs=[VMEM, SMEM, VMEM, VMEM],
        out_specs=[VMEM] * 3,
        cost_estimate=cost(2 * everyone * one, 2 * one),
        compiler_params=params(6),
        name="gate_up",
    )(x, block_masks, gate, up)
    pieces = [packet_column] + pieces

    hidden, d_gate, d_up, *partials = pl.pallas_call(
        functools.partial(hidden_kernel, sources),
        out_shape=[units] * 3
        + [struct((columns * rows, 2 * part + 2 * lanes), bf16)] * sources,
        in_specs=[VMEM] * (5 + sources) + [HBM],
        out_specs=[VMEM] * (3 + sources),
        scratch_shapes=[
            pltpu.VMEM((everyone, width + lanes), bf16),
            pltpu.VMEM((everyone, lanes), f32),
            pltpu.VMEM((everyone, part), f32),
            pltpu.VMEM((everyone, part), f32),
            pltpu.VMEM((min(2, local_experts), hidden_units, width), bf16),
            pltpu.SemaphoreType.DMA((2, hidden_units // CHUNK)),
        ],
        cost_estimate=cost(2 * everyone * one, 2 * one),
        compiler_params=params(12 + (everyone - TILE) * (2 * part + lanes) * 14 // MIB),
        name="hidden",
    )(*pieces, *factors, gate, up, w_down)
    arrived = [
        swap(partial, "expert", other) if other else partial
        for other, partial in zip(expert_order, partials)
    ]

    grad_gate, grad_up, done_in = pl.pallas_call(
        grad_in_kernel,
        out_shape=[struct((local_experts, part, hidden_units), f32)] * 2 + [dummy],
        in_specs=[VMEM] * 3,
        out_specs=[HBM] * 2 + [VMEM],
        scratch_shapes=[
            pltpu.VMEM((part, everyone), bf16),
            pltpu.VMEM((2, min(part, CHUNK), hidden_units), f32),
            pltpu.VMEM((2, min(part, CHUNK), hidden_units), f32),
            pltpu.SemaphoreType.DMA((2, 2)),
        ],
        cost_estimate=cost(2 * everyone * one // columns, 4 * one // columns),
        compiler_params=params(16),
        name="grad_in",
    )(x, d_gate, d_up)

    route_grad, *blocks, done_sum = pl.pallas_call(
        functools.partial(reduce_kernel, sources),
        out_shape=[struct(ids_t.shape, f32)] + [struct((rows, 2 * part), bf16)] * columns + [dummy],
        in_specs=[VMEM] * (sources + 2),
        out_specs=[VMEM] * (columns + 2),
        compiler_params=params(4),
        name="reduce",
    )(*arrived, ids_t, done_in)
    blocks = [
        swap(block, "dp", other) if other else block for other, block in zip(column_order, blocks)
    ]

    grad_down, done_out = pl.pallas_call(
        functools.partial(grad_out_kernel, sources),
        out_shape=[struct((local_experts, hidden_units, part), f32), dummy],
        in_specs=[VMEM] * (2 + sources),
        out_specs=[HBM, VMEM],
        scratch_shapes=[
            pltpu.VMEM((everyone, part), bf16),
            pltpu.VMEM((2, CHUNK, part), f32),
            pltpu.SemaphoreType.DMA((2, 1)),
        ],
        cost_estimate=cost(everyone * one // columns, 2 * one // columns),
        compiler_params=params(16),
        name="grad_out",
    )(*pieces, hidden, done_sum)

    mixed, token_grad = pl.pallas_call(
        functools.partial(join_kernel, column_order),
        out_shape=[struct((rows, width), bf16)] * 2,
        in_specs=[VMEM] * (columns + 1),
        out_specs=[VMEM] * 2,
        compiler_params=params(4),
        name="join",
    )(*blocks, done_out)
    return (mixed, token_grad, route_grad.T, grad_gate, grad_up, grad_down)


def solution(mesh):
    rows = P(("groups", "expert", "dp"), None)
    experts = P("expert", None, None)
    return jax.shard_map(
        per_device,
        mesh=mesh,
        in_specs=(rows, rows, rows, rows, experts, experts, experts, P("expert", None), rows),
        out_specs=(
            rows,
            rows,
            rows,
            P(("groups", "expert"), "dp", None),
            P(("groups", "expert"), "dp", None),
            P(("groups", "expert"), None, "dp"),
        ),
        check_vma=False,
    )
```

```python
import functools

import jax
import jax.numpy as jnp
from jax import lax
from jax.experimental import pallas as pl
from jax.experimental.pallas import tpu as pltpu
from jax.sharding import PartitionSpec as P

BLK = 128
LANES = 128
CHUNK = 256
TILE = 256
MIB = 1 << 20

VMEM = pl.BlockSpec(memory_space=pltpu.VMEM)
SMEM = pl.BlockSpec(memory_space=pltpu.SMEM)
HBM = pl.BlockSpec(memory_space=pltpu.HBM)

NN = (((1,), (0,)), ((), ()))
NT = (((1,), (1,)), ((), ()))


def dot(a, b, dims):
    return lax.dot_general(a, b, dims, preferred_element_type=jnp.float32)


def ids_along(shape, axis):
    return lax.broadcasted_iota(jnp.int32, shape, axis)


def aligned(index, size):
    return pl.ds(pl.multiple_of(index * size, size), size)


def route_kernel(tokens, cotangent, expert_ids, route_weights, packet, ids, values, sems):
    rows, width = tokens.shape
    lanes = packet.shape[1] - 2 * width
    copies = [
        pltpu.make_async_copy(expert_ids, ids, sems.at[0]),
        pltpu.make_async_copy(route_weights, values, sems.at[1]),
        pltpu.make_async_copy(tokens, packet.at[:, :width], sems.at[2]),
        pltpu.make_async_copy(cotangent, packet.at[:, width : 2 * width], sems.at[3]),
    ]
    for copy in copies:
        copy.start()
    for copy in copies:
        copy.wait()
    at = ids_along((lanes, rows), 0)
    weights = values[...].astype(jnp.float32)
    dense = jnp.zeros((lanes, rows), jnp.float32)
    for k in range(ids.shape[0]):
        dense += jnp.where(ids[k : k + 1, :] == at, weights[k : k + 1, :], 0.0)
    packet[:, 2 * width :] = dense.T.astype(packet.dtype)


def load_kernel(source, value, target, same, sem):
    copy = pltpu.make_async_copy(source, target, sem)
    copy.start()
    same[...] = value[...]
    copy.wait()


def over_tiles(tokens, body):
    if tokens == TILE:
        body(slice(0, TILE))
    else:

        def turn(tile, carry):
            body(aligned(tile, TILE))
            return carry

        lax.fori_loop(0, tokens // TILE, turn, 0)


def gate_up_kernel(x, masks, gate, up, value, hidden, slope_up, slope_gate, same):
    local_experts, _, hidden_units = gate.shape
    bf16 = jnp.bfloat16
    same[...] = value[...]

    def tile(rows):
        for expert in range(local_experts):
            for start in range(0, hidden_units, CHUNK):
                cols = slice(start, start + CHUNK)
                gate_pre = dot(x[rows, :], gate[expert, :, cols], NN)
                up_proj = dot(x[rows, :], up[expert, :, cols], NN)
                at = ids_along((1, CHUNK), 1)
                keep = jnp.zeros((1, CHUNK), jnp.float32)
                for j in range(CHUNK // BLK):
                    kept = masks[expert, start // BLK + j].astype(jnp.float32)
                    keep = jnp.where(at // BLK == j, kept, keep)
                sigma = 0.5 + 0.5 * jnp.tanh(0.5 * gate_pre)
                silu = gate_pre * sigma
                up_kept = up_proj * keep
                hidden[expert, rows, cols] = (silu * up_kept).astype(bf16)
                slope_up[expert, rows, cols] = (silu * keep).astype(bf16)
                slope = up_kept * (sigma + silu * (1.0 - sigma))
                slope_gate[expert, rows, cols] = slope.astype(bf16)

    over_tiles(x.shape[0], tile)


def stack(pieces, target, cols=slice(None)):
    rows = pieces[0].shape[0]
    for i, piece in enumerate(pieces):
        target[i * rows : (i + 1) * rows] = piece[:, cols]


def hidden_kernel(count, blocks, *refs):
    pieces, refs = refs[:count], refs[count:]
    units, slope_up, slope_gate, gate, up, w_down, hidden, d_gate, d_up = refs[:9]
    outs, refs = refs[9 : 9 + blocks], refs[9 + blocks :]
    packet, inner, mixed, token_grad, down_buf, sems = refs
    local_experts, hidden_units, width = w_down.shape
    tokens, part = mixed.shape
    lanes = packet.shape[1] - width
    half = lanes // 2
    base = lax.axis_index("expert") * local_experts
    mine = aligned(lax.axis_index("dp"), part)
    bf16, f32 = jnp.bfloat16, jnp.float32

    def copies(expert):
        return [
            pltpu.make_async_copy(
                w_down.at[expert, slice(start, start + CHUNK), :],
                down_buf.at[expert % 2, slice(start, start + CHUNK), :],
                sems.at[expert % 2, start // CHUNK],
            )
            for start in range(0, hidden_units, CHUNK)
        ]

    for copy in copies(0):
        copy.start()
    stack(pieces, packet)
    for expert in range(local_experts):
        if expert + 1 < local_experts:
            for copy in copies(expert + 1):
                copy.start()
        down = down_buf.at[expert % 2]
        for copy in copies(expert):
            copy.wait()

        def tile(rows, expert=expert, down=down):
            dense = packet[rows, width:].astype(f32)
            at = ids_along((TILE, lanes), 1)
            hit = at == base + expert
            weights = jnp.sum(jnp.where(hit, dense, 0.0), axis=1, keepdims=True)
            total = jnp.zeros((TILE, 1), f32)
            for start in range(0, hidden_units, CHUNK):
                cols = slice(start, start + CHUNK)
                back = dot(packet[rows, :width], down[cols, :], NT)
                part_units = units[expert, rows, cols].astype(f32)
                total += jnp.sum(part_units * back, axis=1, keepdims=True)
                back = back * weights
                hidden[expert, rows, cols] = (part_units * weights).astype(bf16)
                d_gate[expert, rows, cols] = (back * slope_gate[expert, rows, cols].astype(f32)).astype(bf16)
                d_up[expert, rows, cols] = (back * slope_up[expert, rows, cols].astype(f32)).astype(bf16)
            high = total.astype(bf16).astype(f32)
            both = jnp.where(hit, high, jnp.where(at == base + expert + half, total - high, 0.0))
            new_mixed = dot(hidden[expert, rows, :], down[:, mine], NN)
            new_grad = dot(d_gate[expert, rows, :], gate[expert, mine, :], NT) + dot(
                d_up[expert, rows, :], up[expert, mine, :], NT
            )
            if expert == 0:
                inner[rows, :] = both
                mixed[rows, :] = new_mixed
                token_grad[rows, :] = new_grad
            else:
                inner[rows, :] += both
                mixed[rows, :] += new_mixed
                token_grad[rows, :] += new_grad

        over_tiles(tokens, tile)

    rows = outs[0].shape[0]
    for i, out in enumerate(outs):
        block = slice(i * rows, (i + 1) * rows)
        out[:, :part] = mixed[block].astype(bf16)
        out[:, part : 2 * part] = token_grad[block].astype(bf16)
        out[:, 2 * part :] = inner[block].astype(bf16)


def write_out(steps, place, outs, bufs, sems, body):
    def copies(step, slot):
        return [
            pltpu.make_async_copy(buf.at[slot], out.at[place(step)], sems.at[slot, i])
            for i, (out, buf) in enumerate(zip(outs, bufs))
        ]

    def turn(step, carry):
        slot = lax.rem(step, 2)

        @pl.when(step >= 2)
        def _():
            for copy in copies(step - 2, slot):
                copy.wait()

        body(step, slot)
        for copy in copies(step, slot):
            copy.start()
        return carry

    lax.fori_loop(0, steps, turn, 0)
    for step in range(max(steps - 2, 0), steps):
        for copy in copies(step, step % 2):
            copy.wait()


def grad_in_kernel(x, d_gate, d_up, grad_gate, grad_up, done, x_part, out_gate, out_up, sems):
    local_experts, _, hidden_units = d_gate.shape
    part, rows = x_part.shape[0], out_gate.shape[1]
    x_part[...] = x[:, aligned(lax.axis_index("dp"), part)].T
    done[...] = jnp.zeros(done.shape, done.dtype)
    blocks = part // rows

    def place(step):
        return step // blocks, aligned(lax.rem(step, blocks), rows), slice(None)

    def body(step, slot):
        expert, block, _ = place(step)
        out_gate[slot] = dot(x_part[block, :], d_gate[expert], NN)
        out_up[slot] = dot(x_part[block, :], d_up[expert], NN)

    write_out(
        local_experts * blocks, place, (grad_gate, grad_up), (out_gate, out_up), sems, body
    )


def grad_out_kernel(count, *refs):
    pieces, refs = refs[:count], refs[count:]
    hidden, after, grad_down, done, cot_part, out_down, sems = refs
    local_experts = hidden.shape[0]
    part = cot_part.shape[1]
    stack(pieces, cot_part, aligned(lax.axis_index("dp"), part))
    done[...] = jnp.zeros(done.shape, done.dtype)

    def place(step):
        return (step,)

    def body(step, slot):
        out_down[slot] = dot(hidden[step].T, cot_part[...], NN)

    write_out(local_experts, place, (grad_down,), (out_down,), sems, body)


def reduce_kernel(count, *refs):
    blocks, refs = refs[:count], refs[count:]
    expert_ids, after, route_grad = refs[:3]
    outs, done = refs[3:-1], refs[-1]
    done[...] = jnp.zeros(done.shape, done.dtype)
    rows, both = outs[0].shape
    half = (blocks[0].shape[1] - both) // 2
    for j, out in enumerate(outs):
        total = jnp.zeros((rows, both), jnp.float32)
        for block in blocks:
            total += block[j * rows : (j + 1) * rows, :both].astype(jnp.float32)
        out[...] = total.astype(out.dtype)
    inner = jnp.zeros((rows, 2 * half), jnp.float32)
    for block in blocks:
        inner += block[:rows, both:].astype(jnp.float32)
    inner = inner.T
    inner = inner[:half] + inner[half:]
    at = ids_along(inner.shape, 0)
    for k in range(expert_ids.shape[0]):
        hit = jnp.where(expert_ids[k : k + 1, :] == at, inner, 0.0)
        route_grad[k : k + 1, :] = jnp.sum(hit, axis=0, keepdims=True)


def join_kernel(count, *refs):
    blocks, (after, mixed, token_grad) = refs[:count], refs[count:]
    part = blocks[0].shape[1] // 2
    column = lax.axis_index("dp")
    for other, block in enumerate(blocks):
        cols = aligned(column ^ other, part)
        mixed[:, cols] = block[:, :part]
        token_grad[:, cols] = block[:, part:]


def swap(value, axis, mask):
    size = lax.axis_size(axis)
    return lax.ppermute(value, axis, [(i, i ^ mask) for i in range(size)])


def exchange(value, axis, masks):
    return [swap(value, axis, mask) for mask in masks]


def in_hbm(array):
    return pltpu.with_memory_space_constraint(array, pltpu.HBM)


def in_vmem(array):
    return pltpu.with_memory_space_constraint(array, pltpu.VMEM)


def cost(flops, moved):
    return pl.CostEstimate(flops=flops, bytes_accessed=moved, transcendentals=0)


def params(mib):
    return pltpu.CompilerParams(vmem_limit_bytes=mib * MIB)


def per_device(
    tokens, expert_ids, slot_index, route_weights, w_gate, w_up, w_down, block_masks, cotangent
):
    rows, width = tokens.shape
    local_experts, _, hidden_units = w_gate.shape
    sources, columns = lax.axis_size("expert"), lax.axis_size("dp")
    chips = list(range(2, sources, 2))
    expert_order = [0] + chips + [chip ^ 1 for chip in [0] + chips]
    lanes = -(-2 * local_experts * sources // LANES) * LANES
    part = width // columns
    everyone = sources * columns * rows
    bf16, f32 = jnp.bfloat16, jnp.float32
    struct = jax.ShapeDtypeStruct
    one = 2 * local_experts * width * hidden_units
    dummy = struct((8, LANES), f32)
    ids_t = expert_ids.T
    w_gate, w_up, w_down = [in_hbm(w) for w in (w_gate, w_up, w_down)]

    packet = pl.pallas_call(
        route_kernel,
        out_shape=struct((rows, 2 * width + lanes), bf16),
        in_specs=[HBM] * 4,
        out_specs=VMEM,
        scratch_shapes=[
            pltpu.VMEM(ids_t.shape, jnp.int32),
            pltpu.VMEM(ids_t.shape, bf16),
            pltpu.SemaphoreType.DMA((4,)),
        ],
        compiler_params=params(2),
        name="route",
    )(*[in_hbm(a) for a in (tokens, cotangent, ids_t, route_weights.T)])

    def load(weight, value, name):
        return pl.pallas_call(
            load_kernel,
            out_shape=[
                pltpu.VMEM(weight.shape, weight.dtype),
                struct(value.shape, value.dtype),
            ],
            in_specs=[HBM, VMEM],
            out_specs=[VMEM] * 2,
            scratch_shapes=[pltpu.SemaphoreType.DMA],
            cost_estimate=cost(0, one),
            compiler_params=params(1),
            name=name,
        )(weight, value)

    arrived = exchange(packet, "dp", range(1, columns))
    gate, packet = load(w_gate, packet, "load_gate")
    x_column = jnp.concatenate([p[:, :width] for p in [packet] + arrived])
    c_column = jnp.concatenate([p[:, width:] for p in [packet] + arrived])
    x_across = exchange(x_column, "expert", chips)
    c_across = exchange(c_column, "expert", chips)
    up, x_column = load(w_up, x_column, "load_up")
    gate, up = in_vmem(gate), in_vmem(up)
    x = jnp.concatenate([x_column] + x_across)
    x = jnp.concatenate([x, swap(x, "expert", 1)])

    units = struct((local_experts, everyone, hidden_units), bf16)
    *factors, c_column = pl.pallas_call(
        gate_up_kernel,
        out_shape=[units] * 3 + [struct(c_column.shape, bf16)],
        in_specs=[VMEM, SMEM] + [VMEM] * 3,
        out_specs=[VMEM] * 4,
        cost_estimate=cost(2 * everyone * one, 2 * one),
        compiler_params=params(6),
        name="gate_up",
    )(x, block_masks, gate, up, c_column)
    c_half = jnp.concatenate([c_column] + c_across)
    pieces = [c_half, swap(c_half, "expert", 1)]

    hidden, d_gate, d_up, *partials = pl.pallas_call(
        functools.partial(hidden_kernel, 2, sources),
        out_shape=[units] * 3
        + [struct((columns * rows, 2 * part + lanes), bf16)] * sources,
        in_specs=[VMEM] * 7 + [HBM],
        out_specs=[VMEM] * (3 + sources),
        scratch_shapes=[
            pltpu.VMEM((everyone, width + lanes), bf16),
            pltpu.VMEM((everyone, lanes), f32),
            pltpu.VMEM((everyone, part), f32),
            pltpu.VMEM((everyone, part), f32),
            pltpu.VMEM((min(2, local_experts), hidden_units, width), bf16),
            pltpu.SemaphoreType.DMA((2, hidden_units // CHUNK)),
        ],
        cost_estimate=cost(2 * everyone * one, 2 * one),
        compiler_params=params(12 + (everyone - TILE) * (2 * part + lanes) * 14 // MIB),
        name="hidden",
    )(*pieces, *factors, gate, up, w_down)
    arrived = [
        swap(partial, "expert", other) if other else partial
        for other, partial in zip(expert_order, partials)
    ]

    grad_gate, grad_up, done_in = pl.pallas_call(
        grad_in_kernel,
        out_shape=[struct((local_experts, part, hidden_units), f32)] * 2 + [dummy],
        in_specs=[VMEM] * 3,
        out_specs=[HBM] * 2 + [VMEM],
        scratch_shapes=[
            pltpu.VMEM((part, everyone), bf16),
            pltpu.VMEM((2, min(part, CHUNK), hidden_units), f32),
            pltpu.VMEM((2, min(part, CHUNK), hidden_units), f32),
            pltpu.SemaphoreType.DMA((2, 2)),
        ],
        cost_estimate=cost(2 * everyone * one // columns, 4 * one // columns),
        compiler_params=params(16),
        name="grad_in",
    )(x, d_gate, d_up)

    route_grad, *blocks, done_sum = pl.pallas_call(
        functools.partial(reduce_kernel, sources),
        out_shape=[struct(ids_t.shape, f32)] + [struct((rows, 2 * part), bf16)] * columns + [dummy],
        in_specs=[VMEM] * (sources + 2),
        out_specs=[VMEM] * (columns + 2),
        compiler_params=params(4),
        name="reduce",
    )(*arrived, ids_t, done_in)
    blocks = [
        swap(block, "dp", other) if other else block for other, block in enumerate(blocks)
    ]

    grad_down, done_out = pl.pallas_call(
        functools.partial(grad_out_kernel, 2),
        out_shape=[struct((local_experts, hidden_units, part), f32), dummy],
        in_specs=[VMEM] * 4,
        out_specs=[HBM, VMEM],
        scratch_shapes=[
            pltpu.VMEM((everyone, part), bf16),
            pltpu.VMEM((2, hidden_units, part), f32),
            pltpu.SemaphoreType.DMA((2, 1)),
        ],
        cost_estimate=cost(everyone * one // columns, 2 * one // columns),
        compiler_params=params(16),
        name="grad_out",
    )(*pieces, hidden, done_sum)

    mixed, token_grad = pl.pallas_call(
        functools.partial(join_kernel, columns),
        out_shape=[struct((rows, width), bf16)] * 2,
        in_specs=[VMEM] * (columns + 1),
        out_specs=[VMEM] * 2,
        compiler_params=params(4),
        name="join",
    )(*blocks, done_out)
    return (mixed, token_grad, route_grad.T, grad_gate, grad_up, grad_down)


def solution(mesh):
    rows = P(("groups", "expert", "dp"), None)
    experts = P("expert", None, None)
    return jax.shard_map(
        per_device,
        mesh=mesh,
        in_specs=(rows, rows, rows, rows, experts, experts, experts, P("expert", None), rows),
        out_specs=(
            rows,
            rows,
            rows,
            P(("groups", "expert"), "dp", None),
            P(("groups", "expert"), "dp", None),
            P(("groups", "expert"), None, "dp"),
        ),
        check_vma=False,
    )
```

```python
import functools

import jax
import jax.numpy as jnp
from jax import lax
from jax.experimental import pallas as pl
from jax.experimental.pallas import tpu as pltpu
from jax.sharding import PartitionSpec as P

BLK = 128
LANES = 128
CHUNK = 256
TILE = 256
MIB = 1 << 20

VMEM = pl.BlockSpec(memory_space=pltpu.VMEM)
SMEM = pl.BlockSpec(memory_space=pltpu.SMEM)
HBM = pl.BlockSpec(memory_space=pltpu.HBM)

NN = (((1,), (0,)), ((), ()))
NT = (((1,), (1,)), ((), ()))


def dot(a, b, dims):
    return lax.dot_general(a, b, dims, preferred_element_type=jnp.float32)


def ids_along(shape, axis):
    return lax.broadcasted_iota(jnp.int32, shape, axis)


def aligned(index, size):
    return pl.ds(pl.multiple_of(index * size, size), size)


def route_kernel(
    tokens, cotangent, expert_ids, route_weights, own_tokens, packet, ids, values, sems
):
    rows, width = tokens.shape
    lanes = packet.shape[1] - width
    copies = [
        pltpu.make_async_copy(expert_ids, ids, sems.at[0]),
        pltpu.make_async_copy(route_weights, values, sems.at[1]),
        pltpu.make_async_copy(tokens, own_tokens, sems.at[2]),
        pltpu.make_async_copy(cotangent, packet.at[:, :width], sems.at[3]),
    ]
    for copy in copies:
        copy.start()
    for copy in copies:
        copy.wait()
    at = ids_along((lanes, rows), 0)
    weights = values[...].astype(jnp.float32)
    dense = jnp.zeros((lanes, rows), jnp.float32)
    for k in range(ids.shape[0]):
        dense += jnp.where(ids[k : k + 1, :] == at, weights[k : k + 1, :], 0.0)
    packet[:, width:] = dense.T.astype(packet.dtype)


def load_kernel(source, value, target, same, sem):
    copy = pltpu.make_async_copy(source, target, sem)
    copy.start()
    same[...] = value[...]
    copy.wait()


def over_tiles(tokens, body):
    if tokens == TILE:
        body(slice(0, TILE))
    else:

        def turn(tile, carry):
            body(aligned(tile, TILE))
            return carry

        lax.fori_loop(0, tokens // TILE, turn, 0)


def gate_up_kernel(
    x, masks, gate, w_up, value, hidden, slope_up, slope_gate, x_part, same, up, sems
):
    local_experts, _, hidden_units = gate.shape
    bf16 = jnp.bfloat16
    loads = [
        pltpu.make_async_copy(w_up.at[e], up.at[e], sems.at[e]) for e in range(local_experts)
    ]
    for load in loads:
        load.start()
    same[...] = value[...]
    x_part[...] = x[:, aligned(lax.axis_index("dp"), x_part.shape[0])].T

    for expert in range(local_experts):
        at = ids_along((1, hidden_units), 1)
        keep = jnp.zeros((1, hidden_units), jnp.float32)
        for j in range(hidden_units // BLK):
            keep = jnp.where(at // BLK == j, masks[expert, j].astype(jnp.float32), keep)

        def tile(rows, expert=expert, keep=keep, wait=True):
            gate_pre = dot(x[rows, :], gate[expert], NN)
            if wait:
                loads[expert].wait()
            up_kept = dot(x[rows, :], up[expert], NN) * keep
            sigma = 0.5 + 0.5 * jnp.tanh(0.5 * gate_pre)
            silu = gate_pre * sigma
            hidden[expert, rows, :] = (silu * up_kept).astype(bf16)
            slope_up[expert, rows, :] = (silu * keep).astype(bf16)
            slope = up_kept * (sigma + silu * (1.0 - sigma))
            slope_gate[expert, rows, :] = slope.astype(bf16)

        if x.shape[0] == TILE:
            tile(slice(0, TILE))
        else:
            loads[expert].wait()
            over_tiles(x.shape[0], functools.partial(tile, wait=False))


def stack(pieces, target, cols=slice(None)):
    rows = pieces[0].shape[0]
    for i, piece in enumerate(pieces):
        target[i * rows : (i + 1) * rows] = piece[:, cols]


def hidden_kernel(count, blocks, *refs):
    pieces, refs = refs[:count], refs[count:]
    units, slope_up, slope_gate, gate, up, w_down, hidden, d_gate, d_up = refs[:9]
    outs, refs = refs[9 : 9 + blocks], refs[9 + blocks :]
    packet, inner, mixed, token_grad, down_buf, sems = refs
    local_experts, hidden_units, width = w_down.shape
    tokens, part = mixed.shape
    lanes = packet.shape[1] - width
    half = lanes // 2
    base = lax.axis_index("expert") * local_experts
    mine = aligned(lax.axis_index("dp"), part)
    bf16, f32 = jnp.bfloat16, jnp.float32

    def copies(expert):
        return [
            pltpu.make_async_copy(
                w_down.at[expert, slice(start, start + CHUNK), :],
                down_buf.at[expert % 2, slice(start, start + CHUNK), :],
                sems.at[expert % 2, start // CHUNK],
            )
            for start in range(0, hidden_units, CHUNK)
        ]

    for copy in copies(0):
        copy.start()
    stack(pieces, packet)
    for expert in range(local_experts):
        if expert + 1 < local_experts:
            for copy in copies(expert + 1):
                copy.start()
        down = down_buf.at[expert % 2]
        for copy in copies(expert):
            copy.wait()

        def tile(rows, expert=expert, down=down):
            dense = packet[rows, width:].astype(f32)
            at = ids_along((TILE, lanes), 1)
            hit = at == base + expert
            weights = jnp.sum(jnp.where(hit, dense, 0.0), axis=1, keepdims=True)
            back = dot(packet[rows, :width], down[...], NT)
            part_units = units[expert, rows, :].astype(f32)
            total = jnp.sum(part_units * back, axis=1, keepdims=True)
            back = back * weights
            new_hidden = (part_units * weights).astype(bf16)
            new_gate = (back * slope_gate[expert, rows, :].astype(f32)).astype(bf16)
            new_up = (back * slope_up[expert, rows, :].astype(f32)).astype(bf16)
            hidden[expert, rows, :] = new_hidden
            d_gate[expert, rows, :] = new_gate
            d_up[expert, rows, :] = new_up
            high = total.astype(bf16).astype(f32)
            both = jnp.where(hit, high, jnp.where(at == base + expert + half, total - high, 0.0))
            new_mixed = dot(new_hidden, down[:, mine], NN)
            new_grad = dot(new_gate, gate[expert, mine, :], NT) + dot(
                new_up, up[expert, mine, :], NT
            )
            if expert == 0:
                inner[rows, :] = both
                mixed[rows, :] = new_mixed
                token_grad[rows, :] = new_grad
            else:
                inner[rows, :] += both
                mixed[rows, :] += new_mixed
                token_grad[rows, :] += new_grad

        over_tiles(tokens, tile)

    rows = outs[0].shape[0]
    for i, out in enumerate(outs):
        block = slice(i * rows, (i + 1) * rows)
        out[:, :part] = mixed[block].astype(bf16)
        out[:, part : 2 * part] = token_grad[block].astype(bf16)
        out[:, 2 * part :] = inner[block].astype(bf16)


def write_out(steps, place, outs, bufs, sems, body):
    def copies(step, slot):
        return [
            pltpu.make_async_copy(buf.at[slot], out.at[place(step)], sems.at[slot, i])
            for i, (out, buf) in enumerate(zip(outs, bufs))
        ]

    def turn(step, carry):
        slot = lax.rem(step, 2)

        @pl.when(step >= 2)
        def _():
            for copy in copies(step - 2, slot):
                copy.wait()

        body(step, slot)
        for copy in copies(step, slot):
            copy.start()
        return carry

    lax.fori_loop(0, steps, turn, 0)
    for step in range(max(steps - 2, 0), steps):
        for copy in copies(step, step % 2):
            copy.wait()


def grad_in_kernel(x_part, d_gate, d_up, grad_gate, grad_up, done, out_gate, out_up, sems):
    local_experts = d_gate.shape[0]
    part, rows = x_part.shape[0], out_gate.shape[1]
    done[...] = jnp.zeros(done.shape, done.dtype)
    blocks = part // rows

    def place(step):
        return step // blocks, aligned(lax.rem(step, blocks), rows), slice(None)

    def body(step, slot):
        expert, block, _ = place(step)
        out_gate[slot] = dot(x_part[block, :], d_gate[expert], NN)
        out_up[slot] = dot(x_part[block, :], d_up[expert], NN)

    write_out(
        local_experts * blocks, place, (grad_gate, grad_up), (out_gate, out_up), sems, body
    )


def grad_out_kernel(count, *refs):
    pieces, refs = refs[:count], refs[count:]
    hidden, after, grad_down, done, cot_part, out_down, sems = refs
    local_experts = hidden.shape[0]
    part = cot_part.shape[1]
    stack(pieces, cot_part, aligned(lax.axis_index("dp"), part))
    done[...] = jnp.zeros(done.shape, done.dtype)

    def place(step):
        return (step,)

    def body(step, slot):
        out_down[slot] = dot(hidden[step].T, cot_part[...], NN)

    write_out(local_experts, place, (grad_down,), (out_down,), sems, body)


def reduce_kernel(count, *refs):
    blocks, refs = refs[:count], refs[count:]
    expert_ids, after, route_grad = refs[:3]
    outs, done = refs[3:-1], refs[-1]
    done[...] = jnp.zeros(done.shape, done.dtype)
    rows, both = outs[0].shape
    half = (blocks[0].shape[1] - both) // 2
    for j, out in enumerate(outs):
        total = jnp.zeros((rows, both), jnp.float32)
        for block in blocks:
            total += block[j * rows : (j + 1) * rows, :both].astype(jnp.float32)
        out[...] = total.astype(out.dtype)
    inner = jnp.zeros((rows, 2 * half), jnp.float32)
    for block in blocks:
        inner += block[:rows, both:].astype(jnp.float32)
    inner = inner.T
    inner = inner[:half] + inner[half:]
    at = ids_along(inner.shape, 0)
    for k in range(expert_ids.shape[0]):
        hit = jnp.where(expert_ids[k : k + 1, :] == at, inner, 0.0)
        route_grad[k : k + 1, :] = jnp.sum(hit, axis=0, keepdims=True)


def join_kernel(count, *refs):
    blocks, (after, mixed, token_grad) = refs[:count], refs[count:]
    part = blocks[0].shape[1] // 2
    column = lax.axis_index("dp")
    for other, block in enumerate(blocks):
        cols = aligned(column ^ other, part)
        mixed[:, cols] = block[:, :part]
        token_grad[:, cols] = block[:, part:]


def swap(value, axis, mask):
    size = lax.axis_size(axis)
    return lax.ppermute(value, axis, [(i, i ^ mask) for i in range(size)])


def exchange(value, axis, masks):
    return [swap(value, axis, mask) for mask in masks]


def in_hbm(array):
    return pltpu.with_memory_space_constraint(array, pltpu.HBM)


def in_vmem(array):
    return pltpu.with_memory_space_constraint(array, pltpu.VMEM)


def cost(flops, moved):
    return pl.CostEstimate(flops=flops, bytes_accessed=moved, transcendentals=0)


def params(mib):
    return pltpu.CompilerParams(vmem_limit_bytes=mib * MIB)


def per_device(
    tokens, expert_ids, slot_index, route_weights, w_gate, w_up, w_down, block_masks, cotangent
):
    rows, width = tokens.shape
    local_experts, _, hidden_units = w_gate.shape
    sources, columns = lax.axis_size("expert"), lax.axis_size("dp")
    chips = list(range(2, sources, 2))
    expert_order = [0] + chips + [chip ^ 1 for chip in [0] + chips]
    lanes = -(-2 * local_experts * sources // LANES) * LANES
    part = width // columns
    everyone = sources * columns * rows
    bf16, f32 = jnp.bfloat16, jnp.float32
    struct = jax.ShapeDtypeStruct
    one = 2 * local_experts * width * hidden_units
    dummy = struct((8, LANES), f32)
    ids_t = expert_ids.T
    w_gate, w_up, w_down = [in_hbm(w) for w in (w_gate, w_up, w_down)]

    own_tokens, packet = pl.pallas_call(
        route_kernel,
        out_shape=[struct(tokens.shape, bf16), struct((rows, width + lanes), bf16)],
        in_specs=[HBM] * 4,
        out_specs=[VMEM] * 2,
        scratch_shapes=[
            pltpu.VMEM(ids_t.shape, jnp.int32),
            pltpu.VMEM(ids_t.shape, bf16),
            pltpu.SemaphoreType.DMA((4,)),
        ],
        compiler_params=params(2),
        name="route",
    )(*[in_hbm(a) for a in (tokens, cotangent, ids_t, route_weights.T)])

    def load(weight, value, name):
        return pl.pallas_call(
            load_kernel,
            out_shape=[
                pltpu.VMEM(weight.shape, weight.dtype),
                struct(value.shape, value.dtype),
            ],
            in_specs=[HBM, VMEM],
            out_specs=[VMEM] * 2,
            scratch_shapes=[pltpu.SemaphoreType.DMA],
            cost_estimate=cost(0, one),
            compiler_params=params(1),
            name=name,
        )(weight, value)

    x_column = jnp.concatenate([own_tokens] + exchange(own_tokens, "dp", range(1, columns)))
    c_column = jnp.concatenate([packet] + exchange(packet, "dp", range(1, columns)))
    x_across = exchange(x_column, "expert", chips)
    c_across = exchange(c_column, "expert", chips)
    gate, x_column = load(w_gate, x_column, "load_gate")
    gate = in_vmem(gate)
    x = jnp.concatenate([x_column] + x_across)
    x = jnp.concatenate([x, swap(x, "expert", 1)])

    units = struct((local_experts, everyone, hidden_units), bf16)
    *factors, x_part, c_column, up = pl.pallas_call(
        gate_up_kernel,
        out_shape=[units] * 3
        + [struct((part, everyone), bf16), struct(c_column.shape, bf16)]
        + [pltpu.VMEM(w_up.shape, bf16)],
        in_specs=[VMEM, SMEM, VMEM, HBM, VMEM],
        out_specs=[VMEM] * 6,
        scratch_shapes=[pltpu.SemaphoreType.DMA((local_experts,))],
        cost_estimate=cost(2 * everyone * one, 2 * one),
        compiler_params=params(6),
        name="gate_up",
    )(x, block_masks, gate, w_up, c_column)
    up = in_vmem(up)
    c_half = jnp.concatenate([c_column] + c_across)
    pieces = [c_half, swap(c_half, "expert", 1)]

    hidden, d_gate, d_up, *partials = pl.pallas_call(
        functools.partial(hidden_kernel, 2, sources),
        out_shape=[units] * 3
        + [struct((columns * rows, 2 * part + lanes), bf16)] * sources,
        in_specs=[VMEM] * 7 + [HBM],
        out_specs=[VMEM] * (3 + sources),
        scratch_shapes=[
            pltpu.VMEM((everyone, width + lanes), bf16),
            pltpu.VMEM((everyone, lanes), f32),
            pltpu.VMEM((everyone, part), f32),
            pltpu.VMEM((everyone, part), f32),
            pltpu.VMEM((min(2, local_experts), hidden_units, width), bf16),
            pltpu.SemaphoreType.DMA((2, hidden_units // CHUNK)),
        ],
        cost_estimate=cost(2 * everyone * one, 2 * one),
        compiler_params=params(12 + (everyone - TILE) * (2 * part + lanes) * 14 // MIB),
        name="hidden",
    )(*pieces, *factors, gate, up, w_down)
    arrived = [
        swap(partial, "expert", other) if other else partial
        for other, partial in zip(expert_order, partials)
    ]

    grad_gate, grad_up, done_in = pl.pallas_call(
        grad_in_kernel,
        out_shape=[struct((local_experts, part, hidden_units), f32)] * 2 + [dummy],
        in_specs=[VMEM] * 3,
        out_specs=[HBM] * 2 + [VMEM],
        scratch_shapes=[
            pltpu.VMEM((2, min(part, CHUNK), hidden_units), f32),
            pltpu.VMEM((2, min(part, CHUNK), hidden_units), f32),
            pltpu.SemaphoreType.DMA((2, 2)),
        ],
        cost_estimate=cost(2 * everyone * one // columns, 4 * one // columns),
        compiler_params=params(16),
        name="grad_in",
    )(x_part, d_gate, d_up)

    route_grad, *blocks, done_sum = pl.pallas_call(
        functools.partial(reduce_kernel, sources),
        out_shape=[struct(ids_t.shape, f32)] + [struct((rows, 2 * part), bf16)] * columns + [dummy],
        in_specs=[VMEM] * (sources + 2),
        out_specs=[VMEM] * (columns + 2),
        compiler_params=params(4),
        name="reduce",
    )(*arrived, ids_t, done_in)
    blocks = [
        swap(block, "dp", other) if other else block for other, block in enumerate(blocks)
    ]

    grad_down, done_out = pl.pallas_call(
        functools.partial(grad_out_kernel, 2),
        out_shape=[struct((local_experts, hidden_units, part), f32), dummy],
        in_specs=[VMEM] * 4,
        out_specs=[HBM, VMEM],
        scratch_shapes=[
            pltpu.VMEM((everyone, part), bf16),
            pltpu.VMEM((2, hidden_units, part), f32),
            pltpu.SemaphoreType.DMA((2, 1)),
        ],
        cost_estimate=cost(everyone * one // columns, 2 * one // columns),
        compiler_params=params(16),
        name="grad_out",
    )(*pieces, hidden, done_sum)

    mixed, token_grad = pl.pallas_call(
        functools.partial(join_kernel, columns),
        out_shape=[struct((rows, width), bf16)] * 2,
        in_specs=[VMEM] * (columns + 1),
        out_specs=[VMEM] * 2,
        compiler_params=params(4),
        name="join",
    )(*blocks, done_out)
    return (mixed, token_grad, route_grad.T, grad_gate, grad_up, grad_down)


def solution(mesh):
    rows = P(("groups", "expert", "dp"), None)
    experts = P("expert", None, None)
    return jax.shard_map(
        per_device,
        mesh=mesh,
        in_specs=(rows, rows, rows, rows, experts, experts, experts, P("expert", None), rows),
        out_specs=(
            rows,
            rows,
            rows,
            P(("groups", "expert"), "dp", None),
            P(("groups", "expert"), "dp", None),
            P(("groups", "expert"), None, "dp"),
        ),
        check_vma=False,
    )
```

```python
import functools

import jax
import jax.numpy as jnp
from jax import lax
from jax.experimental import pallas as pl
from jax.experimental.pallas import tpu as pltpu
from jax.sharding import PartitionSpec as P

BLK = 128
LANES = 128
CHUNK = 256
TILE = 256
MIB = 1 << 20

VMEM = pl.BlockSpec(memory_space=pltpu.VMEM)
SMEM = pl.BlockSpec(memory_space=pltpu.SMEM)
HBM = pl.BlockSpec(memory_space=pltpu.HBM)

NN = (((1,), (0,)), ((), ()))
NT = (((1,), (1,)), ((), ()))


def dot(a, b, dims):
    return lax.dot_general(a, b, dims, preferred_element_type=jnp.float32)


def ids_along(shape, axis):
    return lax.broadcasted_iota(jnp.int32, shape, axis)


def aligned(index, size):
    return pl.ds(pl.multiple_of(index * size, size), size)


def route_kernel(cotangent, expert_ids, route_weights, value, packet, same, ids, values, sems):
    rows, width = cotangent.shape
    lanes = packet.shape[1] - width
    copies = [
        pltpu.make_async_copy(expert_ids, ids, sems.at[0]),
        pltpu.make_async_copy(route_weights, values, sems.at[1]),
        pltpu.make_async_copy(cotangent, packet.at[:, :width], sems.at[2]),
    ]
    for copy in copies:
        copy.start()
    same[...] = value[...]
    for copy in copies:
        copy.wait()
    at = ids_along((lanes, rows), 0)
    weights = values[...].astype(jnp.float32)
    dense = jnp.zeros((lanes, rows), jnp.float32)
    for k in range(ids.shape[0]):
        dense += jnp.where(ids[k : k + 1, :] == at, weights[k : k + 1, :], 0.0)
    packet[:, width:] = dense.T.astype(packet.dtype)


def load_kernel(weight, tokens, target, own_tokens, sems):
    copies = [
        pltpu.make_async_copy(tokens, own_tokens, sems.at[0]),
        pltpu.make_async_copy(weight, target, sems.at[1]),
    ]
    for copy in copies:
        copy.start()
    for copy in copies:
        copy.wait()


def turn_kernel(x, after, x_part):
    x_part[...] = x[:, aligned(lax.axis_index("dp"), x_part.shape[0])].T


def over_tiles(tokens, body):
    if tokens == TILE:
        body(slice(0, TILE))
    else:

        def turn(tile, carry):
            body(aligned(tile, TILE))
            return carry

        lax.fori_loop(0, tokens // TILE, turn, 0)


def gate_up_kernel(first, last, *refs):
    x, masks, gate, w_up, value = refs[:5]
    hidden, slope_up, slope_gate, same, up_buf, sems = refs[-6:]
    hidden_units = gate.shape[2]
    bf16 = jnp.bfloat16
    loads = [
        pltpu.make_async_copy(w_up.at[e], up_buf.at[(e - first) % 2], sems.at[(e - first) % 2])
        for e in range(first, last)
    ]
    for load in loads[:2]:
        load.start()
    same[...] = value[...]

    for expert in range(first, last):
        up = up_buf.at[(expert - first) % 2]
        loads[expert - first].wait()

        def tile(rows, expert=expert, up=up):
            for start in range(0, hidden_units, CHUNK):
                cols = slice(start, start + CHUNK)
                gate_pre = dot(x[rows, :], gate[expert, :, cols], NN)
                up_proj = dot(x[rows, :], up[:, cols], NN)
                at = ids_along((1, CHUNK), 1)
                keep = jnp.zeros((1, CHUNK), jnp.float32)
                for j in range(CHUNK // BLK):
                    kept = masks[expert, start // BLK + j].astype(jnp.float32)
                    keep = jnp.where(at // BLK == j, kept, keep)
                sigma = 0.5 + 0.5 * jnp.tanh(0.5 * gate_pre)
                silu = gate_pre * sigma
                up_kept = up_proj * keep
                hidden[expert, rows, cols] = (silu * up_kept).astype(bf16)
                slope_up[expert, rows, cols] = (silu * keep).astype(bf16)
                slope = up_kept * (sigma + silu * (1.0 - sigma))
                slope_gate[expert, rows, cols] = slope.astype(bf16)

        over_tiles(x.shape[0], tile)
        if expert + 2 < last:
            loads[expert + 2 - first].start()


def hidden_kernel(count, *refs):
    packet, units, slope_up, slope_gate, w_gate, w_up, w_down, hidden, d_gate, d_up = refs[:10]
    outs, refs = refs[10 : 10 + count], refs[10 + count :]
    inner, mixed, token_grad, down_buf, gate_buf, up_buf, sems = refs
    local_experts, hidden_units, width = w_down.shape
    tokens, part = mixed.shape
    lanes = packet.shape[1] - width
    half = lanes // 2
    base = lax.axis_index("expert") * local_experts
    mine = aligned(lax.axis_index("dp"), part)
    bf16, f32 = jnp.bfloat16, jnp.float32

    def copies(expert):
        slot = lax.rem(expert, 2)
        return [
            pltpu.make_async_copy(
                w_down.at[expert, slice(i * CHUNK, (i + 1) * CHUNK), :],
                down_buf.at[slot, slice(i * CHUNK, (i + 1) * CHUNK), :],
                sems.at[slot, 2 + i],
            )
            for i in range(hidden_units // CHUNK)
        ] + [
            pltpu.make_async_copy(w_gate.at[expert, mine, :], gate_buf.at[slot], sems.at[slot, 0]),
            pltpu.make_async_copy(w_up.at[expert, mine, :], up_buf.at[slot], sems.at[slot, 1]),
        ]

    for copy in copies(0):
        copy.start()
    inner[...] = jnp.zeros(inner.shape, inner.dtype)
    mixed[...] = jnp.zeros(mixed.shape, mixed.dtype)
    token_grad[...] = jnp.zeros(token_grad.shape, token_grad.dtype)

    def one_expert(expert, carry):
        @pl.when(expert + 1 < local_experts)
        def _():
            for copy in copies(expert + 1):
                copy.start()

        slot = lax.rem(expert, 2)
        down, gate, up = down_buf.at[slot], gate_buf.at[slot], up_buf.at[slot]
        arriving = copies(expert)
        if tokens != TILE:
            for copy in arriving:
                copy.wait()

        def tile(rows):
            dense = packet[rows, width:].astype(f32)
            at = ids_along((TILE, lanes), 1)
            hit = at == base + expert
            weights = jnp.sum(jnp.where(hit, dense, 0.0), axis=1, keepdims=True)
            total = jnp.zeros((TILE, 1), f32)
            for start in range(0, hidden_units, CHUNK):
                cols = slice(start, start + CHUNK)
                if tokens == TILE:
                    arriving[start // CHUNK].wait()
                back = dot(packet[rows, :width], down[cols, :], NT)
                part_units = units[expert, rows, cols].astype(f32)
                total += jnp.sum(part_units * back, axis=1, keepdims=True)
                back = back * weights
                new_gate = back * slope_gate[expert, rows, cols].astype(f32)
                new_up = back * slope_up[expert, rows, cols].astype(f32)
                hidden[expert, rows, cols] = (part_units * weights).astype(bf16)
                d_gate[expert, rows, cols] = new_gate.astype(bf16)
                d_up[expert, rows, cols] = new_up.astype(bf16)
            high = total.astype(bf16).astype(f32)
            inner[rows, :] += jnp.where(
                hit, high, jnp.where(at == base + expert + half, total - high, 0.0)
            )
            if tokens == TILE:
                for copy in arriving[-2:]:
                    copy.wait()
            mixed[rows, :] += dot(hidden[expert, rows, :], down[:, mine], NN)
            token_grad[rows, :] += dot(d_gate[expert, rows, :], gate[...], NT) + dot(
                d_up[expert, rows, :], up[...], NT
            )

        over_tiles(tokens, tile)
        return carry

    lax.fori_loop(0, local_experts, one_expert, 0)
    rows = outs[0].shape[0]
    for i, out in enumerate(outs):
        block = slice(i * rows, (i + 1) * rows)
        out[:, :part] = mixed[block].astype(bf16)
        out[:, part : 2 * part] = token_grad[block].astype(bf16)
        out[:, 2 * part :] = inner[block].astype(bf16)


def write_out(steps, place, outs, bufs, sems, body):
    def copies(step, slot):
        return [
            pltpu.make_async_copy(buf.at[slot], out.at[place(step)], sems.at[slot, i])
            for i, (out, buf) in enumerate(zip(outs, bufs))
        ]

    def turn(step, carry):
        slot = lax.rem(step, 2)

        @pl.when(step >= 2)
        def _():
            for copy in copies(step - 2, slot):
                copy.wait()

        body(step, slot)
        for copy in copies(step, slot):
            copy.start()
        return carry

    lax.fori_loop(0, steps, turn, 0)
    for step in range(max(steps - 2, 0), steps):
        for copy in copies(step, step % 2):
            copy.wait()


def grad_in_kernel(x_part, d_gate, d_up, grad_gate, grad_up, done, out_gate, out_up, sems):
    local_experts = d_gate.shape[0]
    part, rows = x_part.shape[0], out_gate.shape[1]
    done[...] = jnp.zeros(done.shape, done.dtype)
    blocks = part // rows

    def place(step):
        return step // blocks, aligned(lax.rem(step, blocks), rows), slice(None)

    def body(step, slot):
        expert, block, _ = place(step)
        out_gate[slot] = dot(x_part[block, :], d_gate[expert], NN)
        out_up[slot] = dot(x_part[block, :], d_up[expert], NN)

    write_out(
        local_experts * blocks, place, (grad_gate, grad_up), (out_gate, out_up), sems, body
    )


def grad_out_kernel(packet, hidden, after, grad_down, done, cot_part, out_down, sems):
    local_experts = hidden.shape[0]
    part = cot_part.shape[1]
    cot_part[...] = packet[:, aligned(lax.axis_index("dp"), part)]
    done[...] = jnp.zeros(done.shape, done.dtype)

    def place(step):
        return (step,)

    def body(step, slot):
        out_down[slot] = dot(hidden[step].T, cot_part[...], NN)

    write_out(local_experts, place, (grad_down,), (out_down,), sems, body)


def reduce_kernel(count, *refs):
    blocks, refs = refs[:count], refs[count:]
    expert_ids, after, route_grad = refs[:3]
    outs, done = refs[3:-1], refs[-1]
    done[...] = jnp.zeros(done.shape, done.dtype)
    rows, both = outs[0].shape
    half = (blocks[0].shape[1] - both) // 2
    for j, out in enumerate(outs):
        total = jnp.zeros((rows, both), jnp.float32)
        for block in blocks:
            total += block[j * rows : (j + 1) * rows, :both].astype(jnp.float32)
        out[...] = total.astype(out.dtype)
    inner = jnp.zeros((rows, 2 * half), jnp.float32)
    for block in blocks:
        inner += block[:rows, both:].astype(jnp.float32)
    inner = inner.T
    inner = inner[:half] + inner[half:]
    at = ids_along(inner.shape, 0)
    for k in range(expert_ids.shape[0]):
        hit = jnp.where(expert_ids[k : k + 1, :] == at, inner, 0.0)
        route_grad[k : k + 1, :] = jnp.sum(hit, axis=0, keepdims=True)


def join_kernel(count, *refs):
    blocks, (after, mixed, token_grad) = refs[:count], refs[count:]
    part = blocks[0].shape[1] // 2
    column = lax.axis_index("dp")
    for other, block in enumerate(blocks):
        cols = aligned(column ^ other, part)
        mixed[:, cols] = block[:, :part]
        token_grad[:, cols] = block[:, part:]


def swap(value, axis, mask):
    size = lax.axis_size(axis)
    return lax.ppermute(value, axis, [(i, i ^ mask) for i in range(size)])


def exchange(value, axis, masks):
    return [swap(value, axis, mask) for mask in masks]


def in_hbm(array):
    return pltpu.with_memory_space_constraint(array, pltpu.HBM)


def in_vmem(array):
    return pltpu.with_memory_space_constraint(array, pltpu.VMEM)


def cost(flops, moved):
    return pl.CostEstimate(flops=flops, bytes_accessed=moved, transcendentals=0)


def params(mib):
    return pltpu.CompilerParams(vmem_limit_bytes=mib * MIB)


def per_device(
    tokens, expert_ids, slot_index, route_weights, w_gate, w_up, w_down, block_masks, cotangent
):
    rows, width = tokens.shape
    local_experts, _, hidden_units = w_gate.shape
    sources, columns = lax.axis_size("expert"), lax.axis_size("dp")
    chips = list(range(2, sources, 2))
    expert_order = [0] + chips + [chip ^ 1 for chip in [0] + chips]
    lanes = -(-2 * local_experts * sources // LANES) * LANES
    part = width // columns
    everyone = sources * columns * rows
    bf16, f32 = jnp.bfloat16, jnp.float32
    struct = jax.ShapeDtypeStruct
    one = 2 * local_experts * width * hidden_units
    room = 16 + (everyone - TILE) * (2 * part + lanes) * 14 // MIB
    dummy = struct((8, LANES), f32)
    ids_t = expert_ids.T
    w_gate, w_up, w_down = [in_hbm(w) for w in (w_gate, w_up, w_down)]

    tokens_near = exchange(tokens, "dp", range(1, columns))
    gate, own_tokens = pl.pallas_call(
        load_kernel,
        out_shape=[pltpu.VMEM(w_gate.shape, bf16), struct(tokens.shape, bf16)],
        in_specs=[HBM] * 2,
        out_specs=[VMEM] * 2,
        scratch_shapes=[pltpu.SemaphoreType.DMA((2,))],
        cost_estimate=cost(0, one),
        compiler_params=params(room),
        name="load_gate",
    )(w_gate, in_hbm(tokens))
    gate = in_vmem(gate)
    x_column = jnp.concatenate([own_tokens] + tokens_near)
    x_across = exchange(x_column, "expert", chips)

    packet, x_column = pl.pallas_call(
        route_kernel,
        out_shape=[struct((rows, width + lanes), bf16), struct(x_column.shape, bf16)],
        in_specs=[HBM] * 3 + [VMEM],
        out_specs=[VMEM] * 2,
        scratch_shapes=[
            pltpu.VMEM(ids_t.shape, jnp.int32),
            pltpu.VMEM(ids_t.shape, bf16),
            pltpu.SemaphoreType.DMA((3,)),
        ],
        compiler_params=params(room),
        name="route",
    )(*[in_hbm(a) for a in (cotangent, ids_t, route_weights.T)], x_column)
    c_column = jnp.concatenate([packet] + exchange(packet, "dp", range(1, columns)))
    x = jnp.concatenate([x_column] + x_across)
    x = jnp.concatenate([x, swap(x, "expert", 1)])

    units = struct((local_experts, everyone, hidden_units), bf16)
    def gate_up(first, last, value, known):
        return pl.pallas_call(
            functools.partial(gate_up_kernel, first, last),
            out_shape=[units] * 3
            + [struct(value.shape, value.dtype)],
            in_specs=[VMEM, SMEM, VMEM, HBM] + [VMEM] * (1 + len(known)),
            out_specs=[VMEM] * 4,
            scratch_shapes=[
                pltpu.VMEM((min(2, last - first), width, hidden_units), bf16),
                pltpu.SemaphoreType.DMA((2,)),
            ],
            input_output_aliases={5 + i: i for i in range(len(known))},
            cost_estimate=cost(
                2 * everyone * one * (last - first) // local_experts,
                2 * one * (last - first) // local_experts,
            ),
            compiler_params=params(room),
            name="gate_up",
        )(x, block_masks, gate, w_up, value, *known)

    *factors, c_column = gate_up(0, 1, c_column, [])
    c_across = exchange(c_column, "expert", chips)
    if local_experts > 1:
        *factors, c_column = gate_up(1, local_experts, c_column, factors)
    c_half = jnp.concatenate([c_column] + c_across)
    packets = jnp.concatenate([c_half, swap(c_half, "expert", 1)])
    x_part = pl.pallas_call(
        turn_kernel,
        out_shape=struct((part, everyone), bf16),
        in_specs=[VMEM] * 2,
        out_specs=VMEM,
        compiler_params=params(room),
        name="turn",
    )(x, c_half)

    hidden, d_gate, d_up, *partials = pl.pallas_call(
        functools.partial(hidden_kernel, sources),
        out_shape=[units] * 3
        + [struct((columns * rows, 2 * part + lanes), bf16)] * sources,
        in_specs=[VMEM] * 4 + [HBM] * 3,
        out_specs=[VMEM] * (3 + sources),
        scratch_shapes=[
            pltpu.VMEM((everyone, lanes), f32),
            pltpu.VMEM((everyone, part), f32),
            pltpu.VMEM((everyone, part), f32),
            pltpu.VMEM((min(2, local_experts), hidden_units, width), bf16),
            pltpu.VMEM((min(2, local_experts), part, hidden_units), bf16),
            pltpu.VMEM((min(2, local_experts), part, hidden_units), bf16),
            pltpu.SemaphoreType.DMA((2, 2 + hidden_units // CHUNK)),
        ],
        cost_estimate=cost(2 * everyone * one, 2 * one),
        compiler_params=params(room),
        name="hidden",
    )(packets, *factors, w_gate, w_up, w_down)
    arrived = [
        swap(partial, "expert", other) if other else partial
        for other, partial in zip(expert_order, partials)
    ]

    grad_gate, grad_up, done_in = pl.pallas_call(
        grad_in_kernel,
        out_shape=[struct((local_experts, part, hidden_units), f32)] * 2 + [dummy],
        in_specs=[VMEM] * 3,
        out_specs=[HBM] * 2 + [VMEM],
        scratch_shapes=[
            pltpu.VMEM((2, min(part, CHUNK), hidden_units), f32),
            pltpu.VMEM((2, min(part, CHUNK), hidden_units), f32),
            pltpu.SemaphoreType.DMA((2, 2)),
        ],
        cost_estimate=cost(2 * everyone * one // columns, 4 * one // columns),
        compiler_params=params(room),
        name="grad_in",
    )(x_part, d_gate, d_up)

    route_grad, *blocks, done_sum = pl.pallas_call(
        functools.partial(reduce_kernel, sources),
        out_shape=[struct(ids_t.shape, f32)] + [struct((rows, 2 * part), bf16)] * columns + [dummy],
        in_specs=[VMEM] * (sources + 2),
        out_specs=[VMEM] * (columns + 2),
        compiler_params=params(room),
        name="reduce",
    )(*arrived, ids_t, done_in)
    blocks = [
        swap(block, "dp", other) if other else block for other, block in enumerate(blocks)
    ]

    grad_down, done_out = pl.pallas_call(
        grad_out_kernel,
        out_shape=[struct((local_experts, hidden_units, part), f32), dummy],
        in_specs=[VMEM] * 3,
        out_specs=[HBM, VMEM],
        scratch_shapes=[
            pltpu.VMEM((everyone, part), bf16),
            pltpu.VMEM((2, hidden_units, part), f32),
            pltpu.SemaphoreType.DMA((2, 1)),
        ],
        cost_estimate=cost(everyone * one // columns, 2 * one // columns),
        compiler_params=params(room),
        name="grad_out",
    )(packets, hidden, done_sum)

    mixed, token_grad = pl.pallas_call(
        functools.partial(join_kernel, columns),
        out_shape=[struct((rows, width), bf16)] * 2,
        in_specs=[VMEM] * (columns + 1),
        out_specs=[VMEM] * 2,
        compiler_params=params(room),
        name="join",
    )(*blocks, done_out)
    return (mixed, token_grad, route_grad.T, grad_gate, grad_up, grad_down)


def solution(mesh):
    rows = P(("groups", "expert", "dp"), None)
    experts = P("expert", None, None)
    return jax.shard_map(
        per_device,
        mesh=mesh,
        in_specs=(rows, rows, rows, rows, experts, experts, experts, P("expert", None), rows),
        out_specs=(
            rows,
            rows,
            rows,
            P(("groups", "expert"), "dp", None),
            P(("groups", "expert"), "dp", None),
            P(("groups", "expert"), None, "dp"),
        ),
        check_vma=False,
    )
```

```python
import functools

import jax
import jax.numpy as jnp
from jax import lax
from jax.experimental import pallas as pl
from jax.experimental.pallas import tpu as pltpu
from jax.sharding import PartitionSpec as P

BLK = 128
LANES = 128
CHUNK = 256
TILE = 256
MIB = 1 << 20

VMEM = pl.BlockSpec(memory_space=pltpu.VMEM)
SMEM = pl.BlockSpec(memory_space=pltpu.SMEM)
HBM = pl.BlockSpec(memory_space=pltpu.HBM)

NN = (((1,), (0,)), ((), ()))
NT = (((1,), (1,)), ((), ()))


def dot(a, b, dims):
    return lax.dot_general(a, b, dims, preferred_element_type=jnp.float32)


def ids_along(shape, axis):
    return lax.broadcasted_iota(jnp.int32, shape, axis)


def aligned(index, size):
    return pl.ds(pl.multiple_of(index * size, size), size)


def route_kernel(
    tokens, cotangent, expert_ids, route_weights, own_tokens, packet, ids, values, sems
):
    rows, width = tokens.shape
    lanes = packet.shape[1] - width
    copies = [
        pltpu.make_async_copy(expert_ids, ids, sems.at[0]),
        pltpu.make_async_copy(route_weights, values, sems.at[1]),
        pltpu.make_async_copy(tokens, own_tokens, sems.at[2]),
        pltpu.make_async_copy(cotangent, packet.at[:, :width], sems.at[3]),
    ]
    for copy in copies:
        copy.start()
    for copy in copies:
        copy.wait()
    at = ids_along((lanes, rows), 0)
    weights = values[...].astype(jnp.float32)
    dense = jnp.zeros((lanes, rows), jnp.float32)
    for k in range(ids.shape[0]):
        dense += jnp.where(ids[k : k + 1, :] == at, weights[k : k + 1, :], 0.0)
    packet[:, width:] = dense.T.astype(packet.dtype)


def load_kernel(source, value, target, same, sem):
    copy = pltpu.make_async_copy(source, target, sem)
    copy.start()
    same[...] = value[...]
    copy.wait()


def turn_kernel(x, after, x_part):
    x_part[...] = x[:, aligned(lax.axis_index("dp"), x_part.shape[0])].T


def over_tiles(tokens, body):
    if tokens == TILE:
        body(slice(0, TILE))
    else:

        def turn(tile, carry):
            body(aligned(tile, TILE))
            return carry

        lax.fori_loop(0, tokens // TILE, turn, 0)


def gate_kernel(x, gate, w_up, gate_pre, gate_part, up, sems):
    local_experts, _, hidden_units = gate.shape
    mine = aligned(lax.axis_index("dp"), gate_part.shape[1])
    loads = [
        pltpu.make_async_copy(w_up, up, sems.at[0]),
        pltpu.make_async_copy(gate.at[:, mine, :], gate_part, sems.at[1]),
    ]
    for load in loads:
        load.start()

    def tile(rows):
        for expert in range(local_experts):
            for start in range(0, hidden_units, CHUNK):
                cols = slice(start, start + CHUNK)
                gate_pre[expert, rows, cols] = dot(x[rows, :], gate[expert, :, cols], NN)

    over_tiles(x.shape[0], tile)
    for load in loads:
        load.wait()


def up_kernel(first, last, *refs):
    x, masks, gate_pre, up, w_down, value = refs[:6]
    hidden, slope_up, slope_gate, down, up_part, same, sems = refs[-7:]
    hidden_units = up.shape[2]
    bf16 = jnp.bfloat16
    mine = aligned(lax.axis_index("dp"), up_part.shape[1])
    loads = [
        pltpu.make_async_copy(w_down.at[first:last], down, sems.at[0]),
        pltpu.make_async_copy(up.at[first:last, mine, :], up_part, sems.at[1]),
    ]
    for load in loads:
        load.start()
    same[...] = value[...]

    def tile(rows):
        for expert in range(first, last):
            for start in range(0, hidden_units, CHUNK):
                cols = slice(start, start + CHUNK)
                up_proj = dot(x[rows, :], up[expert, :, cols], NN)
                at = ids_along((1, CHUNK), 1)
                keep = jnp.zeros((1, CHUNK), jnp.float32)
                for j in range(CHUNK // BLK):
                    kept = masks[expert, start // BLK + j].astype(jnp.float32)
                    keep = jnp.where(at // BLK == j, kept, keep)
                gated = gate_pre[expert, rows, cols]
                sigma = 0.5 + 0.5 * jnp.tanh(0.5 * gated)
                silu = gated * sigma
                up_kept = up_proj * keep
                hidden[expert, rows, cols] = (silu * up_kept).astype(bf16)
                slope_up[expert, rows, cols] = (silu * keep).astype(bf16)
                slope = up_kept * (sigma + silu * (1.0 - sigma))
                slope_gate[expert, rows, cols] = slope.astype(bf16)

    over_tiles(x.shape[0], tile)
    for load in loads:
        load.wait()


def hidden_kernel(halves, count, *refs):
    packet, units, slope_up, slope_gate, gate = refs[:5]
    ups, refs = refs[5 : 5 + len(halves)], refs[5 + len(halves) :]
    downs, refs = refs[: len(halves)], refs[len(halves) :]
    hidden, d_gate, d_up = refs[:3]
    outs, (inner, mixed, token_grad) = refs[3 : 3 + count], refs[3 + count :]
    hidden_units, width = downs[0].shape[1:]
    tokens, part = mixed.shape
    local_experts = gate.shape[0]
    lanes = packet.shape[1] - width
    half = lanes // 2
    base = lax.axis_index("expert") * local_experts
    mine = aligned(lax.axis_index("dp"), part)
    bf16, f32 = jnp.bfloat16, jnp.float32
    inner[...] = jnp.zeros(inner.shape, inner.dtype)
    mixed[...] = jnp.zeros(mixed.shape, mixed.dtype)
    token_grad[...] = jnp.zeros(token_grad.shape, token_grad.dtype)

    def one_expert(up, down, first, expert, carry):
        def tile(rows):
            dense = packet[rows, width:].astype(f32)
            at = ids_along((TILE, lanes), 1)
            hit = at == base + expert
            weights = jnp.sum(jnp.where(hit, dense, 0.0), axis=1, keepdims=True)
            total = jnp.zeros((TILE, 1), f32)
            for start in range(0, hidden_units, CHUNK):
                cols = slice(start, start + CHUNK)
                back = dot(packet[rows, :width], down[expert - first, cols, :], NT)
                part_units = units[expert, rows, cols].astype(f32)
                total += jnp.sum(part_units * back, axis=1, keepdims=True)
                back = back * weights
                new_gate = back * slope_gate[expert, rows, cols].astype(f32)
                new_up = back * slope_up[expert, rows, cols].astype(f32)
                hidden[expert, rows, cols] = (part_units * weights).astype(bf16)
                d_gate[expert, rows, cols] = new_gate.astype(bf16)
                d_up[expert, rows, cols] = new_up.astype(bf16)
            high = total.astype(bf16).astype(f32)
            inner[rows, :] += jnp.where(
                hit, high, jnp.where(at == base + expert + half, total - high, 0.0)
            )
            mixed[rows, :] += dot(hidden[expert, rows, :], down[expert - first, :, mine], NN)
            token_grad[rows, :] += dot(d_gate[expert, rows, :], gate[expert], NT) + dot(
                d_up[expert, rows, :], up[expert - first], NT
            )

        over_tiles(tokens, tile)
        return carry

    for (first, last), up, down in zip(halves, ups, downs):
        lax.fori_loop(first, last, functools.partial(one_expert, up, down, first), 0)
    rows = outs[0].shape[0]
    for i, out in enumerate(outs):
        block = slice(i * rows, (i + 1) * rows)
        out[:, :part] = mixed[block].astype(bf16)
        out[:, part : 2 * part] = token_grad[block].astype(bf16)
        out[:, 2 * part :] = inner[block].astype(bf16)


def write_out(steps, place, outs, bufs, sems, body):
    def copies(step, slot):
        return [
            pltpu.make_async_copy(buf.at[slot], out.at[place(step)], sems.at[slot, i])
            for i, (out, buf) in enumerate(zip(outs, bufs))
        ]

    def turn(step, carry):
        slot = lax.rem(step, 2)

        @pl.when(step >= 2)
        def _():
            for copy in copies(step - 2, slot):
                copy.wait()

        body(step, slot)
        for copy in copies(step, slot):
            copy.start()
        return carry

    lax.fori_loop(0, steps, turn, 0)
    for step in range(max(steps - 2, 0), steps):
        for copy in copies(step, step % 2):
            copy.wait()


def grad_in_kernel(x_part, d_gate, d_up, grad_gate, grad_up, done, out_gate, out_up, sems):
    local_experts = d_gate.shape[0]
    part, rows = x_part.shape[0], out_gate.shape[1]
    done[...] = jnp.zeros(done.shape, done.dtype)
    blocks = part // rows

    def place(step):
        return step // blocks, aligned(lax.rem(step, blocks), rows), slice(None)

    def body(step, slot):
        expert, block, _ = place(step)
        out_gate[slot] = dot(x_part[block, :], d_gate[expert], NN)
        out_up[slot] = dot(x_part[block, :], d_up[expert], NN)

    write_out(
        local_experts * blocks, place, (grad_gate, grad_up), (out_gate, out_up), sems, body
    )


def grad_out_kernel(packet, hidden, after, grad_down, done, cot_part, out_down, sems):
    local_experts = hidden.shape[0]
    part = cot_part.shape[1]
    cot_part[...] = packet[:, aligned(lax.axis_index("dp"), part)]
    done[...] = jnp.zeros(done.shape, done.dtype)

    def place(step):
        return (step,)

    def body(step, slot):
        out_down[slot] = dot(hidden[step].T, cot_part[...], NN)

    write_out(local_experts, place, (grad_down,), (out_down,), sems, body)


def reduce_kernel(count, *refs):
    blocks, refs = refs[:count], refs[count:]
    expert_ids, after, route_grad = refs[:3]
    outs, done = refs[3:-1], refs[-1]
    done[...] = jnp.zeros(done.shape, done.dtype)
    rows, both = outs[0].shape
    half = (blocks[0].shape[1] - both) // 2
    for j, out in enumerate(outs):
        total = jnp.zeros((rows, both), jnp.float32)
        for block in blocks:
            total += block[j * rows : (j + 1) * rows, :both].astype(jnp.float32)
        out[...] = total.astype(out.dtype)
    inner = jnp.zeros((rows, 2 * half), jnp.float32)
    for block in blocks:
        inner += block[:rows, both:].astype(jnp.float32)
    inner = inner.T
    inner = inner[:half] + inner[half:]
    at = ids_along(inner.shape, 0)
    for k in range(expert_ids.shape[0]):
        hit = jnp.where(expert_ids[k : k + 1, :] == at, inner, 0.0)
        route_grad[k : k + 1, :] = jnp.sum(hit, axis=0, keepdims=True)


def join_kernel(count, *refs):
    blocks, (after, mixed, token_grad) = refs[:count], refs[count:]
    part = blocks[0].shape[1] // 2
    column = lax.axis_index("dp")
    for other, block in enumerate(blocks):
        cols = aligned(column ^ other, part)
        mixed[:, cols] = block[:, :part]
        token_grad[:, cols] = block[:, part:]


def swap(value, axis, mask):
    size = lax.axis_size(axis)
    return lax.ppermute(value, axis, [(i, i ^ mask) for i in range(size)])


def exchange(value, axis, masks):
    return [swap(value, axis, mask) for mask in masks]


def in_hbm(array):
    return pltpu.with_memory_space_constraint(array, pltpu.HBM)


def in_vmem(array):
    return pltpu.with_memory_space_constraint(array, pltpu.VMEM)


def cost(flops, moved):
    return pl.CostEstimate(flops=flops, bytes_accessed=moved, transcendentals=0)


def params(mib):
    return pltpu.CompilerParams(vmem_limit_bytes=mib * MIB)


def per_device(
    tokens, expert_ids, slot_index, route_weights, w_gate, w_up, w_down, block_masks, cotangent
):
    rows, width = tokens.shape
    local_experts, _, hidden_units = w_gate.shape
    sources, columns = lax.axis_size("expert"), lax.axis_size("dp")
    chips = list(range(2, sources, 2))
    expert_order = [0] + chips + [chip ^ 1 for chip in [0] + chips]
    lanes = -(-2 * local_experts * sources // LANES) * LANES
    part = width // columns
    everyone = sources * columns * rows
    bf16, f32 = jnp.bfloat16, jnp.float32
    struct = jax.ShapeDtypeStruct
    one = 2 * local_experts * width * hidden_units
    room = 8 + (everyone - TILE) * (2 * part + lanes) * 10 // MIB
    dummy = struct((8, LANES), f32)
    ids_t = expert_ids.T
    w_gate, w_up, w_down = [in_hbm(w) for w in (w_gate, w_up, w_down)]

    own_tokens, packet = pl.pallas_call(
        route_kernel,
        out_shape=[struct(tokens.shape, bf16), struct((rows, width + lanes), bf16)],
        in_specs=[HBM] * 4,
        out_specs=[VMEM] * 2,
        scratch_shapes=[
            pltpu.VMEM(ids_t.shape, jnp.int32),
            pltpu.VMEM(ids_t.shape, bf16),
            pltpu.SemaphoreType.DMA((4,)),
        ],
        compiler_params=params(room),
        name="route",
    )(*[in_hbm(a) for a in (tokens, cotangent, ids_t, route_weights.T)])

    def load(weight, value, name):
        return pl.pallas_call(
            load_kernel,
            out_shape=[
                pltpu.VMEM(weight.shape, weight.dtype),
                struct(value.shape, value.dtype),
            ],
            in_specs=[HBM, VMEM],
            out_specs=[VMEM] * 2,
            scratch_shapes=[pltpu.SemaphoreType.DMA],
            cost_estimate=cost(0, one),
            compiler_params=params(room),
            name=name,
        )(weight, value)

    x_column = jnp.concatenate([own_tokens] + exchange(tokens, "dp", range(1, columns)))
    c_column = jnp.concatenate([packet] + exchange(packet, "dp", range(1, columns)))
    x_across = exchange(x_column, "expert", chips)
    c_across = exchange(c_column, "expert", chips)
    gate, x_column = load(w_gate, x_column, "load_gate")
    gate = in_vmem(gate)
    x = jnp.concatenate([x_column] + x_across)
    x = jnp.concatenate([x, swap(x, "expert", 1)])

    gate_pre, gate_part, up = pl.pallas_call(
        gate_kernel,
        out_shape=[
            struct((local_experts, everyone, hidden_units), f32),
            pltpu.VMEM((local_experts, part, hidden_units), bf16),
            pltpu.VMEM(w_up.shape, bf16),
        ],
        in_specs=[VMEM] * 2 + [HBM],
        out_specs=[VMEM] * 3,
        scratch_shapes=[pltpu.SemaphoreType.DMA((2,))],
        cost_estimate=cost(everyone * one, one),
        compiler_params=params(room),
        name="gate",
    )(x, gate, w_up)
    up = in_vmem(up)

    units = struct((local_experts, everyone, hidden_units), bf16)

    def up_call(first, last, value, known):
        return pl.pallas_call(
            functools.partial(up_kernel, first, last),
            out_shape=[units] * 3
            + [pltpu.VMEM((last - first,) + w_down.shape[1:], bf16)]
            + [pltpu.VMEM((last - first, part, hidden_units), bf16)]
            + [struct(value.shape, value.dtype)],
            in_specs=[VMEM, SMEM, VMEM, VMEM, HBM] + [VMEM] * (1 + len(known)),
            out_specs=[VMEM] * 6,
            scratch_shapes=[pltpu.SemaphoreType.DMA((2,))],
            input_output_aliases={6 + i: i for i in range(len(known))},
            cost_estimate=cost(
                everyone * one * (last - first) // local_experts,
                one * (last - first) // local_experts,
            ),
            compiler_params=params(room),
            name="up",
        )(x, block_masks, gate_pre, up, w_down, value, *known)

    middle = local_experts // 2
    halves = [(0, middle), (middle, local_experts)] if middle else [(0, local_experts)]
    factors, downs, ups = [], [], []
    for first, last in halves:
        *factors, down, up_part, same = up_call(first, last, c_column, factors)
        downs.append(in_vmem(down))
        ups.append(in_vmem(up_part))
        if first == 0:
            c_column = same
    c_half = jnp.concatenate([c_column] + c_across)
    packets = jnp.concatenate([c_half, swap(c_half, "expert", 1)])
    x_part = pl.pallas_call(
        turn_kernel,
        out_shape=struct((part, everyone), bf16),
        in_specs=[VMEM] * 2,
        out_specs=VMEM,
        compiler_params=params(room),
        name="turn",
    )(x, c_half)

    hidden, d_gate, d_up, *partials = pl.pallas_call(
        functools.partial(hidden_kernel, halves, sources),
        out_shape=[units] * 3
        + [struct((columns * rows, 2 * part + lanes), bf16)] * sources,
        in_specs=[VMEM] * (5 + 2 * len(halves)),
        out_specs=[VMEM] * (3 + sources),
        scratch_shapes=[
            pltpu.VMEM((everyone, lanes), f32),
            pltpu.VMEM((everyone, part), f32),
            pltpu.VMEM((everyone, part), f32),
        ],
        cost_estimate=cost(2 * everyone * one, 2 * one),
        compiler_params=params(room),
        name="hidden",
    )(packets, *factors, in_vmem(gate_part), *ups, *downs)
    arrived = [
        swap(partial, "expert", other) if other else partial
        for other, partial in zip(expert_order, partials)
    ]

    grad_gate, grad_up, done_in = pl.pallas_call(
        grad_in_kernel,
        out_shape=[struct((local_experts, part, hidden_units), f32)] * 2 + [dummy],
        in_specs=[VMEM] * 3,
        out_specs=[HBM] * 2 + [VMEM],
        scratch_shapes=[
            pltpu.VMEM((2, min(part, CHUNK), hidden_units), f32),
            pltpu.VMEM((2, min(part, CHUNK), hidden_units), f32),
            pltpu.SemaphoreType.DMA((2, 2)),
        ],
        cost_estimate=cost(2 * everyone * one // columns, 4 * one // columns),
        compiler_params=params(room),
        name="grad_in",
    )(x_part, d_gate, d_up)

    route_grad, *blocks, done_sum = pl.pallas_call(
        functools.partial(reduce_kernel, sources),
        out_shape=[struct(ids_t.shape, f32)] + [struct((rows, 2 * part), bf16)] * columns + [dummy],
        in_specs=[VMEM] * (sources + 2),
        out_specs=[VMEM] * (columns + 2),
        compiler_params=params(room),
        name="reduce",
    )(*arrived, ids_t, done_in)
    blocks = [
        swap(block, "dp", other) if other else block for other, block in enumerate(blocks)
    ]

    grad_down, done_out = pl.pallas_call(
        grad_out_kernel,
        out_shape=[struct((local_experts, hidden_units, part), f32), dummy],
        in_specs=[VMEM] * 3,
        out_specs=[HBM, VMEM],
        scratch_shapes=[
            pltpu.VMEM((everyone, part), bf16),
            pltpu.VMEM((2, hidden_units, part), f32),
            pltpu.SemaphoreType.DMA((2, 1)),
        ],
        cost_estimate=cost(everyone * one // columns, 2 * one // columns),
        compiler_params=params(room),
        name="grad_out",
    )(packets, hidden, done_sum)

    mixed, token_grad = pl.pallas_call(
        functools.partial(join_kernel, columns),
        out_shape=[struct((rows, width), bf16)] * 2,
        in_specs=[VMEM] * (columns + 1),
        out_specs=[VMEM] * 2,
        compiler_params=params(room),
        name="join",
    )(*blocks, done_out)
    return (mixed, token_grad, route_grad.T, grad_gate, grad_up, grad_down)


def solution(mesh):
    rows = P(("groups", "expert", "dp"), None)
    experts = P("expert", None, None)
    return jax.shard_map(
        per_device,
        mesh=mesh,
        in_specs=(rows, rows, rows, rows, experts, experts, experts, P("expert", None), rows),
        out_specs=(
            rows,
            rows,
            rows,
            P(("groups", "expert"), "dp", None),
            P(("groups", "expert"), "dp", None),
            P(("groups", "expert"), None, "dp"),
        ),
        check_vma=False,
    )
```

```python
import functools

import jax
import jax.numpy as jnp
from jax import lax
from jax.experimental import pallas as pl
from jax.experimental.pallas import tpu as pltpu
from jax.sharding import PartitionSpec as P

BLK = 128
LANES = 128
CHUNK = 256
TILE = 256
MIB = 1 << 20

VMEM = pl.BlockSpec(memory_space=pltpu.VMEM)
SMEM = pl.BlockSpec(memory_space=pltpu.SMEM)
HBM = pl.BlockSpec(memory_space=pltpu.HBM)

NN = (((1,), (0,)), ((), ()))
NT = (((1,), (1,)), ((), ()))


def dot(a, b, dims):
    return lax.dot_general(a, b, dims, preferred_element_type=jnp.float32)


def ids_along(shape, axis):
    return lax.broadcasted_iota(jnp.int32, shape, axis)


def aligned(index, size):
    return pl.ds(pl.multiple_of(index * size, size), size)


def route_kernel(
    tokens, cotangent, expert_ids, route_weights, own_tokens, packet, ids, values, sems
):
    rows, width = tokens.shape
    lanes = packet.shape[1] - width
    copies = [
        pltpu.make_async_copy(expert_ids, ids, sems.at[0]),
        pltpu.make_async_copy(route_weights, values, sems.at[1]),
        pltpu.make_async_copy(tokens, own_tokens, sems.at[2]),
        pltpu.make_async_copy(cotangent, packet.at[:, :width], sems.at[3]),
    ]
    for copy in copies:
        copy.start()
    for copy in copies:
        copy.wait()
    at = ids_along((lanes, rows), 0)
    weights = values[...].astype(jnp.float32)
    dense = jnp.zeros((lanes, rows), jnp.float32)
    for k in range(ids.shape[0]):
        dense += jnp.where(ids[k : k + 1, :] == at, weights[k : k + 1, :], 0.0)
    packet[:, width:] = dense.T.astype(packet.dtype)


def load_kernel(weight, value, same, *refs):
    targets, sems = refs[:-1], refs[-1]
    copies = [
        pltpu.make_async_copy(weight.at[i], target, sems.at[i]) for i, target in enumerate(targets)
    ]
    for copy in copies:
        copy.start()
    same[...] = value[...]
    for copy in copies:
        copy.wait()


def turn_kernel(x, after, x_part):
    x_part[...] = x[:, aligned(lax.axis_index("dp"), x_part.shape[0])].T


def over_tiles(tokens, body):
    if tokens == TILE:
        body(slice(0, TILE))
    else:

        def turn(tile, carry):
            body(aligned(tile, TILE))
            return carry

        lax.fori_loop(0, tokens // TILE, turn, 0)


def gate_up_kernel(first, last, *refs):
    count = last - first
    gates, refs = refs[:count], refs[count:]
    x, masks, w_up, w_down, value = refs[:5]
    known, (same, up, sems) = refs[5:-3], refs[-3:]
    hidden_units = gates[0].shape[1]
    bf16 = jnp.bfloat16
    hiddens, slope_ups, slope_gates, gate_parts, up_parts, downs = [known[k::6] for k in range(6)]
    mine = aligned(lax.axis_index("dp"), gate_parts[0].shape[0])
    ups = [
        pltpu.make_async_copy(w_up.at[first + i], up.at[i % 2], sems.at[i]) for i in range(count)
    ]
    keeps = [
        pltpu.make_async_copy(up.at[i % 2, mine, :], up_parts[i], sems.at[3 * count + i])
        for i in range(count)
    ]
    loads = [
        pltpu.make_async_copy(gates[i].at[mine, :], gate_parts[i], sems.at[count + i])
        for i in range(count)
    ] + [
        pltpu.make_async_copy(w_down.at[first + i], downs[i], sems.at[2 * count + i])
        for i in range(count)
    ]
    for load in ups[:2] + loads:
        load.start()
    same[...] = value[...]
    chunks = [slice(start, start + CHUNK) for start in range(0, hidden_units, CHUNK)]

    def products(rows, weights):
        return [dot(x[rows, :], weights[:, cols], NN) for cols in chunks]

    def finish(i, rows, cols, gate_pre, up_proj):
        at = ids_along((1, CHUNK), 1)
        keep = jnp.zeros((1, CHUNK), jnp.float32)
        for j in range(CHUNK // BLK):
            kept = masks[first + i, cols.start // BLK + j].astype(jnp.float32)
            keep = jnp.where(at // BLK == j, kept, keep)
        sigma = 0.5 + 0.5 * jnp.tanh(0.5 * gate_pre)
        silu = gate_pre * sigma
        up_kept = up_proj * keep
        hiddens[i][rows, cols] = (silu * up_kept).astype(bf16)
        slope_ups[i][rows, cols] = (silu * keep).astype(bf16)
        slope = up_kept * (sigma + silu * (1.0 - sigma))
        slope_gates[i][rows, cols] = slope.astype(bf16)

    for i in range(count):

        def tile(rows, i=i, early=None):
            gate_pres = early or products(rows, gates[i])
            for cols, gate_pre, up_proj in zip(chunks, gate_pres, products(rows, up.at[i % 2])):
                finish(i, rows, cols, gate_pre, up_proj)

        if x.shape[0] == TILE:
            early = products(slice(0, TILE), gates[i])
            ups[i].wait()
            tile(slice(0, TILE), early=early)
        else:
            ups[i].wait()
            over_tiles(x.shape[0], tile)
        keeps[i].start()
        if i + 2 < count:
            keeps[i].wait()
            ups[i + 2].start()
    for load in loads + keeps[max(count - 2, 0) :]:
        load.wait()


def hidden_kernel(local_experts, count, *refs):
    packet, refs = refs[0], refs[1:]
    known = [refs[i * 6 : i * 6 + 6] for i in range(local_experts)]
    refs = refs[6 * local_experts :]
    hidden, d_gate, d_up = refs[:3]
    outs, (inner, mixed, token_grad) = refs[3 : 3 + count], refs[3 + count :]
    hidden_units, width = known[0][5].shape
    tokens, part = mixed.shape
    lanes = packet.shape[1] - width
    half = lanes // 2
    base = lax.axis_index("expert") * local_experts
    mine = aligned(lax.axis_index("dp"), part)
    bf16, f32 = jnp.bfloat16, jnp.float32
    inner[...] = jnp.zeros(inner.shape, inner.dtype)
    mixed[...] = jnp.zeros(mixed.shape, mixed.dtype)
    token_grad[...] = jnp.zeros(token_grad.shape, token_grad.dtype)

    for expert in range(local_experts):

        def tile(rows, expert=expert):
            units, slope_up, slope_gate, gate, up, down = known[expert]
            dense = packet[rows, width:].astype(f32)
            at = ids_along((TILE, lanes), 1)
            hit = at == base + expert
            weights = jnp.sum(jnp.where(hit, dense, 0.0), axis=1, keepdims=True)
            total = jnp.zeros((TILE, 1), f32)
            for start in range(0, hidden_units, CHUNK):
                cols = slice(start, start + CHUNK)
                back = dot(packet[rows, :width], down[cols, :], NT)
                part_units = units[rows, cols].astype(f32)
                total += jnp.sum(part_units * back, axis=1, keepdims=True)
                back = back * weights
                new_gate = back * slope_gate[rows, cols].astype(f32)
                new_up = back * slope_up[rows, cols].astype(f32)
                hidden[expert, rows, cols] = (part_units * weights).astype(bf16)
                d_gate[expert, rows, cols] = new_gate.astype(bf16)
                d_up[expert, rows, cols] = new_up.astype(bf16)
            high = total.astype(bf16).astype(f32)
            inner[rows, :] += jnp.where(
                hit, high, jnp.where(at == base + expert + half, total - high, 0.0)
            )
            mixed[rows, :] += dot(hidden[expert, rows, :], down[:, mine], NN)
            token_grad[rows, :] += dot(d_gate[expert, rows, :], gate[...], NT) + dot(
                d_up[expert, rows, :], up[...], NT
            )

        over_tiles(tokens, tile)

    rows = outs[0].shape[0]
    for i, out in enumerate(outs):
        block = slice(i * rows, (i + 1) * rows)
        out[:, :part] = mixed[block].astype(bf16)
        out[:, part : 2 * part] = token_grad[block].astype(bf16)
        out[:, 2 * part :] = inner[block].astype(bf16)


def write_out(steps, place, outs, bufs, sems, body):
    def copies(step, slot):
        return [
            pltpu.make_async_copy(buf.at[slot], out.at[place(step)], sems.at[slot, i])
            for i, (out, buf) in enumerate(zip(outs, bufs))
        ]

    def turn(step, carry):
        slot = lax.rem(step, 2)

        @pl.when(step >= 2)
        def _():
            for copy in copies(step - 2, slot):
                copy.wait()

        body(step, slot)
        for copy in copies(step, slot):
            copy.start()
        return carry

    lax.fori_loop(0, steps, turn, 0)
    for step in range(max(steps - 2, 0), steps):
        for copy in copies(step, step % 2):
            copy.wait()


def grad_in_kernel(x_part, d_gate, d_up, grad_gate, grad_up, done, out_gate, out_up, sems):
    local_experts = d_gate.shape[0]
    part, rows = x_part.shape[0], out_gate.shape[1]
    done[...] = jnp.zeros(done.shape, done.dtype)
    blocks = part // rows

    def place(step):
        return step // blocks, aligned(lax.rem(step, blocks), rows), slice(None)

    def body(step, slot):
        expert, block, _ = place(step)
        out_gate[slot] = dot(x_part[block, :], d_gate[expert], NN)
        out_up[slot] = dot(x_part[block, :], d_up[expert], NN)

    write_out(
        local_experts * blocks, place, (grad_gate, grad_up), (out_gate, out_up), sems, body
    )


def grad_out_kernel(packet, hidden, after, grad_down, done, cot_part, out_down, sems):
    local_experts = hidden.shape[0]
    part = cot_part.shape[1]
    cot_part[...] = packet[:, aligned(lax.axis_index("dp"), part)]
    done[...] = jnp.zeros(done.shape, done.dtype)

    def place(step):
        return (step,)

    def body(step, slot):
        out_down[slot] = dot(hidden[step].T, cot_part[...], NN)

    write_out(local_experts, place, (grad_down,), (out_down,), sems, body)


def reduce_kernel(count, *refs):
    blocks, refs = refs[:count], refs[count:]
    expert_ids, after, route_grad = refs[:3]
    outs, done = refs[3:-1], refs[-1]
    done[...] = jnp.zeros(done.shape, done.dtype)
    rows, both = outs[0].shape
    half = (blocks[0].shape[1] - both) // 2
    for j, out in enumerate(outs):
        total = jnp.zeros((rows, both), jnp.float32)
        for block in blocks:
            total += block[j * rows : (j + 1) * rows, :both].astype(jnp.float32)
        out[...] = total.astype(out.dtype)
    inner = jnp.zeros((rows, 2 * half), jnp.float32)
    for block in blocks:
        inner += block[:rows, both:].astype(jnp.float32)
    inner = inner.T
    inner = inner[:half] + inner[half:]
    at = ids_along(inner.shape, 0)
    for k in range(expert_ids.shape[0]):
        hit = jnp.where(expert_ids[k : k + 1, :] == at, inner, 0.0)
        route_grad[k : k + 1, :] = jnp.sum(hit, axis=0, keepdims=True)


def join_kernel(count, *refs):
    blocks, (after, mixed, token_grad) = refs[:count], refs[count:]
    part = blocks[0].shape[1] // 2
    column = lax.axis_index("dp")
    for other, block in enumerate(blocks):
        cols = aligned(column ^ other, part)
        mixed[:, cols] = block[:, :part]
        token_grad[:, cols] = block[:, part:]


def swap(value, axis, mask):
    size = lax.axis_size(axis)
    return lax.ppermute(value, axis, [(i, i ^ mask) for i in range(size)])


def exchange(value, axis, masks):
    return [swap(value, axis, mask) for mask in masks]


def in_hbm(array):
    return pltpu.with_memory_space_constraint(array, pltpu.HBM)


def in_vmem(array):
    return pltpu.with_memory_space_constraint(array, pltpu.VMEM)


def cost(flops, moved):
    return pl.CostEstimate(flops=flops, bytes_accessed=moved, transcendentals=0)


def params(mib):
    return pltpu.CompilerParams(vmem_limit_bytes=mib * MIB)


def per_device(
    tokens, expert_ids, slot_index, route_weights, w_gate, w_up, w_down, block_masks, cotangent
):
    rows, width = tokens.shape
    local_experts, _, hidden_units = w_gate.shape
    sources, columns = lax.axis_size("expert"), lax.axis_size("dp")
    chips = list(range(2, sources, 2))
    expert_order = [0] + chips + [chip ^ 1 for chip in [0] + chips]
    lanes = -(-2 * local_experts * sources // LANES) * LANES
    part = width // columns
    everyone = sources * columns * rows
    bf16, f32 = jnp.bfloat16, jnp.float32
    struct = jax.ShapeDtypeStruct
    one = 2 * local_experts * width * hidden_units
    room = 11 + (everyone - TILE) * (2 * part + lanes) * 10 // MIB
    dummy = struct((8, LANES), f32)
    ids_t = expert_ids.T
    w_gate, w_up, w_down = [in_hbm(w) for w in (w_gate, w_up, w_down)]

    own_tokens, packet = pl.pallas_call(
        route_kernel,
        out_shape=[struct(tokens.shape, bf16), struct((rows, width + lanes), bf16)],
        in_specs=[HBM] * 4,
        out_specs=[VMEM] * 2,
        scratch_shapes=[
            pltpu.VMEM(ids_t.shape, jnp.int32),
            pltpu.VMEM(ids_t.shape, bf16),
            pltpu.SemaphoreType.DMA((4,)),
        ],
        compiler_params=params(room),
        name="route",
    )(*[in_hbm(a) for a in (tokens, cotangent, ids_t, route_weights.T)])

    x_column = jnp.concatenate([own_tokens] + exchange(tokens, "dp", range(1, columns)))
    c_column = jnp.concatenate([packet] + exchange(packet, "dp", range(1, columns)))
    x_across = exchange(x_column, "expert", chips)
    c_across = exchange(c_column, "expert", chips)
    x_column, *gates = pl.pallas_call(
        load_kernel,
        out_shape=[struct(x_column.shape, bf16)]
        + [pltpu.VMEM(w_gate.shape[1:], bf16)] * local_experts,
        in_specs=[HBM, VMEM],
        out_specs=[VMEM] * (1 + local_experts),
        scratch_shapes=[pltpu.SemaphoreType.DMA((local_experts,))],
        cost_estimate=cost(0, one),
        compiler_params=params(room),
        name="load_gate",
    )(w_gate, x_column)
    gates = [in_vmem(gate) for gate in gates]
    x = jnp.concatenate([x_column] + x_across)
    x = jnp.concatenate([x, swap(x, "expert", 1)])

    def gate_up(first, last, value):
        count = last - first
        one_expert = [struct((everyone, hidden_units), bf16)] * 3
        one_expert += [pltpu.VMEM((part, hidden_units), bf16)] * 2
        one_expert += [pltpu.VMEM(w_down.shape[1:], bf16)]
        *known, same = pl.pallas_call(
            functools.partial(gate_up_kernel, first, last),
            out_shape=one_expert * count + [struct(value.shape, value.dtype)],
            in_specs=[VMEM] * (count + 1) + [SMEM, HBM, HBM, VMEM],
            out_specs=[VMEM] * (6 * count + 1),
            scratch_shapes=[
                pltpu.VMEM((min(2, count), width, hidden_units), bf16),
                pltpu.SemaphoreType.DMA((4 * count,)),
            ],
            cost_estimate=cost(
                2 * everyone * one * count // local_experts, 2 * one * count // local_experts
            ),
            compiler_params=params(room),
            name="gate_up",
        )(*gates[first:last], x, block_masks, w_up, w_down, value)
        return [in_vmem(a) if i % 6 >= 3 else a for i, a in enumerate(known)], same

    middle = local_experts // 2
    known, c_column = gate_up(0, middle or local_experts, c_column)
    if middle:
        more, _ = gate_up(middle, local_experts, c_column)
        known = known + more
    c_half = jnp.concatenate([c_column] + c_across)
    packets = jnp.concatenate([c_half, swap(c_half, "expert", 1)])
    x_part = pl.pallas_call(
        turn_kernel,
        out_shape=struct((part, everyone), bf16),
        in_specs=[VMEM] * 2,
        out_specs=VMEM,
        compiler_params=params(room),
        name="turn",
    )(x, c_half)

    units = struct((local_experts, everyone, hidden_units), bf16)
    hidden, d_gate, d_up, *partials = pl.pallas_call(
        functools.partial(hidden_kernel, local_experts, sources),
        out_shape=[units] * 3
        + [struct((columns * rows, 2 * part + lanes), bf16)] * sources,
        in_specs=[VMEM] * (1 + len(known)),
        out_specs=[VMEM] * (3 + sources),
        scratch_shapes=[
            pltpu.VMEM((everyone, lanes), f32),
            pltpu.VMEM((everyone, part), f32),
            pltpu.VMEM((everyone, part), f32),
        ],
        cost_estimate=cost(2 * everyone * one, 2 * one),
        compiler_params=params(room),
        name="hidden",
    )(packets, *known)
    arrived = [
        swap(partial, "expert", other) if other else partial
        for other, partial in zip(expert_order, partials)
    ]

    grad_gate, grad_up, done_in = pl.pallas_call(
        grad_in_kernel,
        out_shape=[struct((local_experts, part, hidden_units), f32)] * 2 + [dummy],
        in_specs=[VMEM] * 3,
        out_specs=[HBM] * 2 + [VMEM],
        scratch_shapes=[
            pltpu.VMEM((2, min(part, CHUNK), hidden_units), f32),
            pltpu.VMEM((2, min(part, CHUNK), hidden_units), f32),
            pltpu.SemaphoreType.DMA((2, 2)),
        ],
        cost_estimate=cost(2 * everyone * one // columns, 4 * one // columns),
        compiler_params=params(room),
        name="grad_in",
    )(x_part, d_gate, d_up)

    route_grad, *blocks, done_sum = pl.pallas_call(
        functools.partial(reduce_kernel, sources),
        out_shape=[struct(ids_t.shape, f32)] + [struct((rows, 2 * part), bf16)] * columns + [dummy],
        in_specs=[VMEM] * (sources + 2),
        out_specs=[VMEM] * (columns + 2),
        compiler_params=params(room),
        name="reduce",
    )(*arrived, ids_t, done_in)
    blocks = [
        swap(block, "dp", other) if other else block for other, block in enumerate(blocks)
    ]

    grad_down, done_out = pl.pallas_call(
        grad_out_kernel,
        out_shape=[struct((local_experts, hidden_units, part), f32), dummy],
        in_specs=[VMEM] * 3,
        out_specs=[HBM, VMEM],
        scratch_shapes=[
            pltpu.VMEM((everyone, part), bf16),
            pltpu.VMEM((2, hidden_units, part), f32),
            pltpu.SemaphoreType.DMA((2, 1)),
        ],
        cost_estimate=cost(everyone * one // columns, 2 * one // columns),
        compiler_params=params(room),
        name="grad_out",
    )(packets, hidden, done_sum)

    mixed, token_grad = pl.pallas_call(
        functools.partial(join_kernel, columns),
        out_shape=[struct((rows, width), bf16)] * 2,
        in_specs=[VMEM] * (columns + 1),
        out_specs=[VMEM] * 2,
        compiler_params=params(room),
        name="join",
    )(*blocks, done_out)
    return (mixed, token_grad, route_grad.T, grad_gate, grad_up, grad_down)


def solution(mesh):
    rows = P(("groups", "expert", "dp"), None)
    experts = P("expert", None, None)
    return jax.shard_map(
        per_device,
        mesh=mesh,
        in_specs=(rows, rows, rows, rows, experts, experts, experts, P("expert", None), rows),
        out_specs=(
            rows,
            rows,
            rows,
            P(("groups", "expert"), "dp", None),
            P(("groups", "expert"), "dp", None),
            P(("groups", "expert"), None, "dp"),
        ),
        check_vma=False,
    )
```

```python
import functools

import jax
import jax.numpy as jnp
from jax import lax
from jax.experimental import pallas as pl
from jax.experimental.pallas import tpu as pltpu
from jax.sharding import PartitionSpec as P

BLK = 128
LANES = 128
CHUNK = 256
TILE = 256
MIB = 1 << 20

VMEM = pl.BlockSpec(memory_space=pltpu.VMEM)
SMEM = pl.BlockSpec(memory_space=pltpu.SMEM)
HBM = pl.BlockSpec(memory_space=pltpu.HBM)

NN = (((1,), (0,)), ((), ()))
NT = (((1,), (1,)), ((), ()))


def dot(a, b, dims):
    return lax.dot_general(a, b, dims, preferred_element_type=jnp.float32)


def ids_along(shape, axis):
    return lax.broadcasted_iota(jnp.int32, shape, axis)


def aligned(index, size):
    return pl.ds(pl.multiple_of(index * size, size), size)


def route_kernel(
    tokens, cotangent, expert_ids, route_weights, own_tokens, packet, ids, values, sems
):
    rows, width = tokens.shape
    lanes = packet.shape[1] - width
    copies = [
        pltpu.make_async_copy(expert_ids, ids, sems.at[0]),
        pltpu.make_async_copy(route_weights, values, sems.at[1]),
        pltpu.make_async_copy(tokens, own_tokens, sems.at[2]),
        pltpu.make_async_copy(cotangent, packet.at[:, :width], sems.at[3]),
    ]
    for copy in copies:
        copy.start()
    for copy in copies:
        copy.wait()
    at = ids_along((lanes, rows), 0)
    weights = values[...].astype(jnp.float32)
    dense = jnp.zeros((lanes, rows), jnp.float32)
    for k in range(ids.shape[0]):
        dense += jnp.where(ids[k : k + 1, :] == at, weights[k : k + 1, :], 0.0)
    packet[:, width:] = dense.T.astype(packet.dtype)


def load_kernel(weight, value, same, *refs):
    targets, sems = refs[:-1], refs[-1]
    copies = [
        pltpu.make_async_copy(weight.at[i], target, sems.at[i]) for i, target in enumerate(targets)
    ]
    for copy in copies:
        copy.start()
    same[...] = value[...]
    for copy in copies:
        copy.wait()


def turn_kernel(x, after, x_part):
    x_part[...] = x[:, aligned(lax.axis_index("dp"), x_part.shape[0])].T


def over_tiles(tokens, body):
    if tokens == TILE:
        body(slice(0, TILE))
    else:

        def turn(tile, carry):
            body(aligned(tile, TILE))
            return carry

        lax.fori_loop(0, tokens // TILE, turn, 0)


def gate_up_kernel(first, last, *refs):
    count = last - first
    gates, ups, refs = refs[:count], refs[count : 2 * count], refs[2 * count :]
    x, masks, w_down, value = refs[:4]
    known, (same, sems) = refs[4:-2], refs[-2:]
    hidden_units = gates[0].shape[1]
    bf16 = jnp.bfloat16
    hiddens, slope_ups, slope_gates, gate_parts, up_parts, downs = [known[k::6] for k in range(6)]
    mine = aligned(lax.axis_index("dp"), gate_parts[0].shape[0])
    loads = []
    for i in range(count):
        loads += [
            pltpu.make_async_copy(w_down.at[first + i], downs[i], sems.at[3 * i]),
            pltpu.make_async_copy(gates[i].at[mine, :], gate_parts[i], sems.at[3 * i + 1]),
            pltpu.make_async_copy(ups[i].at[mine, :], up_parts[i], sems.at[3 * i + 2]),
        ]
    for load in loads:
        load.start()
    same[...] = value[...]

    def tile(rows):
        for i in range(count):
            for start in range(0, hidden_units, CHUNK):
                cols = slice(start, start + CHUNK)
                gate_pre = dot(x[rows, :], gates[i][:, cols], NN)
                up_proj = dot(x[rows, :], ups[i][:, cols], NN)
                at = ids_along((1, CHUNK), 1)
                keep = jnp.zeros((1, CHUNK), jnp.float32)
                for j in range(CHUNK // BLK):
                    kept = masks[first + i, start // BLK + j].astype(jnp.float32)
                    keep = jnp.where(at // BLK == j, kept, keep)
                sigma = 0.5 + 0.5 * jnp.tanh(0.5 * gate_pre)
                silu = gate_pre * sigma
                up_kept = up_proj * keep
                hiddens[i][rows, cols] = (silu * up_kept).astype(bf16)
                slope_ups[i][rows, cols] = (silu * keep).astype(bf16)
                slope = up_kept * (sigma + silu * (1.0 - sigma))
                slope_gates[i][rows, cols] = slope.astype(bf16)

    over_tiles(x.shape[0], tile)
    for load in loads:
        load.wait()


def hidden_kernel(local_experts, count, *refs):
    packet, refs = refs[0], refs[1:]
    known = [refs[i * 6 : i * 6 + 6] for i in range(local_experts)]
    refs = refs[6 * local_experts :]
    hidden, d_gate, d_up = refs[:3]
    outs, (inner, mixed, token_grad) = refs[3 : 3 + count], refs[3 + count :]
    hidden_units, width = known[0][5].shape
    tokens, part = mixed.shape
    lanes = packet.shape[1] - width
    half = lanes // 2
    base = lax.axis_index("expert") * local_experts
    mine = aligned(lax.axis_index("dp"), part)
    bf16, f32 = jnp.bfloat16, jnp.float32
    inner[...] = jnp.zeros(inner.shape, inner.dtype)
    mixed[...] = jnp.zeros(mixed.shape, mixed.dtype)
    token_grad[...] = jnp.zeros(token_grad.shape, token_grad.dtype)

    for expert in range(local_experts):

        def tile(rows, expert=expert):
            units, slope_up, slope_gate, gate, up, down = known[expert]
            dense = packet[rows, width:].astype(f32)
            at = ids_along((TILE, lanes), 1)
            hit = at == base + expert
            weights = jnp.sum(jnp.where(hit, dense, 0.0), axis=1, keepdims=True)
            total = jnp.zeros((TILE, 1), f32)
            for start in range(0, hidden_units, CHUNK):
                cols = slice(start, start + CHUNK)
                back = dot(packet[rows, :width], down[cols, :], NT)
                part_units = units[rows, cols].astype(f32)
                total += jnp.sum(part_units * back, axis=1, keepdims=True)
                back = back * weights
                new_gate = back * slope_gate[rows, cols].astype(f32)
                new_up = back * slope_up[rows, cols].astype(f32)
                hidden[expert, rows, cols] = (part_units * weights).astype(bf16)
                d_gate[expert, rows, cols] = new_gate.astype(bf16)
                d_up[expert, rows, cols] = new_up.astype(bf16)
            high = total.astype(bf16).astype(f32)
            inner[rows, :] += jnp.where(
                hit, high, jnp.where(at == base + expert + half, total - high, 0.0)
            )
            mixed[rows, :] += dot(hidden[expert, rows, :], down[:, mine], NN)
            token_grad[rows, :] += dot(d_gate[expert, rows, :], gate[...], NT) + dot(
                d_up[expert, rows, :], up[...], NT
            )

        over_tiles(tokens, tile)

    rows = outs[0].shape[0]
    for i, out in enumerate(outs):
        block = slice(i * rows, (i + 1) * rows)
        out[:, :part] = mixed[block].astype(bf16)
        out[:, part : 2 * part] = token_grad[block].astype(bf16)
        out[:, 2 * part :] = inner[block].astype(bf16)


def write_out(steps, place, outs, bufs, sems, body):
    def copies(step, slot):
        return [
            pltpu.make_async_copy(buf.at[slot], out.at[place(step)], sems.at[slot, i])
            for i, (out, buf) in enumerate(zip(outs, bufs))
        ]

    def turn(step, carry):
        slot = lax.rem(step, 2)

        @pl.when(step >= 2)
        def _():
            for copy in copies(step - 2, slot):
                copy.wait()

        body(step, slot)
        for copy in copies(step, slot):
            copy.start()
        return carry

    lax.fori_loop(0, steps, turn, 0)
    for step in range(max(steps - 2, 0), steps):
        for copy in copies(step, step % 2):
            copy.wait()


def grad_in_kernel(x_part, d_gate, d_up, grad_gate, grad_up, done, out_gate, out_up, sems):
    local_experts = d_gate.shape[0]
    part, rows = x_part.shape[0], out_gate.shape[1]
    done[...] = jnp.zeros(done.shape, done.dtype)
    blocks = part // rows

    def place(step):
        return step // blocks, aligned(lax.rem(step, blocks), rows), slice(None)

    def body(step, slot):
        expert, block, _ = place(step)
        out_gate[slot] = dot(x_part[block, :], d_gate[expert], NN)
        out_up[slot] = dot(x_part[block, :], d_up[expert], NN)

    write_out(
        local_experts * blocks, place, (grad_gate, grad_up), (out_gate, out_up), sems, body
    )


def grad_out_kernel(packet, hidden, after, grad_down, done, cot_part, out_down, sems):
    local_experts = hidden.shape[0]
    part = cot_part.shape[1]
    cot_part[...] = packet[:, aligned(lax.axis_index("dp"), part)]
    done[...] = jnp.zeros(done.shape, done.dtype)

    def place(step):
        return (step,)

    def body(step, slot):
        out_down[slot] = dot(hidden[step].T, cot_part[...], NN)

    write_out(local_experts, place, (grad_down,), (out_down,), sems, body)


def reduce_kernel(count, *refs):
    blocks, refs = refs[:count], refs[count:]
    expert_ids, after, route_grad = refs[:3]
    outs, done = refs[3:-1], refs[-1]
    done[...] = jnp.zeros(done.shape, done.dtype)
    rows, both = outs[0].shape
    half = (blocks[0].shape[1] - both) // 2
    for j, out in enumerate(outs):
        total = jnp.zeros((rows, both), jnp.float32)
        for block in blocks:
            total += block[j * rows : (j + 1) * rows, :both].astype(jnp.float32)
        out[...] = total.astype(out.dtype)
    inner = jnp.zeros((rows, 2 * half), jnp.float32)
    for block in blocks:
        inner += block[:rows, both:].astype(jnp.float32)
    inner = inner.T
    inner = inner[:half] + inner[half:]
    at = ids_along(inner.shape, 0)
    for k in range(expert_ids.shape[0]):
        hit = jnp.where(expert_ids[k : k + 1, :] == at, inner, 0.0)
        route_grad[k : k + 1, :] = jnp.sum(hit, axis=0, keepdims=True)


def join_kernel(count, *refs):
    blocks, (after, mixed, token_grad) = refs[:count], refs[count:]
    part = blocks[0].shape[1] // 2
    column = lax.axis_index("dp")
    for other, block in enumerate(blocks):
        cols = aligned(column ^ other, part)
        mixed[:, cols] = block[:, :part]
        token_grad[:, cols] = block[:, part:]


def swap(value, axis, mask):
    size = lax.axis_size(axis)
    return lax.ppermute(value, axis, [(i, i ^ mask) for i in range(size)])


def exchange(value, axis, masks):
    return [swap(value, axis, mask) for mask in masks]


def in_hbm(array):
    return pltpu.with_memory_space_constraint(array, pltpu.HBM)


def in_vmem(array):
    return pltpu.with_memory_space_constraint(array, pltpu.VMEM)


def cost(flops, moved):
    return pl.CostEstimate(flops=flops, bytes_accessed=moved, transcendentals=0)


def params(mib):
    return pltpu.CompilerParams(vmem_limit_bytes=mib * MIB)


def per_device(
    tokens, expert_ids, slot_index, route_weights, w_gate, w_up, w_down, block_masks, cotangent
):
    rows, width = tokens.shape
    local_experts, _, hidden_units = w_gate.shape
    sources, columns = lax.axis_size("expert"), lax.axis_size("dp")
    chips = list(range(2, sources, 2))
    expert_order = [0] + chips + [chip ^ 1 for chip in [0] + chips]
    lanes = -(-2 * local_experts * sources // LANES) * LANES
    part = width // columns
    everyone = sources * columns * rows
    bf16, f32 = jnp.bfloat16, jnp.float32
    struct = jax.ShapeDtypeStruct
    one = 2 * local_experts * width * hidden_units
    room = 8 + (everyone - TILE) * (2 * part + lanes) * 10 // MIB
    dummy = struct((8, LANES), f32)
    ids_t = expert_ids.T
    w_gate, w_up, w_down = [in_hbm(w) for w in (w_gate, w_up, w_down)]

    own_tokens, packet = pl.pallas_call(
        route_kernel,
        out_shape=[struct(tokens.shape, bf16), struct((rows, width + lanes), bf16)],
        in_specs=[HBM] * 4,
        out_specs=[VMEM] * 2,
        scratch_shapes=[
            pltpu.VMEM(ids_t.shape, jnp.int32),
            pltpu.VMEM(ids_t.shape, bf16),
            pltpu.SemaphoreType.DMA((4,)),
        ],
        compiler_params=params(room),
        name="route",
    )(*[in_hbm(a) for a in (tokens, cotangent, ids_t, route_weights.T)])

    def load(weight, value, name):
        same, *loaded = pl.pallas_call(
            load_kernel,
            out_shape=[struct(value.shape, bf16)]
            + [pltpu.VMEM(weight.shape[1:], bf16)] * local_experts,
            in_specs=[HBM, VMEM],
            out_specs=[VMEM] * (1 + local_experts),
            scratch_shapes=[pltpu.SemaphoreType.DMA((local_experts,))],
            cost_estimate=cost(0, one),
            compiler_params=params(room),
            name=name,
        )(weight, value)
        return [in_vmem(array) for array in loaded], same

    tokens_near = exchange(tokens, "dp", range(1, columns))
    c_column = jnp.concatenate([packet] + exchange(packet, "dp", range(1, columns)))
    ups, own_tokens = load(w_up, own_tokens, "load_up")
    x_column = jnp.concatenate([own_tokens] + tokens_near)
    x_across = exchange(x_column, "expert", chips)
    c_across = exchange(c_column, "expert", chips)
    gates, x_column = load(w_gate, x_column, "load_gate")
    x = jnp.concatenate([x_column] + x_across)
    x = jnp.concatenate([x, swap(x, "expert", 1)])

    def gate_up(first, last, value):
        count = last - first
        one_expert = [struct((everyone, hidden_units), bf16)] * 3
        one_expert += [pltpu.VMEM((part, hidden_units), bf16)] * 2
        one_expert += [pltpu.VMEM(w_down.shape[1:], bf16)]
        *known, same = pl.pallas_call(
            functools.partial(gate_up_kernel, first, last),
            out_shape=one_expert * count + [struct(value.shape, value.dtype)],
            in_specs=[VMEM] * (2 * count + 1) + [SMEM, HBM, VMEM],
            out_specs=[VMEM] * (6 * count + 1),
            scratch_shapes=[pltpu.SemaphoreType.DMA((3 * count,))],
            cost_estimate=cost(
                2 * everyone * one * count // local_experts, 2 * one * count // local_experts
            ),
            compiler_params=params(room),
            name="gate_up",
        )(*gates[first:last], *ups[first:last], x, block_masks, w_down, value)
        return [in_vmem(a) if i % 6 >= 3 else a for i, a in enumerate(known)], same

    middle = local_experts // 2
    known, c_column = gate_up(0, middle or local_experts, c_column)
    if middle:
        more, _ = gate_up(middle, local_experts, c_column)
        known = known + more
    c_half = jnp.concatenate([c_column] + c_across)
    packets = jnp.concatenate([c_half, swap(c_half, "expert", 1)])
    x_part = pl.pallas_call(
        turn_kernel,
        out_shape=struct((part, everyone), bf16),
        in_specs=[VMEM] * 2,
        out_specs=VMEM,
        compiler_params=params(room),
        name="turn",
    )(x, c_half)

    units = struct((local_experts, everyone, hidden_units), bf16)
    hidden, d_gate, d_up, *partials = pl.pallas_call(
        functools.partial(hidden_kernel, local_experts, sources),
        out_shape=[units] * 3
        + [struct((columns * rows, 2 * part + lanes), bf16)] * sources,
        in_specs=[VMEM] * (1 + len(known)),
        out_specs=[VMEM] * (3 + sources),
        scratch_shapes=[
            pltpu.VMEM((everyone, lanes), f32),
            pltpu.VMEM((everyone, part), f32),
            pltpu.VMEM((everyone, part), f32),
        ],
        cost_estimate=cost(2 * everyone * one, 2 * one),
        compiler_params=params(room),
        name="hidden",
    )(packets, *known)
    arrived = [
        swap(partial, "expert", other) if other else partial
        for other, partial in zip(expert_order, partials)
    ]

    grad_gate, grad_up, done_in = pl.pallas_call(
        grad_in_kernel,
        out_shape=[struct((local_experts, part, hidden_units), f32)] * 2 + [dummy],
        in_specs=[VMEM] * 3,
        out_specs=[HBM] * 2 + [VMEM],
        scratch_shapes=[
            pltpu.VMEM((2, min(part, CHUNK), hidden_units), f32),
            pltpu.VMEM((2, min(part, CHUNK), hidden_units), f32),
            pltpu.SemaphoreType.DMA((2, 2)),
        ],
        cost_estimate=cost(2 * everyone * one // columns, 4 * one // columns),
        compiler_params=params(room),
        name="grad_in",
    )(x_part, d_gate, d_up)

    route_grad, *blocks, done_sum = pl.pallas_call(
        functools.partial(reduce_kernel, sources),
        out_shape=[struct(ids_t.shape, f32)] + [struct((rows, 2 * part), bf16)] * columns + [dummy],
        in_specs=[VMEM] * (sources + 2),
        out_specs=[VMEM] * (columns + 2),
        compiler_params=params(room),
        name="reduce",
    )(*arrived, ids_t, done_in)
    blocks = [
        swap(block, "dp", other) if other else block for other, block in enumerate(blocks)
    ]

    grad_down, done_out = pl.pallas_call(
        grad_out_kernel,
        out_shape=[struct((local_experts, hidden_units, part), f32), dummy],
        in_specs=[VMEM] * 3,
        out_specs=[HBM, VMEM],
        scratch_shapes=[
            pltpu.VMEM((everyone, part), bf16),
            pltpu.VMEM((2, hidden_units, part), f32),
            pltpu.SemaphoreType.DMA((2, 1)),
        ],
        cost_estimate=cost(everyone * one // columns, 2 * one // columns),
        compiler_params=params(room),
        name="grad_out",
    )(packets, hidden, done_sum)

    mixed, token_grad = pl.pallas_call(
        functools.partial(join_kernel, columns),
        out_shape=[struct((rows, width), bf16)] * 2,
        in_specs=[VMEM] * (columns + 1),
        out_specs=[VMEM] * 2,
        compiler_params=params(room),
        name="join",
    )(*blocks, done_out)
    return (mixed, token_grad, route_grad.T, grad_gate, grad_up, grad_down)


def solution(mesh):
    rows = P(("groups", "expert", "dp"), None)
    experts = P("expert", None, None)
    return jax.shard_map(
        per_device,
        mesh=mesh,
        in_specs=(rows, rows, rows, rows, experts, experts, experts, P("expert", None), rows),
        out_specs=(
            rows,
            rows,
            rows,
            P(("groups", "expert"), "dp", None),
            P(("groups", "expert"), "dp", None),
            P(("groups", "expert"), None, "dp"),
        ),
        check_vma=False,
    )
```

```python
import functools

import jax
import jax.numpy as jnp
from jax import lax
from jax.experimental import pallas as pl
from jax.experimental.pallas import tpu as pltpu
from jax.sharding import PartitionSpec as P

BLK = 128
LANES = 128
CHUNK = 256
TILE = 256
MIB = 1 << 20

VMEM = pl.BlockSpec(memory_space=pltpu.VMEM)
SMEM = pl.BlockSpec(memory_space=pltpu.SMEM)
HBM = pl.BlockSpec(memory_space=pltpu.HBM)

NN = (((1,), (0,)), ((), ()))
NT = (((1,), (1,)), ((), ()))


def dot(a, b, dims):
    return lax.dot_general(a, b, dims, preferred_element_type=jnp.float32)


def ids_along(shape, axis):
    return lax.broadcasted_iota(jnp.int32, shape, axis)


def aligned(index, size):
    return pl.ds(pl.multiple_of(index * size, size), size)


def route_kernel(
    tokens, cotangent, expert_ids, route_weights, own_tokens, packet, ids, values, sems
):
    rows, width = tokens.shape
    lanes = packet.shape[1] - width
    copies = [
        pltpu.make_async_copy(expert_ids, ids, sems.at[0]),
        pltpu.make_async_copy(route_weights, values, sems.at[1]),
        pltpu.make_async_copy(tokens, own_tokens, sems.at[2]),
        pltpu.make_async_copy(cotangent, packet.at[:, :width], sems.at[3]),
    ]
    for copy in copies:
        copy.start()
    for copy in copies:
        copy.wait()
    at = ids_along((lanes, rows), 0)
    weights = values[...].astype(jnp.float32)
    dense = jnp.zeros((lanes, rows), jnp.float32)
    for k in range(ids.shape[0]):
        dense += jnp.where(ids[k : k + 1, :] == at, weights[k : k + 1, :], 0.0)
    packet[:, width:] = dense.T.astype(packet.dtype)


def load_kernel(weight, value, same, *refs):
    targets, sems = refs[:-1], refs[-1]
    copies = [
        pltpu.make_async_copy(weight.at[i], target, sems.at[i]) for i, target in enumerate(targets)
    ]
    for copy in copies:
        copy.start()
    same[...] = value[...]
    for copy in copies:
        copy.wait()


def turn_kernel(x, after, w_gate, w_up, x_part, gate_part, up_part, sems):
    mine = aligned(lax.axis_index("dp"), x_part.shape[0])
    loads = [
        pltpu.make_async_copy(w_gate.at[:, mine, :], gate_part, sems.at[0]),
        pltpu.make_async_copy(w_up.at[:, mine, :], up_part, sems.at[1]),
    ]
    for load in loads:
        load.start()
    x_part[...] = x[:, mine].T
    for load in loads:
        load.wait()


def over_tiles(tokens, body):
    if tokens == TILE:
        body(slice(0, TILE))
    else:

        def turn(tile, carry):
            body(aligned(tile, TILE))
            return carry

        lax.fori_loop(0, tokens // TILE, turn, 0)


def gate_up_kernel(count, *refs):
    gates, ups, refs = refs[:count], refs[count : 2 * count], refs[2 * count :]
    x, masks, w_down, value = refs[:4]
    known, downs, (same, sems) = refs[4 : 4 + 3 * count], refs[4 + 3 * count : -2], refs[-2:]
    hidden_units = gates[0].shape[1]
    bf16 = jnp.bfloat16
    hiddens, slope_ups, slope_gates = [known[k::3] for k in range(3)]
    loads = [
        pltpu.make_async_copy(w_down.at[i], down, sems.at[i]) for i, down in enumerate(downs)
    ]
    for load in loads:
        load.start()
    same[...] = value[...]

    def tile(rows):
        for i in range(count):
            for start in range(0, hidden_units, CHUNK):
                cols = slice(start, start + CHUNK)
                gate_pre = dot(x[rows, :], gates[i][:, cols], NN)
                up_proj = dot(x[rows, :], ups[i][:, cols], NN)
                at = ids_along((1, CHUNK), 1)
                keep = jnp.zeros((1, CHUNK), jnp.float32)
                for j in range(CHUNK // BLK):
                    kept = masks[i, start // BLK + j].astype(jnp.float32)
                    keep = jnp.where(at // BLK == j, kept, keep)
                sigma = 0.5 + 0.5 * jnp.tanh(0.5 * gate_pre)
                silu = gate_pre * sigma
                up_kept = up_proj * keep
                hiddens[i][rows, cols] = (silu * up_kept).astype(bf16)
                slope_ups[i][rows, cols] = (silu * keep).astype(bf16)
                slope = up_kept * (sigma + silu * (1.0 - sigma))
                slope_gates[i][rows, cols] = slope.astype(bf16)

    over_tiles(x.shape[0], tile)
    for load in loads:
        load.wait()


def hidden_kernel(local_experts, middle, count, *refs):
    packet, refs = refs[0], refs[1:]
    gate, up, refs = refs[0], refs[1], refs[2:]
    known = [refs[i * 3 : i * 3 + 3] for i in range(local_experts)]
    refs = refs[3 * local_experts :]
    downs, w_down, refs = refs[:middle], refs[middle], refs[middle + 1 :]
    hidden, d_gate, d_up = refs[:3]
    outs, (inner, mixed, token_grad, down_buf, sems) = refs[3 : 3 + count], refs[3 + count :]
    hidden_units, width = downs[0].shape
    loads = [
        pltpu.make_async_copy(w_down.at[i], down_buf.at[i - middle], sems.at[i - middle])
        for i in range(middle, local_experts)
    ]
    for load in loads:
        load.start()
    tokens, part = mixed.shape
    lanes = packet.shape[1] - width
    half = lanes // 2
    base = lax.axis_index("expert") * local_experts
    mine = aligned(lax.axis_index("dp"), part)
    bf16, f32 = jnp.bfloat16, jnp.float32
    inner[...] = jnp.zeros(inner.shape, inner.dtype)
    mixed[...] = jnp.zeros(mixed.shape, mixed.dtype)
    token_grad[...] = jnp.zeros(token_grad.shape, token_grad.dtype)

    for expert in range(local_experts):
        if expert == middle:
            for load in loads:
                load.wait()

        def tile(rows, expert=expert):
            units, slope_up, slope_gate = known[expert]
            down = downs[expert] if expert < middle else down_buf.at[expert - middle]
            dense = packet[rows, width:].astype(f32)
            at = ids_along((TILE, lanes), 1)
            hit = at == base + expert
            weights = jnp.sum(jnp.where(hit, dense, 0.0), axis=1, keepdims=True)
            total = jnp.zeros((TILE, 1), f32)
            for start in range(0, hidden_units, CHUNK):
                cols = slice(start, start + CHUNK)
                back = dot(packet[rows, :width], down[cols, :], NT)
                part_units = units[rows, cols].astype(f32)
                total += jnp.sum(part_units * back, axis=1, keepdims=True)
                back = back * weights
                new_gate = back * slope_gate[rows, cols].astype(f32)
                new_up = back * slope_up[rows, cols].astype(f32)
                hidden[expert, rows, cols] = (part_units * weights).astype(bf16)
                d_gate[expert, rows, cols] = new_gate.astype(bf16)
                d_up[expert, rows, cols] = new_up.astype(bf16)
            high = total.astype(bf16).astype(f32)
            inner[rows, :] += jnp.where(
                hit, high, jnp.where(at == base + expert + half, total - high, 0.0)
            )
            mixed[rows, :] += dot(hidden[expert, rows, :], down[:, mine], NN)
            token_grad[rows, :] += dot(d_gate[expert, rows, :], gate[expert], NT) + dot(
                d_up[expert, rows, :], up[expert], NT
            )

        over_tiles(tokens, tile)

    rows = outs[0].shape[0]
    for i, out in enumerate(outs):
        block = slice(i * rows, (i + 1) * rows)
        out[:, :part] = mixed[block].astype(bf16)
        out[:, part : 2 * part] = token_grad[block].astype(bf16)
        out[:, 2 * part :] = inner[block].astype(bf16)


def write_out(steps, place, outs, bufs, sems, body):
    def copies(step, slot):
        return [
            pltpu.make_async_copy(buf.at[slot], out.at[place(step)], sems.at[slot, i])
            for i, (out, buf) in enumerate(zip(outs, bufs))
        ]

    def turn(step, carry):
        slot = lax.rem(step, 2)

        @pl.when(step >= 2)
        def _():
            for copy in copies(step - 2, slot):
                copy.wait()

        body(step, slot)
        for copy in copies(step, slot):
            copy.start()
        return carry

    lax.fori_loop(0, steps, turn, 0)
    for step in range(max(steps - 2, 0), steps):
        for copy in copies(step, step % 2):
            copy.wait()


def grad_in_kernel(x_part, d_gate, d_up, grad_gate, grad_up, done, out_gate, out_up, sems):
    local_experts = d_gate.shape[0]
    part, rows = x_part.shape[0], out_gate.shape[1]
    done[...] = jnp.zeros(done.shape, done.dtype)
    blocks = part // rows

    def place(step):
        return step // blocks, aligned(lax.rem(step, blocks), rows), slice(None)

    def body(step, slot):
        expert, block, _ = place(step)
        out_gate[slot] = dot(x_part[block, :], d_gate[expert], NN)
        out_up[slot] = dot(x_part[block, :], d_up[expert], NN)

    write_out(
        local_experts * blocks, place, (grad_gate, grad_up), (out_gate, out_up), sems, body
    )


def grad_out_kernel(first, last, packet, hidden, after, value, *refs):
    grad_down, done, same, cot_part, out_down, sems = refs[-6:]
    same[...] = value[...]
    part = cot_part.shape[1]
    cot_part[...] = packet[:, aligned(lax.axis_index("dp"), part)]
    done[...] = jnp.zeros(done.shape, done.dtype)

    def place(step):
        return (first + step,)

    def body(step, slot):
        out_down[slot] = dot(hidden[first + step].T, cot_part[...], NN)

    write_out(last - first, place, (grad_down,), (out_down,), sems, body)


def reduce_kernel(count, *refs):
    blocks, refs = refs[:count], refs[count:]
    expert_ids, after, route_grad = refs[:3]
    outs, done = refs[3:-1], refs[-1]
    done[...] = jnp.zeros(done.shape, done.dtype)
    rows, both = outs[0].shape
    half = (blocks[0].shape[1] - both) // 2
    for j, out in enumerate(outs):
        total = jnp.zeros((rows, both), jnp.float32)
        for block in blocks:
            total += block[j * rows : (j + 1) * rows, :both].astype(jnp.float32)
        out[...] = total.astype(out.dtype)
    inner = jnp.zeros((rows, 2 * half), jnp.float32)
    for block in blocks:
        inner += block[:rows, both:].astype(jnp.float32)
    inner = inner.T
    inner = inner[:half] + inner[half:]
    at = ids_along(inner.shape, 0)
    for k in range(expert_ids.shape[0]):
        hit = jnp.where(expert_ids[k : k + 1, :] == at, inner, 0.0)
        route_grad[k : k + 1, :] = jnp.sum(hit, axis=0, keepdims=True)


def join_kernel(count, *refs):
    blocks, (after, mixed, token_grad) = refs[:count], refs[count:]
    part = blocks[0].shape[1] // 2
    column = lax.axis_index("dp")
    for other, block in enumerate(blocks):
        cols = aligned(column ^ other, part)
        mixed[:, cols] = block[:, :part]
        token_grad[:, cols] = block[:, part:]


def swap(value, axis, mask):
    size = lax.axis_size(axis)
    return lax.ppermute(value, axis, [(i, i ^ mask) for i in range(size)])


def exchange(value, axis, masks):
    return [swap(value, axis, mask) for mask in masks]


def in_hbm(array):
    return pltpu.with_memory_space_constraint(array, pltpu.HBM)


def in_vmem(array):
    return pltpu.with_memory_space_constraint(array, pltpu.VMEM)


def doubling(size):
    masks = [1 << bit for bit in reversed(range(size.bit_length() - 1))]
    order = [0]
    for mask in masks:
        order = order + [other ^ mask for other in order]
    return masks, order


def pass_on(held, axis, masks):
    for mask in masks:
        names = sorted(name for name in held if name[0] & mask)
        rows = held[names[0]].shape[0]
        sent = swap(jnp.concatenate([held.pop(name) for name in names]), axis, mask)
        for i, (to, source) in enumerate(names):
            held[to ^ mask, source ^ mask] = sent[i * rows : (i + 1) * rows]
    return held


def cost(flops, moved):
    return pl.CostEstimate(flops=flops, bytes_accessed=moved, transcendentals=0)


def params(mib):
    return pltpu.CompilerParams(vmem_limit_bytes=mib * MIB)


def per_device(
    tokens, expert_ids, slot_index, route_weights, w_gate, w_up, w_down, block_masks, cotangent
):
    rows, width = tokens.shape
    local_experts, _, hidden_units = w_gate.shape
    sources, columns = lax.axis_size("expert"), lax.axis_size("dp")
    chips = list(range(2, sources, 2))
    expert_order = [0] + chips + [chip ^ 1 for chip in [0] + chips]
    lanes = -(-2 * local_experts * sources // LANES) * LANES
    part = width // columns
    everyone = sources * columns * rows
    bf16, f32 = jnp.bfloat16, jnp.float32
    struct = jax.ShapeDtypeStruct
    one = 2 * local_experts * width * hidden_units
    room = 12 + (everyone - TILE) * (2 * part + lanes) * 10 // MIB
    dummy = struct((8, LANES), f32)
    ids_t = expert_ids.T
    w_gate, w_up, w_down = [in_hbm(w) for w in (w_gate, w_up, w_down)]

    own_tokens, packet = pl.pallas_call(
        route_kernel,
        out_shape=[struct(tokens.shape, bf16), struct((rows, width + lanes), bf16)],
        in_specs=[HBM] * 4,
        out_specs=[VMEM] * 2,
        scratch_shapes=[
            pltpu.VMEM(ids_t.shape, jnp.int32),
            pltpu.VMEM(ids_t.shape, bf16),
            pltpu.SemaphoreType.DMA((4,)),
        ],
        compiler_params=params(room),
        name="route",
    )(*[in_hbm(a) for a in (tokens, cotangent, ids_t, route_weights.T)])

    def load(weight, value, name):
        same, *loaded = pl.pallas_call(
            load_kernel,
            out_shape=[struct(value.shape, bf16)]
            + [pltpu.VMEM(weight.shape[1:], bf16)] * local_experts,
            in_specs=[HBM, VMEM],
            out_specs=[VMEM] * (1 + local_experts),
            scratch_shapes=[pltpu.SemaphoreType.DMA((local_experts,))],
            cost_estimate=cost(0, one),
            compiler_params=params(room),
            name=name,
        )(weight, value)
        return [in_vmem(array) for array in loaded], same

    masks, order = doubling(columns)
    tokens_near = exchange(tokens, "dp", order[1:])
    c_column = packet
    for mask in masks:
        c_column = jnp.concatenate([c_column, swap(c_column, "dp", mask)])
    ups, own_tokens = load(w_up, own_tokens, "load_up")
    x_column = jnp.concatenate([own_tokens] + tokens_near)
    x_across = exchange(x_column, "expert", chips)
    c_across = exchange(c_column, "expert", chips)
    gates, x_column = load(w_gate, x_column, "load_gate")
    x = jnp.concatenate([x_column] + x_across)
    x = jnp.concatenate([x, swap(x, "expert", 1)])

    middle = max(local_experts // 2, 1)
    *known, c_column = pl.pallas_call(
        functools.partial(gate_up_kernel, local_experts),
        out_shape=[struct((everyone, hidden_units), bf16)] * (3 * local_experts)
        + [pltpu.VMEM(w_down.shape[1:], bf16)] * middle
        + [struct(c_column.shape, bf16)],
        in_specs=[VMEM] * (2 * local_experts + 1) + [SMEM, HBM, VMEM],
        out_specs=[VMEM] * (3 * local_experts + middle + 1),
        scratch_shapes=[pltpu.SemaphoreType.DMA((middle,))],
        cost_estimate=cost(2 * everyone * one, 2 * one),
        compiler_params=params(room),
        name="gate_up",
    )(*gates, *ups, x, block_masks, w_down, c_column)
    known, downs = known[: 3 * local_experts], known[3 * local_experts :]
    downs = [in_vmem(down) for down in downs]
    c_half = jnp.concatenate([c_column] + c_across)
    packets = jnp.concatenate([c_half, swap(c_half, "expert", 1)])
    x_part, *parts = pl.pallas_call(
        turn_kernel,
        out_shape=[struct((part, everyone), bf16)]
        + [pltpu.VMEM((local_experts, part, hidden_units), bf16)] * 2,
        in_specs=[VMEM] * 2 + [HBM] * 2,
        out_specs=[VMEM] * 3,
        scratch_shapes=[pltpu.SemaphoreType.DMA((2,))],
        compiler_params=params(room),
        name="turn",
    )(x, c_half, w_gate, w_up)
    parts = [in_vmem(array) for array in parts]

    units = struct((local_experts, everyone, hidden_units), bf16)
    hidden, d_gate, d_up, *partials = pl.pallas_call(
        functools.partial(hidden_kernel, local_experts, middle, sources),
        out_shape=[units] * 3
        + [struct((columns * rows, 2 * part + lanes), bf16)] * sources,
        in_specs=[VMEM] * (3 + len(known) + middle) + [HBM],
        out_specs=[VMEM] * (3 + sources),
        scratch_shapes=[
            pltpu.VMEM((everyone, lanes), f32),
            pltpu.VMEM((everyone, part), f32),
            pltpu.VMEM((everyone, part), f32),
            pltpu.VMEM((max(local_experts - middle, 1),) + w_down.shape[1:], bf16),
            pltpu.SemaphoreType.DMA((max(local_experts - middle, 1),)),
        ],
        cost_estimate=cost(2 * everyone * one, 2 * one),
        compiler_params=params(room),
        name="hidden",
    )(packets, *parts, *known, *downs, w_down)
    arrived = [
        swap(partial, "expert", other) if other else partial
        for other, partial in zip(expert_order, partials)
    ]

    grad_gate, grad_up, done_in = pl.pallas_call(
        grad_in_kernel,
        out_shape=[struct((local_experts, part, hidden_units), f32)] * 2 + [dummy],
        in_specs=[VMEM] * 3,
        out_specs=[HBM] * 2 + [VMEM],
        scratch_shapes=[
            pltpu.VMEM((2, min(part, CHUNK), hidden_units), f32),
            pltpu.VMEM((2, min(part, CHUNK), hidden_units), f32),
            pltpu.SemaphoreType.DMA((2, 2)),
        ],
        cost_estimate=cost(2 * everyone * one // columns, 4 * one // columns),
        compiler_params=params(room),
        name="grad_in",
    )(x_part, d_gate, d_up)

    route_grad, *blocks, done_sum = pl.pallas_call(
        functools.partial(reduce_kernel, sources),
        out_shape=[struct(ids_t.shape, f32)] + [struct((rows, 2 * part), bf16)] * columns + [dummy],
        in_specs=[VMEM] * (sources + 2),
        out_specs=[VMEM] * (columns + 2),
        compiler_params=params(room),
        name="reduce",
    )(*arrived, ids_t, done_in)
    held = pass_on({(to, 0): block for to, block in zip(order, blocks)}, "dp", masks[:1])

    def grad_out(first, last, value, after, known):
        return pl.pallas_call(
            functools.partial(grad_out_kernel, first, last),
            out_shape=[
                struct((local_experts, hidden_units, part), f32),
                dummy,
                struct(value.shape, value.dtype),
            ],
            in_specs=[VMEM] * 4 + [HBM] * len(known),
            out_specs=[HBM, VMEM, VMEM],
            scratch_shapes=[
                pltpu.VMEM((everyone, part), bf16),
                pltpu.VMEM((2, hidden_units, part), f32),
                pltpu.SemaphoreType.DMA((2, 1)),
            ],
            input_output_aliases={4: 0} if known else {},
            cost_estimate=cost(
                everyone * one // columns * (last - first) // local_experts,
                2 * one // columns * (last - first) // local_experts,
            ),
            compiler_params=params(room),
            name="grad_out",
        )(packets, hidden, after, value, *known)

    later = (masks[-1], 0)
    grad_down, done_out, held[later] = grad_out(0, middle, held[later], done_sum, [])
    held = pass_on(held, "dp", masks[1:])
    if middle < local_experts:
        grad_down, done_out, _ = grad_out(middle, local_experts, done_out, done_out, [grad_down])
    blocks = [held[0, other] for other in range(columns)]

    mixed, token_grad = pl.pallas_call(
        functools.partial(join_kernel, columns),
        out_shape=[struct((rows, width), bf16)] * 2,
        in_specs=[VMEM] * (columns + 1),
        out_specs=[VMEM] * 2,
        compiler_params=params(room),
        name="join",
    )(*blocks, done_out)
    return (mixed, token_grad, route_grad.T, grad_gate, grad_up, grad_down)


def solution(mesh):
    rows = P(("groups", "expert", "dp"), None)
    experts = P("expert", None, None)
    return jax.shard_map(
        per_device,
        mesh=mesh,
        in_specs=(rows, rows, rows, rows, experts, experts, experts, P("expert", None), rows),
        out_specs=(
            rows,
            rows,
            rows,
            P(("groups", "expert"), "dp", None),
            P(("groups", "expert"), "dp", None),
            P(("groups", "expert"), None, "dp"),
        ),
        check_vma=False,
    )
```

```python
import functools

import jax
import jax.numpy as jnp
from jax import lax
from jax.experimental import pallas as pl
from jax.experimental.pallas import tpu as pltpu
from jax.sharding import PartitionSpec as P

BLK = 128
LANES = 128
CHUNK = 256
TILE = 256
MIB = 1 << 20

VMEM = pl.BlockSpec(memory_space=pltpu.VMEM)
SMEM = pl.BlockSpec(memory_space=pltpu.SMEM)
HBM = pl.BlockSpec(memory_space=pltpu.HBM)

NN = (((1,), (0,)), ((), ()))
NT = (((1,), (1,)), ((), ()))


def dot(a, b, dims):
    return lax.dot_general(a, b, dims, preferred_element_type=jnp.float32)


def ids_along(shape, axis):
    return lax.broadcasted_iota(jnp.int32, shape, axis)


def aligned(index, size):
    return pl.ds(pl.multiple_of(index * size, size), size)


def route_kernel(
    tokens, cotangent, expert_ids, route_weights, own_tokens, packet, ids, values, sems
):
    rows, width = tokens.shape
    lanes = packet.shape[1] - width
    copies = [
        pltpu.make_async_copy(expert_ids, ids, sems.at[0]),
        pltpu.make_async_copy(route_weights, values, sems.at[1]),
        pltpu.make_async_copy(tokens, own_tokens, sems.at[2]),
        pltpu.make_async_copy(cotangent, packet.at[:, :width], sems.at[3]),
    ]
    for copy in copies:
        copy.start()
    for copy in copies:
        copy.wait()
    at = ids_along((lanes, rows), 0)
    weights = values[...].astype(jnp.float32)
    dense = jnp.zeros((lanes, rows), jnp.float32)
    for k in range(ids.shape[0]):
        dense += jnp.where(ids[k : k + 1, :] == at, weights[k : k + 1, :], 0.0)
    packet[:, width:] = dense.T.astype(packet.dtype)


def load_kernel(weight, value, same, *refs):
    targets, sems = refs[:-1], refs[-1]
    copies = [
        pltpu.make_async_copy(weight.at[i], target, sems.at[i]) for i, target in enumerate(targets)
    ]
    for copy in copies:
        copy.start()
    same[...] = value[...]
    for copy in copies:
        copy.wait()


def turn_kernel(x, after, x_part):
    x_part[...] = x[:, aligned(lax.axis_index("dp"), x_part.shape[0])].T


def over_tiles(tokens, body):
    if tokens == TILE:
        body(slice(0, TILE))
    else:

        def turn(tile, carry):
            body(aligned(tile, TILE))
            return carry

        lax.fori_loop(0, tokens // TILE, turn, 0)


def load_slices(weights, targets, sems):
    mine = aligned(lax.axis_index("dp"), targets[0].shape[0])
    copies = [
        pltpu.make_async_copy(weight.at[mine, :], target, sems.at[i])
        for i, (weight, target) in enumerate(zip(weights, targets))
    ]
    for copy in copies:
        copy.start()
    return copies


def load_downs(w_down, targets, first, sems):
    copies = [
        pltpu.make_async_copy(w_down.at[first + i], target, sems.at[i])
        for i, target in enumerate(targets)
    ]
    for copy in copies:
        copy.start()
    return copies


def gate_kernel(count, *refs):
    gates, x, w_down, refs = refs[:count], refs[count], refs[count + 1], refs[count + 2 :]
    products, parts, downs = refs[:count], refs[count : 2 * count], refs[2 * count : -2]
    loads = load_downs(w_down, downs, 0, refs[-1]) + load_slices(gates, parts, refs[-2])

    def tile(rows):
        for gate, product in zip(gates, products):
            for start in range(0, product.shape[1], CHUNK):
                cols = slice(start, start + CHUNK)
                product[rows, cols] = dot(x[rows, :], gate[:, cols], NN)

    over_tiles(x.shape[0], tile)
    for load in loads:
        load.wait()


def up_kernel(first, last, start_down, *refs):
    count = last - first
    products, ups, refs = refs[:count], refs[count : 2 * count], refs[2 * count :]
    x, masks, w_down, value = refs[:4]
    known, parts, refs = refs[4 : 4 + 3 * count], refs[4 + 3 * count : 4 + 4 * count], refs[4 + 4 * count :]
    downs, (same, part_sems, down_sems) = refs[:-3], refs[-3:]
    bf16 = jnp.bfloat16
    hidden_units = ups[0].shape[1]
    loads = load_downs(w_down, downs, start_down, down_sems) + load_slices(ups, parts, part_sems)
    same[...] = value[...]

    def tile(rows):
        for i in range(count):
            hidden, slope_up, slope_gate = known[3 * i : 3 * i + 3]
            for start in range(0, hidden_units, CHUNK):
                cols = slice(start, start + CHUNK)
                up_proj = dot(x[rows, :], ups[i][:, cols], NN)
                at = ids_along((1, CHUNK), 1)
                keep = jnp.zeros((1, CHUNK), jnp.float32)
                for j in range(CHUNK // BLK):
                    kept = masks[first + i, start // BLK + j].astype(jnp.float32)
                    keep = jnp.where(at // BLK == j, kept, keep)
                gate_pre = products[i][rows, cols]
                sigma = 0.5 + 0.5 * jnp.tanh(0.5 * gate_pre)
                silu = gate_pre * sigma
                up_kept = up_proj * keep
                hidden[rows, cols] = (silu * up_kept).astype(bf16)
                slope_up[rows, cols] = (silu * keep).astype(bf16)
                slope = up_kept * (sigma + silu * (1.0 - sigma))
                slope_gate[rows, cols] = slope.astype(bf16)

    over_tiles(x.shape[0], tile)
    for load in loads:
        load.wait()


def hidden_kernel(local_experts, count, *refs):
    packet, refs = refs[0], refs[1:]
    known = [refs[i * 6 : i * 6 + 6] for i in range(local_experts)]
    refs = refs[6 * local_experts :]
    hidden, d_gate, d_up = refs[:3]
    outs, (inner, mixed, token_grad) = refs[3 : 3 + count], refs[3 + count :]
    hidden_units, width = known[0][5].shape
    tokens, part = mixed.shape
    lanes = packet.shape[1] - width
    half = lanes // 2
    base = lax.axis_index("expert") * local_experts
    mine = aligned(lax.axis_index("dp"), part)
    bf16, f32 = jnp.bfloat16, jnp.float32
    inner[...] = jnp.zeros(inner.shape, inner.dtype)
    mixed[...] = jnp.zeros(mixed.shape, mixed.dtype)
    token_grad[...] = jnp.zeros(token_grad.shape, token_grad.dtype)

    for expert in range(local_experts):

        def tile(rows, expert=expert):
            units, slope_up, slope_gate, gate, up, down = known[expert]
            dense = packet[rows, width:].astype(f32)
            at = ids_along((TILE, lanes), 1)
            hit = at == base + expert
            weights = jnp.sum(jnp.where(hit, dense, 0.0), axis=1, keepdims=True)
            total = jnp.zeros((TILE, 1), f32)
            for start in range(0, hidden_units, CHUNK):
                cols = slice(start, start + CHUNK)
                back = dot(packet[rows, :width], down[cols, :], NT)
                part_units = units[rows, cols].astype(f32)
                total += jnp.sum(part_units * back, axis=1, keepdims=True)
                back = back * weights
                new_gate = back * slope_gate[rows, cols].astype(f32)
                new_up = back * slope_up[rows, cols].astype(f32)
                hidden[expert, rows, cols] = (part_units * weights).astype(bf16)
                d_gate[expert, rows, cols] = new_gate.astype(bf16)
                d_up[expert, rows, cols] = new_up.astype(bf16)
            high = total.astype(bf16).astype(f32)
            inner[rows, :] += jnp.where(
                hit, high, jnp.where(at == base + expert + half, total - high, 0.0)
            )
            mixed[rows, :] += dot(hidden[expert, rows, :], down[:, mine], NN)
            token_grad[rows, :] += dot(d_gate[expert, rows, :], gate[...], NT) + dot(
                d_up[expert, rows, :], up[...], NT
            )

        over_tiles(tokens, tile)

    rows = outs[0].shape[0]
    for i, out in enumerate(outs):
        block = slice(i * rows, (i + 1) * rows)
        out[:, :part] = mixed[block].astype(bf16)
        out[:, part : 2 * part] = token_grad[block].astype(bf16)
        out[:, 2 * part :] = inner[block].astype(bf16)


def write_out(steps, place, outs, bufs, sems, body):
    def copies(step, slot):
        return [
            pltpu.make_async_copy(buf.at[slot], out.at[place(step)], sems.at[slot, i])
            for i, (out, buf) in enumerate(zip(outs, bufs))
        ]

    def turn(step, carry):
        slot = lax.rem(step, 2)

        @pl.when(step >= 2)
        def _():
            for copy in copies(step - 2, slot):
                copy.wait()

        body(step, slot)
        for copy in copies(step, slot):
            copy.start()
        return carry

    lax.fori_loop(0, steps, turn, 0)
    for step in range(max(steps - 2, 0), steps):
        for copy in copies(step, step % 2):
            copy.wait()


def grad_in_kernel(x_part, d_gate, d_up, grad_gate, grad_up, done, out_gate, out_up, sems):
    local_experts = d_gate.shape[0]
    part, rows = x_part.shape[0], out_gate.shape[1]
    done[...] = jnp.zeros(done.shape, done.dtype)
    blocks = part // rows

    def place(step):
        return step // blocks, aligned(lax.rem(step, blocks), rows), slice(None)

    def body(step, slot):
        expert, block, _ = place(step)
        out_gate[slot] = dot(x_part[block, :], d_gate[expert], NN)
        out_up[slot] = dot(x_part[block, :], d_up[expert], NN)

    write_out(
        local_experts * blocks, place, (grad_gate, grad_up), (out_gate, out_up), sems, body
    )


def grad_out_kernel(packet, hidden, after, grad_down, done, cot_part, out_down, sems):
    local_experts = hidden.shape[0]
    part = cot_part.shape[1]
    cot_part[...] = packet[:, aligned(lax.axis_index("dp"), part)]
    done[...] = jnp.zeros(done.shape, done.dtype)

    def place(step):
        return (step,)

    def body(step, slot):
        out_down[slot] = dot(hidden[step].T, cot_part[...], NN)

    write_out(local_experts, place, (grad_down,), (out_down,), sems, body)


def reduce_kernel(count, *refs):
    blocks, refs = refs[:count], refs[count:]
    expert_ids, after, route_grad = refs[:3]
    outs, done = refs[3:-1], refs[-1]
    done[...] = jnp.zeros(done.shape, done.dtype)
    rows, both = outs[0].shape
    half = (blocks[0].shape[1] - both) // 2
    for j, out in enumerate(outs):
        total = jnp.zeros((rows, both), jnp.float32)
        for block in blocks:
            total += block[j * rows : (j + 1) * rows, :both].astype(jnp.float32)
        out[...] = total.astype(out.dtype)
    inner = jnp.zeros((rows, 2 * half), jnp.float32)
    for block in blocks:
        inner += block[:rows, both:].astype(jnp.float32)
    inner = inner.T
    inner = inner[:half] + inner[half:]
    at = ids_along(inner.shape, 0)
    for k in range(expert_ids.shape[0]):
        hit = jnp.where(expert_ids[k : k + 1, :] == at, inner, 0.0)
        route_grad[k : k + 1, :] = jnp.sum(hit, axis=0, keepdims=True)


def join_kernel(count, *refs):
    blocks, (after, mixed, token_grad) = refs[:count], refs[count:]
    part = blocks[0].shape[1] // 2
    column = lax.axis_index("dp")
    for other, block in enumerate(blocks):
        cols = aligned(column ^ other, part)
        mixed[:, cols] = block[:, :part]
        token_grad[:, cols] = block[:, part:]


def swap(value, axis, mask):
    size = lax.axis_size(axis)
    return lax.ppermute(value, axis, [(i, i ^ mask) for i in range(size)])


def exchange(value, axis, masks):
    return [swap(value, axis, mask) for mask in masks]


def in_hbm(array):
    return pltpu.with_memory_space_constraint(array, pltpu.HBM)


def in_vmem(array):
    return pltpu.with_memory_space_constraint(array, pltpu.VMEM)


def cost(flops, moved):
    return pl.CostEstimate(flops=flops, bytes_accessed=moved, transcendentals=0)


def params(mib):
    return pltpu.CompilerParams(vmem_limit_bytes=mib * MIB)


def per_device(
    tokens, expert_ids, slot_index, route_weights, w_gate, w_up, w_down, block_masks, cotangent
):
    rows, width = tokens.shape
    local_experts, _, hidden_units = w_gate.shape
    sources, columns = lax.axis_size("expert"), lax.axis_size("dp")
    chips = list(range(2, sources, 2))
    expert_order = [0] + chips + [chip ^ 1 for chip in [0] + chips]
    lanes = -(-2 * local_experts * sources // LANES) * LANES
    part = width // columns
    everyone = sources * columns * rows
    bf16, f32 = jnp.bfloat16, jnp.float32
    struct = jax.ShapeDtypeStruct
    one = 2 * local_experts * width * hidden_units
    room = 8 + (everyone - TILE) * (2 * part + lanes) * 10 // MIB
    dummy = struct((8, LANES), f32)
    ids_t = expert_ids.T
    w_gate, w_up, w_down = [in_hbm(w) for w in (w_gate, w_up, w_down)]

    own_tokens, packet = pl.pallas_call(
        route_kernel,
        out_shape=[struct(tokens.shape, bf16), struct((rows, width + lanes), bf16)],
        in_specs=[HBM] * 4,
        out_specs=[VMEM] * 2,
        scratch_shapes=[
            pltpu.VMEM(ids_t.shape, jnp.int32),
            pltpu.VMEM(ids_t.shape, bf16),
            pltpu.SemaphoreType.DMA((4,)),
        ],
        compiler_params=params(room),
        name="route",
    )(*[in_hbm(a) for a in (tokens, cotangent, ids_t, route_weights.T)])

    def load(weight, value, name):
        same, *loaded = pl.pallas_call(
            load_kernel,
            out_shape=[struct(value.shape, bf16)]
            + [pltpu.VMEM(weight.shape[1:], bf16)] * local_experts,
            in_specs=[HBM, VMEM],
            out_specs=[VMEM] * (1 + local_experts),
            scratch_shapes=[pltpu.SemaphoreType.DMA((local_experts,))],
            cost_estimate=cost(0, one),
            compiler_params=params(room),
            name=name,
        )(weight, value)
        return [in_vmem(array) for array in loaded], same

    tokens_near = exchange(tokens, "dp", range(1, columns))
    c_column = jnp.concatenate([packet] + exchange(packet, "dp", range(1, columns)))
    ups, own_tokens = load(w_up, own_tokens, "load_up")
    x_column = jnp.concatenate([own_tokens] + tokens_near)
    x_across = exchange(x_column, "expert", chips)
    c_across = exchange(c_column, "expert", chips)
    gates, x_column = load(w_gate, x_column, "load_gate")
    x = jnp.concatenate([x_column] + x_across)
    x = jnp.concatenate([x, swap(x, "expert", 1)])

    middle = max(local_experts // 2, 1)
    weight_part = pltpu.VMEM((part, hidden_units), bf16)
    weight_down = pltpu.VMEM(w_down.shape[1:], bf16)
    found = pl.pallas_call(
        functools.partial(gate_kernel, local_experts),
        out_shape=[struct((everyone, hidden_units), f32)] * local_experts
        + [weight_part] * local_experts
        + [weight_down] * middle,
        in_specs=[VMEM] * (local_experts + 1) + [HBM],
        out_specs=[VMEM] * (2 * local_experts + middle),
        scratch_shapes=[
            pltpu.SemaphoreType.DMA((local_experts,)),
            pltpu.SemaphoreType.DMA((middle,)),
        ],
        cost_estimate=cost(everyone * one, one),
        compiler_params=params(room),
        name="gate",
    )(*gates, x, w_down)
    found = list(found)
    products = found[:local_experts]
    gate_parts = [in_vmem(array) for array in found[local_experts : 2 * local_experts]]
    downs = [in_vmem(array) for array in found[2 * local_experts :]]

    def up_call(first, last, start_down, value):
        count, more = last - first, local_experts - start_down
        found = pl.pallas_call(
            functools.partial(up_kernel, first, last, start_down),
            out_shape=[struct((everyone, hidden_units), bf16)] * (3 * count)
            + [weight_part] * count
            + [weight_down] * more
            + [struct(value.shape, value.dtype)],
            in_specs=[VMEM] * (2 * count + 1) + [SMEM, HBM, VMEM],
            out_specs=[VMEM] * (4 * count + more + 1),
            scratch_shapes=[
                pltpu.SemaphoreType.DMA((count,)),
                pltpu.SemaphoreType.DMA((max(more, 1),)),
            ],
            cost_estimate=cost(
                everyone * one * count // local_experts, one * count // local_experts
            ),
            compiler_params=params(room),
            name="up",
        )(*products[first:last], *ups[first:last], x, block_masks, w_down, value)
        found = list(found)
        arrays = [in_vmem(array) for array in found[3 * count : -1]]
        return found[: 3 * count], arrays[:count], arrays[count:], found[-1]

    factors, up_parts, more_downs, c_column = up_call(0, middle, middle, c_column)
    downs = downs + more_downs
    if middle < local_experts:
        more, more_parts, _, _ = up_call(middle, local_experts, local_experts, c_column)
        factors, up_parts = factors + more, up_parts + more_parts
    known = []
    for i in range(local_experts):
        known += factors[3 * i : 3 * i + 3] + [gate_parts[i], up_parts[i], downs[i]]
    c_half = jnp.concatenate([c_column] + c_across)
    packets = jnp.concatenate([c_half, swap(c_half, "expert", 1)])
    x_part = pl.pallas_call(
        turn_kernel,
        out_shape=struct((part, everyone), bf16),
        in_specs=[VMEM] * 2,
        out_specs=VMEM,
        compiler_params=params(room),
        name="turn",
    )(x, c_half)

    units = struct((local_experts, everyone, hidden_units), bf16)
    hidden, d_gate, d_up, *partials = pl.pallas_call(
        functools.partial(hidden_kernel, local_experts, sources),
        out_shape=[units] * 3
        + [struct((columns * rows, 2 * part + lanes), bf16)] * sources,
        in_specs=[VMEM] * (1 + len(known)),
        out_specs=[VMEM] * (3 + sources),
        scratch_shapes=[
            pltpu.VMEM((everyone, lanes), f32),
            pltpu.VMEM((everyone, part), f32),
            pltpu.VMEM((everyone, part), f32),
        ],
        cost_estimate=cost(2 * everyone * one, 2 * one),
        compiler_params=params(room),
        name="hidden",
    )(packets, *known)
    arrived = [
        swap(partial, "expert", other) if other else partial
        for other, partial in zip(expert_order, partials)
    ]

    grad_gate, grad_up, done_in = pl.pallas_call(
        grad_in_kernel,
        out_shape=[struct((local_experts, part, hidden_units), f32)] * 2 + [dummy],
        in_specs=[VMEM] * 3,
        out_specs=[HBM] * 2 + [VMEM],
        scratch_shapes=[
            pltpu.VMEM((2, min(part, CHUNK), hidden_units), f32),
            pltpu.VMEM((2, min(part, CHUNK), hidden_units), f32),
            pltpu.SemaphoreType.DMA((2, 2)),
        ],
        cost_estimate=cost(2 * everyone * one // columns, 4 * one // columns),
        compiler_params=params(room),
        name="grad_in",
    )(x_part, d_gate, d_up)

    route_grad, *blocks, done_sum = pl.pallas_call(
        functools.partial(reduce_kernel, sources),
        out_shape=[struct(ids_t.shape, f32)] + [struct((rows, 2 * part), bf16)] * columns + [dummy],
        in_specs=[VMEM] * (sources + 2),
        out_specs=[VMEM] * (columns + 2),
        compiler_params=params(room),
        name="reduce",
    )(*arrived, ids_t, done_in)
    blocks = [
        swap(block, "dp", other) if other else block for other, block in enumerate(blocks)
    ]

    grad_down, done_out = pl.pallas_call(
        grad_out_kernel,
        out_shape=[struct((local_experts, hidden_units, part), f32), dummy],
        in_specs=[VMEM] * 3,
        out_specs=[HBM, VMEM],
        scratch_shapes=[
            pltpu.VMEM((everyone, part), bf16),
            pltpu.VMEM((2, hidden_units, part), f32),
            pltpu.SemaphoreType.DMA((2, 1)),
        ],
        cost_estimate=cost(everyone * one // columns, 2 * one // columns),
        compiler_params=params(room),
        name="grad_out",
    )(packets, hidden, done_sum)

    mixed, token_grad = pl.pallas_call(
        functools.partial(join_kernel, columns),
        out_shape=[struct((rows, width), bf16)] * 2,
        in_specs=[VMEM] * (columns + 1),
        out_specs=[VMEM] * 2,
        compiler_params=params(room),
        name="join",
    )(*blocks, done_out)
    return (mixed, token_grad, route_grad.T, grad_gate, grad_up, grad_down)


def solution(mesh):
    rows = P(("groups", "expert", "dp"), None)
    experts = P("expert", None, None)
    return jax.shard_map(
        per_device,
        mesh=mesh,
        in_specs=(rows, rows, rows, rows, experts, experts, experts, P("expert", None), rows),
        out_specs=(
            rows,
            rows,
            rows,
            P(("groups", "expert"), "dp", None),
            P(("groups", "expert"), "dp", None),
            P(("groups", "expert"), None, "dp"),
        ),
        check_vma=False,
    )
```

```python
import functools

import jax
import jax.numpy as jnp
from jax import lax
from jax.experimental import pallas as pl
from jax.experimental.pallas import tpu as pltpu
from jax.sharding import PartitionSpec as P

BLK = 128
LANES = 128
CHUNK = 256
TILE = 256
MIB = 1 << 20

VMEM = pl.BlockSpec(memory_space=pltpu.VMEM)
SMEM = pl.BlockSpec(memory_space=pltpu.SMEM)
HBM = pl.BlockSpec(memory_space=pltpu.HBM)

NN = (((1,), (0,)), ((), ()))
NT = (((1,), (1,)), ((), ()))


def dot(a, b, dims):
    return lax.dot_general(a, b, dims, preferred_element_type=jnp.float32)


def ids_along(shape, axis):
    return lax.broadcasted_iota(jnp.int32, shape, axis)


def aligned(index, size):
    return pl.ds(pl.multiple_of(index * size, size), size)


def route_kernel(
    tokens, cotangent, expert_ids, route_weights, own_tokens, packet, ids, values, sems
):
    rows, width = tokens.shape
    lanes = packet.shape[1] - width
    copies = [
        pltpu.make_async_copy(expert_ids, ids, sems.at[0]),
        pltpu.make_async_copy(route_weights, values, sems.at[1]),
        pltpu.make_async_copy(tokens, own_tokens, sems.at[2]),
        pltpu.make_async_copy(cotangent, packet.at[:, :width], sems.at[3]),
    ]
    for copy in copies:
        copy.start()
    for copy in copies:
        copy.wait()
    at = ids_along((lanes, rows), 0)
    weights = values[...].astype(jnp.float32)
    dense = jnp.zeros((lanes, rows), jnp.float32)
    for k in range(ids.shape[0]):
        dense += jnp.where(ids[k : k + 1, :] == at, weights[k : k + 1, :], 0.0)
    packet[:, width:] = dense.T.astype(packet.dtype)


def load_kernel(weight, value, same, *refs):
    targets, sems = refs[:-1], refs[-1]
    copies = [
        pltpu.make_async_copy(weight.at[i], target, sems.at[i]) for i, target in enumerate(targets)
    ]
    for copy in copies:
        copy.start()
    same[...] = value[...]
    for copy in copies:
        copy.wait()


def turn_kernel(x, after, x_part):
    x_part[...] = x[:, aligned(lax.axis_index("dp"), x_part.shape[0])].T


def over_tiles(tokens, body):
    if tokens == TILE:
        body(slice(0, TILE))
    else:

        def turn(tile, carry):
            body(aligned(tile, TILE))
            return carry

        lax.fori_loop(0, tokens // TILE, turn, 0)


def load_slices(weights, targets, sems):
    mine = aligned(lax.axis_index("dp"), targets[0].shape[0])
    copies = [
        pltpu.make_async_copy(weight.at[mine, :], target, sems.at[i])
        for i, (weight, target) in enumerate(zip(weights, targets))
    ]
    for copy in copies:
        copy.start()
    return copies


def load_downs(w_down, targets, first, sems):
    copies = [
        pltpu.make_async_copy(w_down.at[first + i], target, sems.at[i])
        for i, target in enumerate(targets)
    ]
    for copy in copies:
        copy.start()
    return copies


def gate_kernel(count, *refs):
    gates, x, w_down, refs = refs[:count], refs[count], refs[count + 1], refs[count + 2 :]
    products, parts, downs = refs[:count], refs[count : 2 * count], refs[2 * count : -2]
    loads = load_downs(w_down, downs, 0, refs[-1]) + load_slices(gates, parts, refs[-2])

    def tile(rows):
        for gate, product in zip(gates, products):
            for start in range(0, product.shape[1], CHUNK):
                cols = slice(start, start + CHUNK)
                product[rows, cols] = dot(x[rows, :], gate[:, cols], NN)

    over_tiles(x.shape[0], tile)
    for load in loads:
        load.wait()


def up_kernel(first, last, start_down, *refs):
    count = last - first
    products, ups, refs = refs[:count], refs[count : 2 * count], refs[2 * count :]
    x, masks, w_down, value = refs[:4]
    known, parts, refs = refs[4 : 4 + 3 * count], refs[4 + 3 * count : 4 + 4 * count], refs[4 + 4 * count :]
    downs, (same, part_sems, down_sems) = refs[:-3], refs[-3:]
    bf16 = jnp.bfloat16
    hidden_units = ups[0].shape[1]
    loads = load_downs(w_down, downs, start_down, down_sems) + load_slices(ups, parts, part_sems)
    same[...] = value[...]

    def tile(rows):
        for i in range(count):
            hidden, slope_up, slope_gate = known[3 * i : 3 * i + 3]
            for start in range(0, hidden_units, CHUNK):
                cols = slice(start, start + CHUNK)
                up_proj = dot(x[rows, :], ups[i][:, cols], NN)
                at = ids_along((1, CHUNK), 1)
                keep = jnp.zeros((1, CHUNK), jnp.float32)
                for j in range(CHUNK // BLK):
                    kept = masks[first + i, start // BLK + j].astype(jnp.float32)
                    keep = jnp.where(at // BLK == j, kept, keep)
                gate_pre = products[i][rows, cols]
                sigma = 0.5 + 0.5 * jnp.tanh(0.5 * gate_pre)
                silu = gate_pre * sigma
                up_kept = up_proj * keep
                hidden[rows, cols] = (silu * up_kept).astype(bf16)
                slope_up[rows, cols] = (silu * keep).astype(bf16)
                slope = up_kept * (sigma + silu * (1.0 - sigma))
                slope_gate[rows, cols] = slope.astype(bf16)

    over_tiles(x.shape[0], tile)
    for load in loads:
        load.wait()


def hidden_kernel(local_experts, count, *refs):
    packet, refs = refs[0], refs[1:]
    known = [refs[i * 6 : i * 6 + 6] for i in range(local_experts)]
    refs = refs[6 * local_experts :]
    hidden, d_gate, d_up = refs[:3]
    outs, (inner, mixed, token_grad) = refs[3 : 3 + count], refs[3 + count :]
    hidden_units, width = known[0][5].shape
    tokens, part = mixed.shape
    lanes = packet.shape[1] - width
    half = lanes // 2
    base = lax.axis_index("expert") * local_experts
    mine = aligned(lax.axis_index("dp"), part)
    bf16, f32 = jnp.bfloat16, jnp.float32
    inner[...] = jnp.zeros(inner.shape, inner.dtype)
    mixed[...] = jnp.zeros(mixed.shape, mixed.dtype)
    token_grad[...] = jnp.zeros(token_grad.shape, token_grad.dtype)

    for expert in range(local_experts):

        def tile(rows, expert=expert):
            units, slope_up, slope_gate, gate, up, down = known[expert]
            dense = packet[rows, width:].astype(f32)
            at = ids_along((TILE, lanes), 1)
            hit = at == base + expert
            weights = jnp.sum(jnp.where(hit, dense, 0.0), axis=1, keepdims=True)
            total = jnp.zeros((TILE, 1), f32)
            for start in range(0, hidden_units, CHUNK):
                cols = slice(start, start + CHUNK)
                back = dot(packet[rows, :width], down[cols, :], NT)
                part_units = units[rows, cols].astype(f32)
                total += jnp.sum(part_units * back, axis=1, keepdims=True)
                back = back * weights
                new_gate = back * slope_gate[rows, cols].astype(f32)
                new_up = back * slope_up[rows, cols].astype(f32)
                hidden[expert, rows, cols] = (part_units * weights).astype(bf16)
                d_gate[expert, rows, cols] = new_gate.astype(bf16)
                d_up[expert, rows, cols] = new_up.astype(bf16)
            high = total.astype(bf16).astype(f32)
            inner[rows, :] += jnp.where(
                hit, high, jnp.where(at == base + expert + half, total - high, 0.0)
            )
            mixed[rows, :] += dot(hidden[expert, rows, :], down[:, mine], NN)
            token_grad[rows, :] += dot(d_gate[expert, rows, :], gate[...], NT) + dot(
                d_up[expert, rows, :], up[...], NT
            )

        over_tiles(tokens, tile)

    rows = outs[0].shape[0]
    for i, out in enumerate(outs):
        block = slice(i * rows, (i + 1) * rows)
        out[:, :part] = mixed[block].astype(bf16)
        out[:, part : 2 * part] = token_grad[block].astype(bf16)
        out[:, 2 * part :] = inner[block].astype(bf16)


def write_out(steps, place, outs, bufs, sems, body):
    def copies(step, slot):
        return [
            pltpu.make_async_copy(buf.at[slot], out.at[place(step)], sems.at[slot, i])
            for i, (out, buf) in enumerate(zip(outs, bufs))
        ]

    def turn(step, carry):
        slot = lax.rem(step, 2)

        @pl.when(step >= 2)
        def _():
            for copy in copies(step - 2, slot):
                copy.wait()

        body(step, slot)
        for copy in copies(step, slot):
            copy.start()
        return carry

    lax.fori_loop(0, steps, turn, 0)
    for step in range(max(steps - 2, 0), steps):
        for copy in copies(step, step % 2):
            copy.wait()


def grad_in_kernel(x_part, d_gate, d_up, grad_gate, grad_up, done, out_gate, out_up, sems):
    local_experts = d_gate.shape[0]
    part, rows = x_part.shape[0], out_gate.shape[1]
    done[...] = jnp.zeros(done.shape, done.dtype)
    blocks = part // rows

    def place(step):
        return step // blocks, aligned(lax.rem(step, blocks), rows), slice(None)

    def body(step, slot):
        expert, block, _ = place(step)
        out_gate[slot] = dot(x_part[block, :], d_gate[expert], NN)
        out_up[slot] = dot(x_part[block, :], d_up[expert], NN)

    write_out(
        local_experts * blocks, place, (grad_gate, grad_up), (out_gate, out_up), sems, body
    )


def grad_out_kernel(packet, hidden, after, grad_down, done, cot_part, out_down, sems):
    local_experts = hidden.shape[0]
    part = cot_part.shape[1]
    cot_part[...] = packet[:, aligned(lax.axis_index("dp"), part)]
    done[...] = jnp.zeros(done.shape, done.dtype)

    size = out_down.shape[1]
    blocks = hidden.shape[2] // size

    def place(step):
        return step // blocks, aligned(lax.rem(step, blocks), size), slice(None)

    def body(step, slot):
        units = hidden[step // blocks, :, aligned(lax.rem(step, blocks), size)]
        out_down[slot] = dot(units.T, cot_part[...], NN)

    write_out(local_experts * blocks, place, (grad_down,), (out_down,), sems, body)


def reduce_kernel(count, *refs):
    blocks, refs = refs[:count], refs[count:]
    expert_ids, after, route_grad = refs[:3]
    outs, done = refs[3:-1], refs[-1]
    done[...] = jnp.zeros(done.shape, done.dtype)
    rows, both = outs[0].shape
    half = (blocks[0].shape[1] - both) // 2
    for j, out in enumerate(outs):
        total = jnp.zeros((rows, both), jnp.float32)
        for block in blocks:
            total += block[j * rows : (j + 1) * rows, :both].astype(jnp.float32)
        out[...] = total.astype(out.dtype)
    inner = jnp.zeros((rows, 2 * half), jnp.float32)
    for block in blocks:
        inner += block[:rows, both:].astype(jnp.float32)
    inner = inner.T
    inner = inner[:half] + inner[half:]
    at = ids_along(inner.shape, 0)
    for k in range(expert_ids.shape[0]):
        hit = jnp.where(expert_ids[k : k + 1, :] == at, inner, 0.0)
        route_grad[k : k + 1, :] = jnp.sum(hit, axis=0, keepdims=True)


def join_kernel(count, *refs):
    blocks, (after, mixed, token_grad) = refs[:count], refs[count:]
    part = blocks[0].shape[1] // 2
    column = lax.axis_index("dp")
    for other, block in enumerate(blocks):
        cols = aligned(column ^ other, part)
        mixed[:, cols] = block[:, :part]
        token_grad[:, cols] = block[:, part:]


def swap(value, axis, mask):
    size = lax.axis_size(axis)
    return lax.ppermute(value, axis, [(i, i ^ mask) for i in range(size)])


def exchange(value, axis, masks):
    return [swap(value, axis, mask) for mask in masks]


def in_hbm(array):
    return pltpu.with_memory_space_constraint(array, pltpu.HBM)


def in_vmem(array):
    return pltpu.with_memory_space_constraint(array, pltpu.VMEM)


def cost(flops, moved):
    return pl.CostEstimate(flops=flops, bytes_accessed=moved, transcendentals=0)


def params(mib):
    return pltpu.CompilerParams(vmem_limit_bytes=mib * MIB)


def per_device(
    tokens, expert_ids, slot_index, route_weights, w_gate, w_up, w_down, block_masks, cotangent
):
    rows, width = tokens.shape
    local_experts, _, hidden_units = w_gate.shape
    sources, columns = lax.axis_size("expert"), lax.axis_size("dp")
    chips = list(range(2, sources, 2))
    expert_order = [0] + chips + [chip ^ 1 for chip in [0] + chips]
    lanes = -(-2 * local_experts * sources // LANES) * LANES
    part = width // columns
    everyone = sources * columns * rows
    bf16, f32 = jnp.bfloat16, jnp.float32
    struct = jax.ShapeDtypeStruct
    one = 2 * local_experts * width * hidden_units
    room = 8 + (everyone - TILE) * (2 * part + lanes) * 10 // MIB
    dummy = struct((8, LANES), f32)
    ids_t = expert_ids.T
    w_gate, w_up, w_down = [in_hbm(w) for w in (w_gate, w_up, w_down)]

    own_tokens, packet = pl.pallas_call(
        route_kernel,
        out_shape=[struct(tokens.shape, bf16), struct((rows, width + lanes), bf16)],
        in_specs=[HBM] * 4,
        out_specs=[VMEM] * 2,
        scratch_shapes=[
            pltpu.VMEM(ids_t.shape, jnp.int32),
            pltpu.VMEM(ids_t.shape, bf16),
            pltpu.SemaphoreType.DMA((4,)),
        ],
        compiler_params=params(room),
        name="route",
    )(*[in_hbm(a) for a in (tokens, cotangent, ids_t, route_weights.T)])

    def load(weight, value, name):
        same, *loaded = pl.pallas_call(
            load_kernel,
            out_shape=[struct(value.shape, bf16)]
            + [pltpu.VMEM(weight.shape[1:], bf16)] * local_experts,
            in_specs=[HBM, VMEM],
            out_specs=[VMEM] * (1 + local_experts),
            scratch_shapes=[pltpu.SemaphoreType.DMA((local_experts,))],
            cost_estimate=cost(0, one),
            compiler_params=params(room),
            name=name,
        )(weight, value)
        return [in_vmem(array) for array in loaded], same

    tokens_near = exchange(tokens, "dp", range(1, columns))
    c_column = jnp.concatenate([packet] + exchange(packet, "dp", range(1, columns)))
    ups, own_tokens = load(w_up, own_tokens, "load_up")
    x_column = jnp.concatenate([own_tokens] + tokens_near)
    x_across = exchange(x_column, "expert", chips)
    c_across = exchange(c_column, "expert", chips)
    gates, x_column = load(w_gate, x_column, "load_gate")
    x = jnp.concatenate([x_column] + x_across)
    x = jnp.concatenate([x, swap(x, "expert", 1)])

    middle = max(local_experts // 2, 1)
    weight_part = pltpu.VMEM((part, hidden_units), bf16)
    weight_down = pltpu.VMEM(w_down.shape[1:], bf16)
    found = pl.pallas_call(
        functools.partial(gate_kernel, local_experts),
        out_shape=[struct((everyone, hidden_units), f32)] * local_experts
        + [weight_part] * local_experts
        + [weight_down] * middle,
        in_specs=[VMEM] * (local_experts + 1) + [HBM],
        out_specs=[VMEM] * (2 * local_experts + middle),
        scratch_shapes=[
            pltpu.SemaphoreType.DMA((local_experts,)),
            pltpu.SemaphoreType.DMA((middle,)),
        ],
        cost_estimate=cost(everyone * one, one),
        compiler_params=params(room),
        name="gate",
    )(*gates, x, w_down)
    found = list(found)
    products = found[:local_experts]
    gate_parts = [in_vmem(array) for array in found[local_experts : 2 * local_experts]]
    downs = [in_vmem(array) for array in found[2 * local_experts :]]

    def up_call(first, last, start_down, value):
        count, more = last - first, local_experts - start_down
        found = pl.pallas_call(
            functools.partial(up_kernel, first, last, start_down),
            out_shape=[struct((everyone, hidden_units), bf16)] * (3 * count)
            + [weight_part] * count
            + [weight_down] * more
            + [struct(value.shape, value.dtype)],
            in_specs=[VMEM] * (2 * count + 1) + [SMEM, HBM, VMEM],
            out_specs=[VMEM] * (4 * count + more + 1),
            scratch_shapes=[
                pltpu.SemaphoreType.DMA((count,)),
                pltpu.SemaphoreType.DMA((max(more, 1),)),
            ],
            cost_estimate=cost(
                everyone * one * count // local_experts, one * count // local_experts
            ),
            compiler_params=params(room),
            name="up",
        )(*products[first:last], *ups[first:last], x, block_masks, w_down, value)
        found = list(found)
        arrays = [in_vmem(array) for array in found[3 * count : -1]]
        return found[: 3 * count], arrays[:count], arrays[count:], found[-1]

    factors, up_parts, more_downs, c_column = up_call(0, middle, middle, c_column)
    downs = downs + more_downs
    if middle < local_experts:
        more, more_parts, _, _ = up_call(middle, local_experts, local_experts, c_column)
        factors, up_parts = factors + more, up_parts + more_parts
    known = []
    for i in range(local_experts):
        known += factors[3 * i : 3 * i + 3] + [gate_parts[i], up_parts[i], downs[i]]
    c_half = jnp.concatenate([c_column] + c_across)
    packets = jnp.concatenate([c_half, swap(c_half, "expert", 1)])
    x_part = pl.pallas_call(
        turn_kernel,
        out_shape=struct((part, everyone), bf16),
        in_specs=[VMEM] * 2,
        out_specs=VMEM,
        compiler_params=params(room),
        name="turn",
    )(x, c_half)

    units = struct((local_experts, everyone, hidden_units), bf16)
    hidden, d_gate, d_up, *partials = pl.pallas_call(
        functools.partial(hidden_kernel, local_experts, sources),
        out_shape=[units] * 3
        + [struct((columns * rows, 2 * part + lanes), bf16)] * sources,
        in_specs=[VMEM] * (1 + len(known)),
        out_specs=[VMEM] * (3 + sources),
        scratch_shapes=[
            pltpu.VMEM((everyone, lanes), f32),
            pltpu.VMEM((everyone, part), f32),
            pltpu.VMEM((everyone, part), f32),
        ],
        cost_estimate=cost(2 * everyone * one, 2 * one),
        compiler_params=params(room),
        name="hidden",
    )(packets, *known)
    arrived = [
        swap(partial, "expert", other) if other else partial
        for other, partial in zip(expert_order, partials)
    ]

    grad_gate, grad_up, done_in = pl.pallas_call(
        grad_in_kernel,
        out_shape=[struct((local_experts, part, hidden_units), f32)] * 2 + [dummy],
        in_specs=[VMEM] * 3,
        out_specs=[HBM] * 2 + [VMEM],
        scratch_shapes=[
            pltpu.VMEM((2, BLK, hidden_units), f32),
            pltpu.VMEM((2, BLK, hidden_units), f32),
            pltpu.SemaphoreType.DMA((2, 2)),
        ],
        cost_estimate=cost(2 * everyone * one // columns, 4 * one // columns),
        compiler_params=params(room),
        name="grad_in",
    )(x_part, d_gate, d_up)

    route_grad, *blocks, done_sum = pl.pallas_call(
        functools.partial(reduce_kernel, sources),
        out_shape=[struct(ids_t.shape, f32)] + [struct((rows, 2 * part), bf16)] * columns + [dummy],
        in_specs=[VMEM] * (sources + 2),
        out_specs=[VMEM] * (columns + 2),
        compiler_params=params(room),
        name="reduce",
    )(*arrived, ids_t, done_in)
    blocks = [
        swap(block, "dp", other) if other else block for other, block in enumerate(blocks)
    ]

    grad_down, done_out = pl.pallas_call(
        grad_out_kernel,
        out_shape=[struct((local_experts, hidden_units, part), f32), dummy],
        in_specs=[VMEM] * 3,
        out_specs=[HBM, VMEM],
        scratch_shapes=[
            pltpu.VMEM((everyone, part), bf16),
            pltpu.VMEM((2, hidden_units // 2, part), f32),
            pltpu.SemaphoreType.DMA((2, 1)),
        ],
        cost_estimate=cost(everyone * one // columns, 2 * one // columns),
        compiler_params=params(room),
        name="grad_out",
    )(packets, hidden, done_sum)

    mixed, token_grad = pl.pallas_call(
        functools.partial(join_kernel, columns),
        out_shape=[struct((rows, width), bf16)] * 2,
        in_specs=[VMEM] * (columns + 1),
        out_specs=[VMEM] * 2,
        compiler_params=params(room),
        name="join",
    )(*blocks, done_out)
    return (mixed, token_grad, route_grad.T, grad_gate, grad_up, grad_down)


def solution(mesh):
    rows = P(("groups", "expert", "dp"), None)
    experts = P("expert", None, None)
    return jax.shard_map(
        per_device,
        mesh=mesh,
        in_specs=(rows, rows, rows, rows, experts, experts, experts, P("expert", None), rows),
        out_specs=(
            rows,
            rows,
            rows,
            P(("groups", "expert"), "dp", None),
            P(("groups", "expert"), "dp", None),
            P(("groups", "expert"), None, "dp"),
        ),
        check_vma=False,
    )
```

```python
import functools

import jax
import jax.numpy as jnp
from jax import lax
from jax.experimental import pallas as pl
from jax.experimental.pallas import tpu as pltpu
from jax.sharding import PartitionSpec as P

BLK = 128
LANES = 128
CHUNK = 256
TILE = 256
MIB = 1 << 20

VMEM = pl.BlockSpec(memory_space=pltpu.VMEM)
SMEM = pl.BlockSpec(memory_space=pltpu.SMEM)
HBM = pl.BlockSpec(memory_space=pltpu.HBM)

NN = (((1,), (0,)), ((), ()))
NT = (((1,), (1,)), ((), ()))


def dot(a, b, dims):
    return lax.dot_general(a, b, dims, preferred_element_type=jnp.float32)


def ids_along(shape, axis):
    return lax.broadcasted_iota(jnp.int32, shape, axis)


def aligned(index, size):
    return pl.ds(pl.multiple_of(index * size, size), size)


def route_kernel(
    tokens, cotangent, expert_ids, route_weights, own_tokens, packet, ids, values, sems
):
    rows, width = tokens.shape
    lanes = packet.shape[1] - width
    copies = [
        pltpu.make_async_copy(expert_ids, ids, sems.at[0]),
        pltpu.make_async_copy(route_weights, values, sems.at[1]),
        pltpu.make_async_copy(tokens, own_tokens, sems.at[2]),
        pltpu.make_async_copy(cotangent, packet.at[:, :width], sems.at[3]),
    ]
    for copy in copies:
        copy.start()
    for copy in copies:
        copy.wait()
    at = ids_along((lanes, rows), 0)
    weights = values[...].astype(jnp.float32)
    dense = jnp.zeros((lanes, rows), jnp.float32)
    for k in range(ids.shape[0]):
        dense += jnp.where(ids[k : k + 1, :] == at, weights[k : k + 1, :], 0.0)
    packet[:, width:] = dense.T.astype(packet.dtype)


def load_kernel(weight, value, same, *refs):
    targets, sems = refs[:-1], refs[-1]
    copies = [
        pltpu.make_async_copy(weight.at[i], target, sems.at[i]) for i, target in enumerate(targets)
    ]
    for copy in copies:
        copy.start()
    same[...] = value[...]
    for copy in copies:
        copy.wait()


def turn_kernel(x, after, x_part):
    x_part[...] = x[:, aligned(lax.axis_index("dp"), x_part.shape[0])].T


def over_tiles(tokens, body):
    if tokens == TILE:
        body(slice(0, TILE))
    else:

        def turn(tile, carry):
            body(aligned(tile, TILE))
            return carry

        lax.fori_loop(0, tokens // TILE, turn, 0)


def load_slices(weights, targets, sems):
    mine = aligned(lax.axis_index("dp"), targets[0].shape[0])
    copies = [
        pltpu.make_async_copy(weight.at[mine, :], target, sems.at[i])
        for i, (weight, target) in enumerate(zip(weights, targets))
    ]
    for copy in copies:
        copy.start()
    return copies


def load_downs(w_down, targets, first, sems):
    copies = [
        pltpu.make_async_copy(w_down.at[first + i], target, sems.at[i])
        for i, target in enumerate(targets)
    ]
    for copy in copies:
        copy.start()
    return copies


def gate_kernel(count, *refs):
    gates, x, w_down, refs = refs[:count], refs[count], refs[count + 1], refs[count + 2 :]
    products, parts, downs = refs[:count], refs[count : 2 * count], refs[2 * count : -2]
    loads = load_downs(w_down, downs, 0, refs[-1]) + load_slices(gates, parts, refs[-2])

    def tile(rows):
        for gate, product in zip(gates, products):
            for start in range(0, product.shape[1], CHUNK):
                cols = slice(start, start + CHUNK)
                product[rows, cols] = dot(x[rows, :], gate[:, cols], NN)

    over_tiles(x.shape[0], tile)
    for load in loads:
        load.wait()


def up_kernel(first, last, start_down, *refs):
    count = last - first
    products, ups, refs = refs[:count], refs[count : 2 * count], refs[2 * count :]
    x, masks, w_down, value = refs[:4]
    known, parts, refs = refs[4 : 4 + 3 * count], refs[4 + 3 * count : 4 + 4 * count], refs[4 + 4 * count :]
    downs, (same, part_sems, down_sems) = refs[:-3], refs[-3:]
    bf16 = jnp.bfloat16
    hidden_units = ups[0].shape[1]
    loads = load_downs(w_down, downs, start_down, down_sems) + load_slices(ups, parts, part_sems)
    same[...] = value[...]

    def tile(rows):
        for i in range(count):
            hidden, slope_up, slope_gate = known[3 * i : 3 * i + 3]
            for start in range(0, hidden_units, CHUNK):
                cols = slice(start, start + CHUNK)
                up_proj = dot(x[rows, :], ups[i][:, cols], NN)
                at = ids_along((1, CHUNK), 1)
                keep = jnp.zeros((1, CHUNK), jnp.float32)
                for j in range(CHUNK // BLK):
                    kept = masks[first + i, start // BLK + j].astype(jnp.float32)
                    keep = jnp.where(at // BLK == j, kept, keep)
                gate_pre = products[i][rows, cols]
                sigma = 0.5 + 0.5 * jnp.tanh(0.5 * gate_pre)
                silu = gate_pre * sigma
                up_kept = up_proj * keep
                hidden[rows, cols] = (silu * up_kept).astype(bf16)
                slope_up[rows, cols] = (silu * keep).astype(bf16)
                slope = up_kept * (sigma + silu * (1.0 - sigma))
                slope_gate[rows, cols] = slope.astype(bf16)

    over_tiles(x.shape[0], tile)
    for load in loads:
        load.wait()


def hidden_kernel(local_experts, count, *refs):
    packet, refs = refs[0], refs[1:]
    known = [refs[i * 6 : i * 6 + 6] for i in range(local_experts)]
    refs = refs[6 * local_experts :]
    hidden, d_gate, d_up = refs[:3]
    outs, (inner, mixed, token_grad) = refs[3 : 3 + count], refs[3 + count :]
    hidden_units, width = known[0][5].shape
    tokens, part = mixed.shape
    lanes = packet.shape[1] - width
    half = lanes // 2
    base = lax.axis_index("expert") * local_experts
    mine = aligned(lax.axis_index("dp"), part)
    bf16, f32 = jnp.bfloat16, jnp.float32
    inner[...] = jnp.zeros(inner.shape, inner.dtype)
    mixed[...] = jnp.zeros(mixed.shape, mixed.dtype)
    token_grad[...] = jnp.zeros(token_grad.shape, token_grad.dtype)

    for expert in range(local_experts):

        def tile(rows, expert=expert):
            units, slope_up, slope_gate, gate, up, down = known[expert]
            dense = packet[rows, width:].astype(f32)
            at = ids_along((TILE, lanes), 1)
            hit = at == base + expert
            weights = jnp.sum(jnp.where(hit, dense, 0.0), axis=1, keepdims=True)
            total = jnp.zeros((TILE, 1), f32)
            for start in range(0, hidden_units, CHUNK):
                cols = slice(start, start + CHUNK)
                back = dot(packet[rows, :width], down[cols, :], NT)
                part_units = units[rows, cols].astype(f32)
                total += jnp.sum(part_units * back, axis=1, keepdims=True)
                back = back * weights
                new_gate = back * slope_gate[rows, cols].astype(f32)
                new_up = back * slope_up[rows, cols].astype(f32)
                hidden[expert, rows, cols] = (part_units * weights).astype(bf16)
                d_gate[expert, rows, cols] = new_gate.astype(bf16)
                d_up[expert, rows, cols] = new_up.astype(bf16)
            high = total.astype(bf16).astype(f32)
            inner[rows, :] += jnp.where(
                hit, high, jnp.where(at == base + expert + half, total - high, 0.0)
            )
            mixed[rows, :] += dot(hidden[expert, rows, :], down[:, mine], NN)
            token_grad[rows, :] += dot(d_gate[expert, rows, :], gate[...], NT) + dot(
                d_up[expert, rows, :], up[...], NT
            )

        over_tiles(tokens, tile)

    rows = outs[0].shape[0]
    for i, out in enumerate(outs):
        block = slice(i * rows, (i + 1) * rows)
        out[:, :part] = mixed[block].astype(bf16)
        out[:, part : 2 * part] = token_grad[block].astype(bf16)
        out[:, 2 * part :] = inner[block].astype(bf16)


def write_out(steps, place, outs, bufs, sems, body):
    def copies(step, slot):
        return [
            pltpu.make_async_copy(buf.at[slot], out.at[place(step)], sems.at[slot, i])
            for i, (out, buf) in enumerate(zip(outs, bufs))
        ]

    def turn(step, carry):
        slot = lax.rem(step, 2)

        @pl.when(step >= 2)
        def _():
            for copy in copies(step - 2, slot):
                copy.wait()

        body(step, slot)
        for copy in copies(step, slot):
            copy.start()
        return carry

    lax.fori_loop(0, steps, turn, 0)
    for step in range(max(steps - 2, 0), steps):
        for copy in copies(step, step % 2):
            copy.wait()


def grad_in_kernel(x_part, d_gate, d_up, grad_gate, grad_up, done, out_gate, out_up, sems):
    local_experts = d_gate.shape[0]
    part, rows = x_part.shape[0], out_gate.shape[1]
    done[...] = jnp.zeros(done.shape, done.dtype)
    blocks = part // rows

    def place(step):
        return step // blocks, aligned(lax.rem(step, blocks), rows), slice(None)

    def body(step, slot):
        expert, block, _ = place(step)
        out_gate[slot] = dot(x_part[block, :], d_gate[expert], NN)
        out_up[slot] = dot(x_part[block, :], d_up[expert], NN)

    write_out(
        local_experts * blocks, place, (grad_gate, grad_up), (out_gate, out_up), sems, body
    )


def grad_out_kernel(packet, hidden, after, grad_down, done, cot_part, out_down, sems):
    local_experts = hidden.shape[0]
    part = cot_part.shape[1]
    cot_part[...] = packet[:, aligned(lax.axis_index("dp"), part)]
    done[...] = jnp.zeros(done.shape, done.dtype)

    def place(step):
        return (step,)

    def body(step, slot):
        out_down[slot] = dot(hidden[step].T, cot_part[...], NN)

    write_out(local_experts, place, (grad_down,), (out_down,), sems, body)


def reduce_kernel(count, *refs):
    blocks, refs = refs[:count], refs[count:]
    expert_ids, after, route_grad = refs[:3]
    outs, done = refs[3:-1], refs[-1]
    done[...] = jnp.zeros(done.shape, done.dtype)
    rows, both = outs[0].shape
    half = (blocks[0].shape[1] - both) // 2
    for j, out in enumerate(outs):
        total = jnp.zeros((rows, both), jnp.float32)
        for block in blocks:
            total += block[j * rows : (j + 1) * rows, :both].astype(jnp.float32)
        out[...] = total.astype(out.dtype)
    inner = jnp.zeros((rows, 2 * half), jnp.float32)
    for block in blocks:
        inner += block[:rows, both:].astype(jnp.float32)
    inner = inner.T
    inner = inner[:half] + inner[half:]
    at = ids_along(inner.shape, 0)
    for k in range(expert_ids.shape[0]):
        hit = jnp.where(expert_ids[k : k + 1, :] == at, inner, 0.0)
        route_grad[k : k + 1, :] = jnp.sum(hit, axis=0, keepdims=True)


def join_kernel(count, *refs):
    blocks, (after, mixed, token_grad) = refs[:count], refs[count:]
    part = blocks[0].shape[1] // 2
    column = lax.axis_index("dp")
    for other, block in enumerate(blocks):
        cols = aligned(column ^ other, part)
        mixed[:, cols] = block[:, :part]
        token_grad[:, cols] = block[:, part:]


def swap(value, axis, mask):
    size = lax.axis_size(axis)
    return lax.ppermute(value, axis, [(i, i ^ mask) for i in range(size)])


def exchange(value, axis, masks):
    return [swap(value, axis, mask) for mask in masks]


def in_hbm(array):
    return pltpu.with_memory_space_constraint(array, pltpu.HBM)


def in_vmem(array):
    return pltpu.with_memory_space_constraint(array, pltpu.VMEM)


def cost(flops, moved):
    return pl.CostEstimate(flops=flops, bytes_accessed=moved, transcendentals=0)


def params(mib):
    return pltpu.CompilerParams(vmem_limit_bytes=mib * MIB)


def per_device(
    tokens, expert_ids, slot_index, route_weights, w_gate, w_up, w_down, block_masks, cotangent
):
    rows, width = tokens.shape
    local_experts, _, hidden_units = w_gate.shape
    sources, columns = lax.axis_size("expert"), lax.axis_size("dp")
    chips = list(range(2, sources, 2))
    expert_order = [0] + chips + [chip ^ 1 for chip in [0] + chips]
    lanes = -(-2 * local_experts * sources // LANES) * LANES
    part = width // columns
    everyone = sources * columns * rows
    bf16, f32 = jnp.bfloat16, jnp.float32
    struct = jax.ShapeDtypeStruct
    one = 2 * local_experts * width * hidden_units
    room = 8 + (everyone - TILE) * (2 * part + lanes) * 10 // MIB
    dummy = struct((8, LANES), f32)
    ids_t = expert_ids.T
    w_gate, w_up, w_down = [in_hbm(w) for w in (w_gate, w_up, w_down)]

    own_tokens, packet = pl.pallas_call(
        route_kernel,
        out_shape=[struct(tokens.shape, bf16), struct((rows, width + lanes), bf16)],
        in_specs=[HBM] * 4,
        out_specs=[VMEM] * 2,
        scratch_shapes=[
            pltpu.VMEM(ids_t.shape, jnp.int32),
            pltpu.VMEM(ids_t.shape, bf16),
            pltpu.SemaphoreType.DMA((4,)),
        ],
        compiler_params=params(room),
        name="route",
    )(*[in_hbm(a) for a in (tokens, cotangent, ids_t, route_weights.T)])

    def load(weight, value, name):
        same, *loaded = pl.pallas_call(
            load_kernel,
            out_shape=[struct(value.shape, bf16)]
            + [pltpu.VMEM(weight.shape[1:], bf16)] * local_experts,
            in_specs=[HBM, VMEM],
            out_specs=[VMEM] * (1 + local_experts),
            scratch_shapes=[pltpu.SemaphoreType.DMA((local_experts,))],
            cost_estimate=cost(0, one),
            compiler_params=params(room),
            name=name,
        )(weight, value)
        return [in_vmem(array) for array in loaded], same

    tokens_near = exchange(tokens, "dp", range(1, columns))
    c_column = jnp.concatenate([packet] + exchange(packet, "dp", range(1, columns)))
    ups, own_tokens = load(w_up, own_tokens, "load_up")
    x_column = jnp.concatenate([own_tokens] + tokens_near)
    x_across = exchange(x_column, "expert", chips)
    c_across = exchange(c_column, "expert", chips)
    gates, x_column = load(w_gate, x_column, "load_gate")
    x = jnp.concatenate([x_column] + x_across)
    x = jnp.concatenate([x, swap(x, "expert", 1)])

    middle = max(local_experts // 2, 1)
    weight_part = pltpu.VMEM((part, hidden_units), bf16)
    weight_down = pltpu.VMEM(w_down.shape[1:], bf16)
    found = pl.pallas_call(
        functools.partial(gate_kernel, local_experts),
        out_shape=[struct((everyone, hidden_units), f32)] * local_experts
        + [weight_part] * local_experts
        + [weight_down] * middle,
        in_specs=[VMEM] * (local_experts + 1) + [HBM],
        out_specs=[VMEM] * (2 * local_experts + middle),
        scratch_shapes=[
            pltpu.SemaphoreType.DMA((local_experts,)),
            pltpu.SemaphoreType.DMA((middle,)),
        ],
        cost_estimate=cost(everyone * one, one),
        compiler_params=params(room),
        name="gate",
    )(*gates, x, w_down)
    found = list(found)
    products = found[:local_experts]
    gate_parts = [in_vmem(array) for array in found[local_experts : 2 * local_experts]]
    downs = [in_vmem(array) for array in found[2 * local_experts :]]

    def up_call(first, last, start_down, value):
        count, more = last - first, local_experts - start_down
        found = pl.pallas_call(
            functools.partial(up_kernel, first, last, start_down),
            out_shape=[struct((everyone, hidden_units), bf16)] * (3 * count)
            + [weight_part] * count
            + [weight_down] * more
            + [struct(value.shape, value.dtype)],
            in_specs=[VMEM] * (2 * count + 1) + [SMEM, HBM, VMEM],
            out_specs=[VMEM] * (4 * count + more + 1),
            scratch_shapes=[
                pltpu.SemaphoreType.DMA((count,)),
                pltpu.SemaphoreType.DMA((max(more, 1),)),
            ],
            cost_estimate=cost(
                everyone * one * count // local_experts, one * count // local_experts
            ),
            compiler_params=params(room),
            name="up",
        )(*products[first:last], *ups[first:last], x, block_masks, w_down, value)
        found = list(found)
        arrays = [in_vmem(array) for array in found[3 * count : -1]]
        return found[: 3 * count], arrays[:count], arrays[count:], found[-1]

    factors, up_parts, more_downs, c_column = up_call(0, middle, middle, c_column)
    downs = downs + more_downs
    if middle < local_experts:
        more, more_parts, _, _ = up_call(middle, local_experts, local_experts, c_column)
        factors, up_parts = factors + more, up_parts + more_parts
    known = []
    for i in range(local_experts):
        known += factors[3 * i : 3 * i + 3] + [gate_parts[i], up_parts[i], downs[i]]
    c_half = jnp.concatenate([c_column] + c_across)
    packets = jnp.concatenate([c_half, swap(c_half, "expert", 1)])
    x_part = pl.pallas_call(
        turn_kernel,
        out_shape=struct((part, everyone), bf16),
        in_specs=[VMEM] * 2,
        out_specs=VMEM,
        compiler_params=params(room),
        name="turn",
    )(x, c_half)

    units = struct((local_experts, everyone, hidden_units), bf16)
    hidden, d_gate, d_up, *partials = pl.pallas_call(
        functools.partial(hidden_kernel, local_experts, sources),
        out_shape=[units] * 3
        + [struct((columns * rows, 2 * part + lanes), bf16)] * sources,
        in_specs=[VMEM] * (1 + len(known)),
        out_specs=[VMEM] * (3 + sources),
        scratch_shapes=[
            pltpu.VMEM((everyone, lanes), f32),
            pltpu.VMEM((everyone, part), f32),
            pltpu.VMEM((everyone, part), f32),
        ],
        cost_estimate=cost(2 * everyone * one, 2 * one),
        compiler_params=params(room),
        name="hidden",
    )(packets, *known)
    arrived = [
        swap(partial, "expert", other) if other else partial
        for other, partial in zip(expert_order, partials)
    ]

    grad_gate, grad_up, done_in = pl.pallas_call(
        grad_in_kernel,
        out_shape=[struct((local_experts, part, hidden_units), f32)] * 2 + [dummy],
        in_specs=[VMEM] * 3,
        out_specs=[HBM] * 2 + [VMEM],
        scratch_shapes=[
            pltpu.VMEM((2, part, hidden_units), f32),
            pltpu.VMEM((2, part, hidden_units), f32),
            pltpu.SemaphoreType.DMA((2, 2)),
        ],
        cost_estimate=cost(2 * everyone * one // columns, 4 * one // columns),
        compiler_params=params(room + 6),
        name="grad_in",
    )(x_part, d_gate, d_up)

    route_grad, *blocks, done_sum = pl.pallas_call(
        functools.partial(reduce_kernel, sources),
        out_shape=[struct(ids_t.shape, f32)] + [struct((rows, 2 * part), bf16)] * columns + [dummy],
        in_specs=[VMEM] * (sources + 2),
        out_specs=[VMEM] * (columns + 2),
        compiler_params=params(room),
        name="reduce",
    )(*arrived, ids_t, done_in)
    blocks = [
        swap(block, "dp", other) if other else block for other, block in enumerate(blocks)
    ]

    grad_down, done_out = pl.pallas_call(
        grad_out_kernel,
        out_shape=[struct((local_experts, hidden_units, part), f32), dummy],
        in_specs=[VMEM] * 3,
        out_specs=[HBM, VMEM],
        scratch_shapes=[
            pltpu.VMEM((everyone, part), bf16),
            pltpu.VMEM((2, hidden_units, part), f32),
            pltpu.SemaphoreType.DMA((2, 1)),
        ],
        cost_estimate=cost(everyone * one // columns, 2 * one // columns),
        compiler_params=params(room),
        name="grad_out",
    )(packets, hidden, done_sum)

    mixed, token_grad = pl.pallas_call(
        functools.partial(join_kernel, columns),
        out_shape=[struct((rows, width), bf16)] * 2,
        in_specs=[VMEM] * (columns + 1),
        out_specs=[VMEM] * 2,
        compiler_params=params(room),
        name="join",
    )(*blocks, done_out)
    return (mixed, token_grad, route_grad.T, grad_gate, grad_up, grad_down)


def solution(mesh):
    rows = P(("groups", "expert", "dp"), None)
    experts = P("expert", None, None)
    return jax.shard_map(
        per_device,
        mesh=mesh,
        in_specs=(rows, rows, rows, rows, experts, experts, experts, P("expert", None), rows),
        out_specs=(
            rows,
            rows,
            rows,
            P(("groups", "expert"), "dp", None),
            P(("groups", "expert"), "dp", None),
            P(("groups", "expert"), None, "dp"),
        ),
        check_vma=False,
    )
```

```python
import functools

import jax
import jax.numpy as jnp
from jax import lax
from jax.experimental import pallas as pl
from jax.experimental.pallas import tpu as pltpu
from jax.sharding import PartitionSpec as P

BLK = 128
LANES = 128
CHUNK = 768
TILE = 256
MIB = 1 << 20

VMEM = pl.BlockSpec(memory_space=pltpu.VMEM)
SMEM = pl.BlockSpec(memory_space=pltpu.SMEM)
HBM = pl.BlockSpec(memory_space=pltpu.HBM)

NN = (((1,), (0,)), ((), ()))
NT = (((1,), (1,)), ((), ()))


def dot(a, b, dims):
    return lax.dot_general(a, b, dims, preferred_element_type=jnp.float32)


def ids_along(shape, axis):
    return lax.broadcasted_iota(jnp.int32, shape, axis)


def aligned(index, size):
    return pl.ds(pl.multiple_of(index * size, size), size)


def route_kernel(
    tokens, cotangent, expert_ids, route_weights, own_tokens, packet, ids, values, sems
):
    rows, width = tokens.shape
    lanes = packet.shape[1] - width
    copies = [
        pltpu.make_async_copy(expert_ids, ids, sems.at[0]),
        pltpu.make_async_copy(route_weights, values, sems.at[1]),
        pltpu.make_async_copy(tokens, own_tokens, sems.at[2]),
        pltpu.make_async_copy(cotangent, packet.at[:, :width], sems.at[3]),
    ]
    for copy in copies:
        copy.start()
    for copy in copies:
        copy.wait()
    at = ids_along((lanes, rows), 0)
    weights = values[...].astype(jnp.float32)
    dense = jnp.zeros((lanes, rows), jnp.float32)
    for k in range(ids.shape[0]):
        dense += jnp.where(ids[k : k + 1, :] == at, weights[k : k + 1, :], 0.0)
    packet[:, width:] = dense.T.astype(packet.dtype)


def load_kernel(weight, value, same, *refs):
    targets, sems = refs[:-1], refs[-1]
    copies = [
        pltpu.make_async_copy(weight.at[i], target, sems.at[i]) for i, target in enumerate(targets)
    ]
    for copy in copies:
        copy.start()
    same[...] = value[...]
    for copy in copies:
        copy.wait()


def turn_kernel(x, after, x_part):
    x_part[...] = x[:, aligned(lax.axis_index("dp"), x_part.shape[0])].T


def over_tiles(tokens, body):
    if tokens == TILE:
        body(slice(0, TILE))
    else:

        def turn(tile, carry):
            body(aligned(tile, TILE))
            return carry

        lax.fori_loop(0, tokens // TILE, turn, 0)


def load_slices(weights, targets, sems):
    mine = aligned(lax.axis_index("dp"), targets[0].shape[0])
    copies = [
        pltpu.make_async_copy(weight.at[mine, :], target, sems.at[i])
        for i, (weight, target) in enumerate(zip(weights, targets))
    ]
    for copy in copies:
        copy.start()
    return copies


def load_downs(w_down, targets, first, sems):
    copies = [
        pltpu.make_async_copy(w_down.at[first + i], target, sems.at[i])
        for i, target in enumerate(targets)
    ]
    for copy in copies:
        copy.start()
    return copies


def gate_kernel(count, *refs):
    gates, x, w_down, refs = refs[:count], refs[count], refs[count + 1], refs[count + 2 :]
    products, parts, downs = refs[:count], refs[count : 2 * count], refs[2 * count : -2]
    loads = load_downs(w_down, downs, 0, refs[-1]) + load_slices(gates, parts, refs[-2])

    def tile(rows):
        for gate, product in zip(gates, products):
            for start in range(0, product.shape[1], CHUNK):
                cols = slice(start, start + CHUNK)
                product[rows, cols] = dot(x[rows, :], gate[:, cols], NN)

    over_tiles(x.shape[0], tile)
    for load in loads:
        load.wait()


def up_kernel(first, last, start_down, *refs):
    count = last - first
    products, ups, refs = refs[:count], refs[count : 2 * count], refs[2 * count :]
    x, masks, w_down, value = refs[:4]
    known, parts, refs = refs[4 : 4 + 3 * count], refs[4 + 3 * count : 4 + 4 * count], refs[4 + 4 * count :]
    downs, (same, part_sems, down_sems) = refs[:-3], refs[-3:]
    bf16 = jnp.bfloat16
    hidden_units = ups[0].shape[1]
    loads = load_downs(w_down, downs, start_down, down_sems) + load_slices(ups, parts, part_sems)
    same[...] = value[...]

    def tile(rows):
        for i in range(count):
            hidden, slope_up, slope_gate = known[3 * i : 3 * i + 3]
            for start in range(0, hidden_units, CHUNK):
                cols = slice(start, start + CHUNK)
                up_proj = dot(x[rows, :], ups[i][:, cols], NN)
                at = ids_along((1, CHUNK), 1)
                keep = jnp.zeros((1, CHUNK), jnp.float32)
                for j in range(CHUNK // BLK):
                    kept = masks[first + i, start // BLK + j].astype(jnp.float32)
                    keep = jnp.where(at // BLK == j, kept, keep)
                gate_pre = products[i][rows, cols]
                sigma = 0.5 + 0.5 * jnp.tanh(0.5 * gate_pre)
                silu = gate_pre * sigma
                up_kept = up_proj * keep
                hidden[rows, cols] = (silu * up_kept).astype(bf16)
                slope_up[rows, cols] = (silu * keep).astype(bf16)
                slope = up_kept * (sigma + silu * (1.0 - sigma))
                slope_gate[rows, cols] = slope.astype(bf16)

    over_tiles(x.shape[0], tile)
    for load in loads:
        load.wait()


def hidden_kernel(local_experts, count, *refs):
    packet, refs = refs[0], refs[1:]
    known = [refs[i * 6 : i * 6 + 6] for i in range(local_experts)]
    refs = refs[6 * local_experts :]
    hidden, d_gate, d_up = refs[:3]
    outs, (inner, mixed, token_grad) = refs[3 : 3 + count], refs[3 + count :]
    hidden_units, width = known[0][5].shape
    tokens, part = mixed.shape
    lanes = packet.shape[1] - width
    half = lanes // 2
    base = lax.axis_index("expert") * local_experts
    mine = aligned(lax.axis_index("dp"), part)
    bf16, f32 = jnp.bfloat16, jnp.float32
    inner[...] = jnp.zeros(inner.shape, inner.dtype)
    mixed[...] = jnp.zeros(mixed.shape, mixed.dtype)
    token_grad[...] = jnp.zeros(token_grad.shape, token_grad.dtype)

    for expert in range(local_experts):

        def tile(rows, expert=expert):
            units, slope_up, slope_gate, gate, up, down = known[expert]
            dense = packet[rows, width:].astype(f32)
            at = ids_along((TILE, lanes), 1)
            hit = at == base + expert
            weights = jnp.sum(jnp.where(hit, dense, 0.0), axis=1, keepdims=True)
            total = jnp.zeros((TILE, 1), f32)
            for start in range(0, hidden_units, CHUNK):
                cols = slice(start, start + CHUNK)
                back = dot(packet[rows, :width], down[cols, :], NT)
                part_units = units[rows, cols].astype(f32)
                total += jnp.sum(part_units * back, axis=1, keepdims=True)
                back = back * weights
                new_gate = back * slope_gate[rows, cols].astype(f32)
                new_up = back * slope_up[rows, cols].astype(f32)
                hidden[expert, rows, cols] = (part_units * weights).astype(bf16)
                d_gate[expert, rows, cols] = new_gate.astype(bf16)
                d_up[expert, rows, cols] = new_up.astype(bf16)
            high = total.astype(bf16).astype(f32)
            inner[rows, :] += jnp.where(
                hit, high, jnp.where(at == base + expert + half, total - high, 0.0)
            )
            mixed[rows, :] += dot(hidden[expert, rows, :], down[:, mine], NN)
            token_grad[rows, :] += dot(d_gate[expert, rows, :], gate[...], NT) + dot(
                d_up[expert, rows, :], up[...], NT
            )

        over_tiles(tokens, tile)

    rows = outs[0].shape[0]
    for i, out in enumerate(outs):
        block = slice(i * rows, (i + 1) * rows)
        out[:, :part] = mixed[block].astype(bf16)
        out[:, part : 2 * part] = token_grad[block].astype(bf16)
        out[:, 2 * part :] = inner[block].astype(bf16)


def write_out(steps, place, outs, bufs, sems, body):
    def copies(step, slot):
        return [
            pltpu.make_async_copy(buf.at[slot], out.at[place(step)], sems.at[slot, i])
            for i, (out, buf) in enumerate(zip(outs, bufs))
        ]

    def turn(step, carry):
        slot = lax.rem(step, 2)

        @pl.when(step >= 2)
        def _():
            for copy in copies(step - 2, slot):
                copy.wait()

        body(step, slot)
        for copy in copies(step, slot):
            copy.start()
        return carry

    lax.fori_loop(0, steps, turn, 0)
    for step in range(max(steps - 2, 0), steps):
        for copy in copies(step, step % 2):
            copy.wait()


def grad_in_kernel(x_part, d_gate, d_up, grad_gate, grad_up, done, out_gate, out_up, sems):
    local_experts = d_gate.shape[0]
    part, rows = x_part.shape[0], out_gate.shape[1]
    done[...] = jnp.zeros(done.shape, done.dtype)
    blocks = part // rows

    def place(step):
        return step // blocks, aligned(lax.rem(step, blocks), rows), slice(None)

    def body(step, slot):
        expert, block, _ = place(step)
        out_gate[slot] = dot(x_part[block, :], d_gate[expert], NN)
        out_up[slot] = dot(x_part[block, :], d_up[expert], NN)

    write_out(
        local_experts * blocks, place, (grad_gate, grad_up), (out_gate, out_up), sems, body
    )


def grad_out_kernel(packet, hidden, after, grad_down, done, cot_part, out_down, sems):
    local_experts = hidden.shape[0]
    part = cot_part.shape[1]
    cot_part[...] = packet[:, aligned(lax.axis_index("dp"), part)]
    done[...] = jnp.zeros(done.shape, done.dtype)

    def place(step):
        return (step,)

    def body(step, slot):
        out_down[slot] = dot(hidden[step].T, cot_part[...], NN)

    write_out(local_experts, place, (grad_down,), (out_down,), sems, body)


def reduce_kernel(count, *refs):
    blocks, refs = refs[:count], refs[count:]
    expert_ids, after, route_grad = refs[:3]
    outs, done = refs[3:-1], refs[-1]
    done[...] = jnp.zeros(done.shape, done.dtype)
    rows, both = outs[0].shape
    half = (blocks[0].shape[1] - both) // 2
    for j, out in enumerate(outs):
        total = jnp.zeros((rows, both), jnp.float32)
        for block in blocks:
            total += block[j * rows : (j + 1) * rows, :both].astype(jnp.float32)
        out[...] = total.astype(out.dtype)
    inner = jnp.zeros((rows, 2 * half), jnp.float32)
    for block in blocks:
        inner += block[:rows, both:].astype(jnp.float32)
    inner = inner.T
    inner = inner[:half] + inner[half:]
    at = ids_along(inner.shape, 0)
    for k in range(expert_ids.shape[0]):
        hit = jnp.where(expert_ids[k : k + 1, :] == at, inner, 0.0)
        route_grad[k : k + 1, :] = jnp.sum(hit, axis=0, keepdims=True)


def join_kernel(count, *refs):
    blocks, (after, mixed, token_grad) = refs[:count], refs[count:]
    part = blocks[0].shape[1] // 2
    column = lax.axis_index("dp")
    for other, block in enumerate(blocks):
        cols = aligned(column ^ other, part)
        mixed[:, cols] = block[:, :part]
        token_grad[:, cols] = block[:, part:]


def swap(value, axis, mask):
    size = lax.axis_size(axis)
    return lax.ppermute(value, axis, [(i, i ^ mask) for i in range(size)])


def exchange(value, axis, masks):
    return [swap(value, axis, mask) for mask in masks]


def in_hbm(array):
    return pltpu.with_memory_space_constraint(array, pltpu.HBM)


def in_vmem(array):
    return pltpu.with_memory_space_constraint(array, pltpu.VMEM)


def cost(flops, moved):
    return pl.CostEstimate(flops=flops, bytes_accessed=moved, transcendentals=0)


def params(mib):
    return pltpu.CompilerParams(vmem_limit_bytes=mib * MIB)


def per_device(
    tokens, expert_ids, slot_index, route_weights, w_gate, w_up, w_down, block_masks, cotangent
):
    rows, width = tokens.shape
    local_experts, _, hidden_units = w_gate.shape
    sources, columns = lax.axis_size("expert"), lax.axis_size("dp")
    chips = list(range(2, sources, 2))
    expert_order = [0] + chips + [chip ^ 1 for chip in [0] + chips]
    lanes = -(-2 * local_experts * sources // LANES) * LANES
    part = width // columns
    everyone = sources * columns * rows
    bf16, f32 = jnp.bfloat16, jnp.float32
    struct = jax.ShapeDtypeStruct
    one = 2 * local_experts * width * hidden_units
    room = 8 + (everyone - TILE) * (2 * part + lanes) * 10 // MIB
    dummy = struct((8, LANES), f32)
    ids_t = expert_ids.T
    w_gate, w_up, w_down = [in_hbm(w) for w in (w_gate, w_up, w_down)]

    own_tokens, packet = pl.pallas_call(
        route_kernel,
        out_shape=[struct(tokens.shape, bf16), struct((rows, width + lanes), bf16)],
        in_specs=[HBM] * 4,
        out_specs=[VMEM] * 2,
        scratch_shapes=[
            pltpu.VMEM(ids_t.shape, jnp.int32),
            pltpu.VMEM(ids_t.shape, bf16),
            pltpu.SemaphoreType.DMA((4,)),
        ],
        compiler_params=params(room),
        name="route",
    )(*[in_hbm(a) for a in (tokens, cotangent, ids_t, route_weights.T)])

    def load(weight, value, name):
        same, *loaded = pl.pallas_call(
            load_kernel,
            out_shape=[struct(value.shape, bf16)]
            + [pltpu.VMEM(weight.shape[1:], bf16)] * local_experts,
            in_specs=[HBM, VMEM],
            out_specs=[VMEM] * (1 + local_experts),
            scratch_shapes=[pltpu.SemaphoreType.DMA((local_experts,))],
            cost_estimate=cost(0, one),
            compiler_params=params(room),
            name=name,
        )(weight, value)
        return [in_vmem(array) for array in loaded], same

    tokens_near = exchange(tokens, "dp", range(1, columns))
    c_column = jnp.concatenate([packet] + exchange(packet, "dp", range(1, columns)))
    ups, own_tokens = load(w_up, own_tokens, "load_up")
    x_column = jnp.concatenate([own_tokens] + tokens_near)
    x_across = exchange(x_column, "expert", chips)
    c_across = exchange(c_column, "expert", chips)
    gates, x_column = load(w_gate, x_column, "load_gate")
    x = jnp.concatenate([x_column] + x_across)
    x = jnp.concatenate([x, swap(x, "expert", 1)])

    middle = max(local_experts // 2, 1)
    weight_part = pltpu.VMEM((part, hidden_units), bf16)
    weight_down = pltpu.VMEM(w_down.shape[1:], bf16)
    found = pl.pallas_call(
        functools.partial(gate_kernel, local_experts),
        out_shape=[struct((everyone, hidden_units), f32)] * local_experts
        + [weight_part] * local_experts
        + [weight_down] * middle,
        in_specs=[VMEM] * (local_experts + 1) + [HBM],
        out_specs=[VMEM] * (2 * local_experts + middle),
        scratch_shapes=[
            pltpu.SemaphoreType.DMA((local_experts,)),
            pltpu.SemaphoreType.DMA((middle,)),
        ],
        cost_estimate=cost(everyone * one, one),
        compiler_params=params(room),
        name="gate",
    )(*gates, x, w_down)
    found = list(found)
    products = found[:local_experts]
    gate_parts = [in_vmem(array) for array in found[local_experts : 2 * local_experts]]
    downs = [in_vmem(array) for array in found[2 * local_experts :]]

    def up_call(first, last, start_down, value):
        count, more = last - first, local_experts - start_down
        found = pl.pallas_call(
            functools.partial(up_kernel, first, last, start_down),
            out_shape=[struct((everyone, hidden_units), bf16)] * (3 * count)
            + [weight_part] * count
            + [weight_down] * more
            + [struct(value.shape, value.dtype)],
            in_specs=[VMEM] * (2 * count + 1) + [SMEM, HBM, VMEM],
            out_specs=[VMEM] * (4 * count + more + 1),
            scratch_shapes=[
                pltpu.SemaphoreType.DMA((count,)),
                pltpu.SemaphoreType.DMA((max(more, 1),)),
            ],
            cost_estimate=cost(
                everyone * one * count // local_experts, one * count // local_experts
            ),
            compiler_params=params(room),
            name="up",
        )(*products[first:last], *ups[first:last], x, block_masks, w_down, value)
        found = list(found)
        arrays = [in_vmem(array) for array in found[3 * count : -1]]
        return found[: 3 * count], arrays[:count], arrays[count:], found[-1]

    factors, up_parts, more_downs, c_column = up_call(0, middle, middle, c_column)
    downs = downs + more_downs
    if middle < local_experts:
        more, more_parts, _, _ = up_call(middle, local_experts, local_experts, c_column)
        factors, up_parts = factors + more, up_parts + more_parts
    known = []
    for i in range(local_experts):
        known += factors[3 * i : 3 * i + 3] + [gate_parts[i], up_parts[i], downs[i]]
    c_half = jnp.concatenate([c_column] + c_across)
    packets = jnp.concatenate([c_half, swap(c_half, "expert", 1)])
    x_part = pl.pallas_call(
        turn_kernel,
        out_shape=struct((part, everyone), bf16),
        in_specs=[VMEM] * 2,
        out_specs=VMEM,
        compiler_params=params(room),
        name="turn",
    )(x, c_half)

    units = struct((local_experts, everyone, hidden_units), bf16)
    hidden, d_gate, d_up, *partials = pl.pallas_call(
        functools.partial(hidden_kernel, local_experts, sources),
        out_shape=[units] * 3
        + [struct((columns * rows, 2 * part + lanes), bf16)] * sources,
        in_specs=[VMEM] * (1 + len(known)),
        out_specs=[VMEM] * (3 + sources),
        scratch_shapes=[
            pltpu.VMEM((everyone, lanes), f32),
            pltpu.VMEM((everyone, part), f32),
            pltpu.VMEM((everyone, part), f32),
        ],
        cost_estimate=cost(2 * everyone * one, 2 * one),
        compiler_params=params(room),
        name="hidden",
    )(packets, *known)
    arrived = [
        swap(partial, "expert", other) if other else partial
        for other, partial in zip(expert_order, partials)
    ]

    grad_gate, grad_up, done_in = pl.pallas_call(
        grad_in_kernel,
        out_shape=[struct((local_experts, part, hidden_units), f32)] * 2 + [dummy],
        in_specs=[VMEM] * 3,
        out_specs=[HBM] * 2 + [VMEM],
        scratch_shapes=[
            pltpu.VMEM((2, part, hidden_units), f32),
            pltpu.VMEM((2, part, hidden_units), f32),
            pltpu.SemaphoreType.DMA((2, 2)),
        ],
        cost_estimate=cost(2 * everyone * one // columns, 4 * one // columns),
        compiler_params=params(room + 6),
        name="grad_in",
    )(x_part, d_gate, d_up)

    route_grad, *blocks, done_sum = pl.pallas_call(
        functools.partial(reduce_kernel, sources),
        out_shape=[struct(ids_t.shape, f32)] + [struct((rows, 2 * part), bf16)] * columns + [dummy],
        in_specs=[VMEM] * (sources + 2),
        out_specs=[VMEM] * (columns + 2),
        compiler_params=params(room),
        name="reduce",
    )(*arrived, ids_t, done_in)
    blocks = [
        swap(block, "dp", other) if other else block for other, block in enumerate(blocks)
    ]

    grad_down, done_out = pl.pallas_call(
        grad_out_kernel,
        out_shape=[struct((local_experts, hidden_units, part), f32), dummy],
        in_specs=[VMEM] * 3,
        out_specs=[HBM, VMEM],
        scratch_shapes=[
            pltpu.VMEM((everyone, part), bf16),
            pltpu.VMEM((2, hidden_units, part), f32),
            pltpu.SemaphoreType.DMA((2, 1)),
        ],
        cost_estimate=cost(everyone * one // columns, 2 * one // columns),
        compiler_params=params(room),
        name="grad_out",
    )(packets, hidden, done_sum)

    mixed, token_grad = pl.pallas_call(
        functools.partial(join_kernel, columns),
        out_shape=[struct((rows, width), bf16)] * 2,
        in_specs=[VMEM] * (columns + 1),
        out_specs=[VMEM] * 2,
        compiler_params=params(room),
        name="join",
    )(*blocks, done_out)
    return (mixed, token_grad, route_grad.T, grad_gate, grad_up, grad_down)


def solution(mesh):
    rows = P(("groups", "expert", "dp"), None)
    experts = P("expert", None, None)
    return jax.shard_map(
        per_device,
        mesh=mesh,
        in_specs=(rows, rows, rows, rows, experts, experts, experts, P("expert", None), rows),
        out_specs=(
            rows,
            rows,
            rows,
            P(("groups", "expert"), "dp", None),
            P(("groups", "expert"), "dp", None),
            P(("groups", "expert"), None, "dp"),
        ),
        check_vma=False,
    )
```
